32 devices in a mesh: section: 2 (over core), dp: 16 (over z, y, x).
Axes of the slice: x: 2, y: 2, z: 4, core: 2. Of those that a mesh axis runs over, the one named last changes fastest.
Arguments:
- features: bfloat16 [64, 28, 12544], P('dp', 'section'), may hold values from -6 to 6
- crop_side: int32 [64], P('dp'), may hold values from 14 to 28, as said below
- upstream: bfloat16 [64, 14, 12544], P('dp', 'section'), may hold values from -6 to 6
- entry_in: bfloat16 [401408], P(('section', 'dp')), may hold values from -0.25 to 0.25
- entry_group: bfloat16 [451584], P(('section', 'dp')), may hold values from -0.25 to 0.25
- entry_out: bfloat16 [802816], P(('section', 'dp')), may hold values from -0.1875 to 0.1875
- entry_down: bfloat16 [100352], P(('section', 'dp')), may hold values from -0.75 to 0.75
- entry_up: bfloat16 [100352], P(('section', 'dp')), may hold values from -2 to 2
- shortcut_weight: bfloat16 [401408], P(('section', 'dp')), may hold values from -0.25 to 0.25
- body_in: bfloat16 [802816], P(('section', 'dp')), may hold values from -0.1875 to 0.1875
- body_group: bfloat16 [451584], P(('section', 'dp')), may hold values from -0.25 to 0.25
- body_out: bfloat16 [802816], P(('section', 'dp')), may hold values from -0.1875 to 0.1875
- body_down: bfloat16 [200704], P(('section', 'dp')), may hold values from -0.75 to 0.75
- body_up: bfloat16 [200704], P(('section', 'dp')), may hold values from -1.5 to 1.5
- norm_gain: float32 [2, 3, 896], P('section'), may hold values from 0.25 to 1.75
- norm_shift: float32 [2, 3, 896], P('section'), may hold values from -3 to 3
- shortcut_gain: bfloat16 [896], P('section'), may hold values from 0.25 to 1.75
- shortcut_shift: bfloat16 [896], P('section'), may hold values from -3 to 3
Outputs:
- output: bfloat16 [64, 14, 12544], P('dp', 'section')
- grad_features: bfloat16 [64, 28, 12544], P('dp', 'section')
- grad_entry_in: float32 [401408], P(('section', 'dp'))
- grad_entry_group: float32 [451584], P(('section', 'dp'))
- grad_entry_out: float32 [802816], P(('section', 'dp'))
- grad_entry_down: float32 [100352], P(('section', 'dp'))
- grad_entry_up: float32 [100352], P(('section', 'dp'))
- grad_shortcut_weight: float32 [401408], P(('section', 'dp'))
- grad_body_in: float32 [802816], P(('section', 'dp'))
- grad_body_group: float32 [451584], P(('section', 'dp'))
- grad_body_out: float32 [802816], P(('section', 'dp'))
- grad_body_down: float32 [200704], P(('section', 'dp'))
- grad_body_up: float32 [200704], P(('section', 'dp'))
- grad_norm_gain: float32 [2, 3, 896], P('section')
- grad_norm_shift: float32 [2, 3, 896], P('section')
- grad_shortcut_gain: float32 [896], P('section')
- grad_shortcut_shift: float32 [896], P('section')
The draws below stay inside these ranges and needn't reach their ends.
Inputs may be any that keep to these rules, and one draw needn't show every extreme that they name: `crop_side`: each crop has side 28 or 14; among the 4 crops of every index of dp at least one has side 28.
All inputs are finite; a program needn't handle non-finite values.
Results may differ from the reference program's by a relative error of at most 0.017.
Values may be sent and summed in bfloat16 or wider, within the bound.
A program may use at most 320 MiB of HBM per device.

```python
import jax
import jax.numpy as jnp
from jax import lax

D = 896
DIN = 448
GROUPS = 16
GW = 56
SE0 = 112
SE1 = 224
OUT = 14
MICRO = 4
CROP_MB = 1
IN = 28
SLOTS = 4
CROPS = 64
N_DP = 16


def draw_crop_side(key, part):
    key = jax.random.fold_in(key, 11)
    coin_key, pick_key = jax.random.split(key)
    coin_flips = jax.random.randint(coin_key, (CROPS,), 0, 2)
    chosen = jax.random.randint(pick_key, (CROPS // SLOTS,), 0, SLOTS)
    slot_index = jnp.arange(CROPS, dtype=jnp.int32) % SLOTS
    forced = slot_index == jnp.repeat(chosen, SLOTS)
    full_size = jnp.logical_or(coin_flips == 1, forced)
    return jnp.where(full_size, IN, IN // 2).astype(jnp.int32)


def steps_of(own_key, extent, cuts, low, high):
    def one(axis_at, shards_of):
        heights = jax.random.uniform(jax.random.fold_in(jax.random.fold_in(own_key, 6), axis_at), (shards_of,), jnp.float32, low / len(cuts), high / len(cuts))
        return jnp.repeat(jnp.exp(heights), extent[axis_at] // shards_of).reshape((-1,) + (1,) * (len(extent) - axis_at - 1))

    loudness = one(*cuts[0])
    for cut in cuts[1:]:
        loudness = loudness * one(*cut)
    return loudness


def centred(rng, shape, deviation, most, cuts=(), kind=jnp.bfloat16):
    loudness = steps_of(rng, shape, cuts, -0.22, 0.18) if cuts else 1.0
    array = jax.random.normal(rng, shape, jnp.float32) * deviation * loudness
    return jnp.minimum(jnp.maximum(array, -most), most).astype(kind)


def setup_inputs(seed: int = 0) -> dict:
    seeds = jax.random.split(jax.random.key(seed), 19)
    return {
        "features": centred(seeds[0], (CROPS, IN, IN * DIN), 1.0, 6.0, ((0, 16), (1, 2))),
        "crop_side": draw_crop_side(jax.random.fold_in(seeds[18], 71), 0),
        "upstream": centred(seeds[2], (CROPS, OUT, OUT * D), 1.0, 6.0, ((0, 16), (1, 2))),
        "entry_in": centred(seeds[3], (DIN * D,), DIN ** -0.5, 0.25, ((0, 32),)),
        "entry_group": centred(seeds[4], (9 * GW * D,), (9 * GW) ** -0.5, 0.25, ((0, 32),)),
        "entry_out": centred(seeds[5], (D * D,), D ** -0.5, 0.1875, ((0, 32),)),
        "entry_down": centred(seeds[6], (D * SE0,), (D // 16) ** -0.5, 0.75, ((0, 32),)),
        "entry_up": centred(seeds[7], (SE0 * D,), (max(SE0 // 16, 1)) ** -0.5, 2.0, ((0, 32),)),
        "shortcut_weight": centred(seeds[8], (DIN * D,), DIN ** -0.5, 0.25, ((0, 32),)),
        "body_in": centred(seeds[9], (D * D,), D ** -0.5, 0.1875, ((0, 32),)),
        "body_group": centred(seeds[10], (9 * GW * D,), (9 * GW) ** -0.5, 0.25, ((0, 32),)),
        "body_out": centred(seeds[11], (D * D,), D ** -0.5, 0.1875, ((0, 32),)),
        "body_down": centred(seeds[12], (D * SE1,), (D // 16) ** -0.5, 0.75, ((0, 32),)),
        "body_up": centred(seeds[13], (SE1 * D,), (max(SE1 // 16, 1)) ** -0.5, 1.5, ((0, 32),)),
        "norm_gain": jnp.clip(1.0 + 0.15 * jax.random.normal(seeds[14], (2, 3, D), jnp.float32), 0.25, 1.75),
        "norm_shift": centred(seeds[15], (2, 3, D), 0.5, 3.0, ((0, 2),), jnp.float32),
        "shortcut_gain": jnp.clip(1.0 + 0.15 * jax.random.normal(seeds[16], (D,), jnp.float32), 0.25, 1.75).astype(jnp.bfloat16),
        "shortcut_shift": centred(seeds[17], (D,), 0.5, 3.0, ((0, 2),)),
    }


@jax.custom_vjp
def low(v):
    return lax.optimization_barrier(v.astype(jnp.bfloat16)).astype(jnp.float32)

@jax.custom_vjp
def low_back(v):
    return v

def low_keep(v):
    return (low(v), None)

def low_pass(kept, grad):
    return (grad,)

def back_keep(v):
    return (v, None)

def back_low(kept, grad):
    return (low(grad),)
low.defvjp(low_keep, low_pass)
low_back.defvjp(back_keep, back_low)
EPSILON = 1e-05
HIGHEST = lax.Precision.HIGHEST

def smooth_gate(tensor):
    return tensor * jax.nn.sigmoid(tensor)

def batch_norm(tensor, masking, population, scale_by, offset):
    center = lax.optimization_barrier(jnp.sum(masking * tensor, axis=(0, 1, 2))) / population
    spread = lax.optimization_barrier(jnp.sum(masking * tensor * tensor, axis=(0, 1, 2))) / population - center * center
    return (tensor - center) * lax.rsqrt(spread + EPSILON) * scale_by + offset

def pixel_product(tensor, weight):
    return jnp.einsum('khwc,cd->khwd', tensor, weight, precision=HIGHEST)

def residual_block(source, weights, gains, shifts, mask_in, mask_out, crop_count, stride, residual):
    weight_in, kernel, weight_out, squeeze, expand = weights
    count_in = jnp.sum(mask_in)
    count_out = jnp.sum(mask_out)
    inner_raw = low_back(pixel_product(source, weight_in))
    activated = low(mask_in * smooth_gate(batch_norm(inner_raw, mask_in, count_in, gains[0], shifts[0])))
    convolved = low_back(lax.conv_general_dilated(activated, kernel.reshape(3, 3, GW, D), (stride, stride), ((1, 1), (1, 1)), dimension_numbers=('NHWC', 'HWIO', 'NHWC'), feature_group_count=GROUPS, precision=HIGHEST))
    excited = mask_out * smooth_gate(batch_norm(convolved, mask_out, count_out, gains[1], shifts[1]))
    pooled = lax.optimization_barrier(jnp.sum(excited, axis=(1, 2))) / crop_count[:, None]
    squeezed = smooth_gate(jnp.dot(pooled, squeeze, precision=HIGHEST))
    gating = jax.nn.sigmoid(jnp.dot(squeezed, expand, precision=HIGHEST))
    gated = low(excited * gating[:, None, None, :])
    projected = low_back(pixel_product(gated, weight_out))
    summed = batch_norm(projected, mask_out, count_out, gains[2], shifts[2]) + residual
    return mask_out * smooth_gate(summed)

def two_blocks(params, source, mask_in, mask_out, crop_count):
    entry_in, entry_group, entry_out, entry_down, entry_up, shortcut_weight, body_in, body_group, body_out, body_down, body_up, norm_gain, norm_shift, shortcut_gain, shortcut_shift = params
    count_out = jnp.sum(mask_out)
    strided = low_back(pixel_product(source[:, ::2, ::2], shortcut_weight))
    residual = batch_norm(strided, mask_out, count_out, shortcut_gain, shortcut_shift)
    first_weights = (entry_in, entry_group, entry_out, entry_down, entry_up)
    hidden = low_back(low(residual_block(source, first_weights, norm_gain[0], norm_shift[0], mask_in, mask_out, crop_count, 2, residual)))
    second_weights = (body_in, body_group, body_out, body_down, body_up)
    return low(residual_block(hidden, second_weights, norm_gain[1], norm_shift[1], mask_out, mask_out, crop_count, 1, hidden))

def reference(features, crop_side, upstream, entry_in, entry_group, entry_out, entry_down, entry_up, shortcut_weight, body_in, body_group, body_out, body_down, body_up, norm_gain, norm_shift, shortcut_gain, shortcut_shift):
    features = features.reshape(CROPS, IN, IN, DIN)
    upstream = upstream.reshape(CROPS, OUT, OUT, D)
    params = (entry_in.astype(jnp.float32).reshape(DIN, D), entry_group.astype(jnp.float32), entry_out.astype(jnp.float32).reshape(D, D), entry_down.astype(jnp.float32).reshape(D, SE0), entry_up.astype(jnp.float32).reshape(SE0, D), shortcut_weight.astype(jnp.float32).reshape(DIN, D), body_in.astype(jnp.float32).reshape(D, D), body_group.astype(jnp.float32), body_out.astype(jnp.float32).reshape(D, D), body_down.astype(jnp.float32).reshape(D, SE1), body_up.astype(jnp.float32).reshape(SE1, D), norm_gain, norm_shift, shortcut_gain.astype(jnp.float32), shortcut_shift.astype(jnp.float32))
    side_in = jnp.arange(IN, dtype=jnp.int32)
    boundary = crop_side[:, None, None]
    mask_in = ((side_in[None, :, None] < boundary) & (side_in[None, None, :] < boundary)).astype(jnp.float32)[..., None]
    half_side = crop_side // 2
    side_out = jnp.arange(OUT, dtype=jnp.int32)
    half_bound = half_side[:, None, None]
    mask_out = ((side_out[None, :, None] < half_bound) & (side_out[None, None, :] < half_bound)).astype(jnp.float32)[..., None]
    crop_count = (half_side * half_side).astype(jnp.float32)

    def by_micro(tensor):
        shaped = tensor.reshape((N_DP, MICRO, CROP_MB) + tensor.shape[1:])
        return jnp.swapaxes(shaped, 0, 1).reshape((MICRO, N_DP * CROP_MB) + tensor.shape[1:])

    def from_micro(tensor):
        shaped = tensor.reshape((MICRO, N_DP, CROP_MB) + tensor.shape[2:])
        return jnp.swapaxes(shaped, 0, 1).reshape((N_DP * MICRO * CROP_MB,) + tensor.shape[2:])

    def one_micro(totals, pieces):
        source, cotangent, inside, outside, counts = pieces
        result, pullback = jax.vjp(lambda weights, values: two_blocks(weights, values, inside, outside, counts), params, source.astype(jnp.float32))
        weight_grads, source_grad = pullback(cotangent.astype(jnp.float32))
        totals = jax.tree.map(lambda running, addend: running + addend, totals, weight_grads)
        return (totals, (result.astype(jnp.bfloat16), source_grad.astype(jnp.bfloat16)))
    zero_grads = jax.tree.map(jnp.zeros_like, params)
    totals, (results, source_grads) = lax.scan(one_micro, zero_grads, (by_micro(features), by_micro(upstream), by_micro(mask_in), by_micro(mask_out), by_micro(crop_count)))
    flat = tuple((totals[index].reshape(-1) for index in range(11)))
    output = from_micro(results).reshape(CROPS, OUT, OUT * D)
    grad_features = from_micro(source_grads).reshape(CROPS, IN, IN * DIN)
    return (output, grad_features, flat[0], flat[1], flat[2], flat[3], flat[4], flat[5], flat[6], flat[7], flat[8], flat[9], flat[10], totals[11], totals[12], totals[13], totals[14])
```

```python
import jax
import jax.numpy as jnp
from jax import lax
from jax.sharding import PartitionSpec as P

D = 896
DIN = 448
GROUPS = 16
GW = 56
SE0 = 112
SE1 = 224
OUT = 14
IN = 28
EPSILON = 1e-05
HIGHEST = lax.Precision.HIGHEST
F32 = jnp.float32
BF16 = jnp.bfloat16


def silu(v):
    return v * jax.nn.sigmoid(v)


def slope(v):
    g = jax.nn.sigmoid(v)
    return g * (1.0 + v * (1.0 - g))


def px_dot(values, weight):
    return jnp.einsum("khwc,cd->khwd", values, weight, preferred_element_type=F32)


def px_back(values, weight):
    return jnp.einsum("khwd,cd->khwc", values, weight, preferred_element_type=F32)


def px_outer(a, b):
    return jnp.einsum("khwc,khwd->cd", a, b, preferred_element_type=F32)


def crop_sums(values):
    return jnp.sum(values, axis=(1, 2))


def moments(sums, count):
    center = sums[:, 0] / count
    scaling = lax.rsqrt(sums[:, 1] / count - center * center + EPSILON)
    return center[:, None, None], scaling[:, None, None]


def conv(x, kernel, stride):
    return lax.conv_general_dilated(
        x,
        kernel,
        (stride, stride),
        ((1, 1), (1, 1)),
        dimension_numbers=("NHWC", "HWIO", "NHWC"),
        feature_group_count=GROUPS,
        preferred_element_type=F32,
    )


def two_sums(values, mask):
    weighted = mask * values
    return jnp.stack([crop_sums(weighted), crop_sums(weighted * values)], 1)


def block_forward(u, weights, gains, shifts, mask_u, mask_out, n_u, n_out, crop_count, stride, short):
    wa, kernel, wc, wd, wu = weights
    inner = px_dot(u, wa)
    sums_a = lax.psum(two_sums(inner, mask_u), "dp")
    center_a, scaling_a = moments(sums_a, n_u)
    hat_a = (inner - center_a) * scaling_a
    activated = (mask_u * silu(hat_a * gains[0] + shifts[0])).astype(BF16)
    convolved = conv(activated, kernel, stride)
    sums_b = lax.psum(two_sums(convolved, mask_out), "dp")
    center_b, scaling_b = moments(sums_b, n_out)
    hat_b = (convolved - center_b) * scaling_b
    excited = mask_out * silu(hat_b * gains[1] + shifts[1])
    pooled = crop_sums(excited) / crop_count
    squeeze_raw = jnp.dot(pooled, wd, precision=HIGHEST)
    squeezed = silu(squeeze_raw)
    gating = jax.nn.sigmoid(jnp.dot(squeezed, wu, precision=HIGHEST))
    gated = (excited * gating[:, None, None]).astype(BF16)
    projected = px_dot(gated, wc)
    sums_c = two_sums(projected, mask_out)
    hat_s = None
    scaling_s = None
    if short is not None:
        weight_s, gain_s, shift_s = short
        strided = px_dot(u[:, ::2, ::2], weight_s)
        sums_c = lax.psum(jnp.concatenate([sums_c, two_sums(strided, mask_out)], 1), "dp")
        center_s, scaling_s = moments(sums_c[:, 2:], n_out)
        hat_s = (strided - center_s) * scaling_s
        residual = hat_s * gain_s + shift_s
    else:
        sums_c = lax.psum(sums_c, "dp")
        residual = u.astype(F32)
    center_c, scaling_c = moments(sums_c[:, :2], n_out)
    hat_c = (projected - center_c) * scaling_c
    summed = hat_c * gains[2] + shifts[2] + residual
    output = (mask_out * silu(summed)).astype(BF16)
    kept = (
        hat_a, scaling_a, activated, hat_b, scaling_b, excited, pooled, squeeze_raw, squeezed,
        gating, gated, hat_c, scaling_c, hat_s, scaling_s, summed,
    )
    return output, kept


def norm_back(dz, hat, scaling, gain, totals, n, mask):
    mean_dz = (totals[:, 0] / n)[:, None, None]
    mean_hat = (totals[:, 1] / n)[:, None, None]
    return (mask * gain * scaling * (dz - mean_dz - hat * mean_hat)).astype(BF16)


def block_backward(
    d_out, u, weights, gains, shifts, mask_u, mask_out, n_u, n_out, crop_count, stride, short, kept
):
    wa, kernel, wc, wd, wu = weights
    (
        hat_a, scaling_a, activated, hat_b, scaling_b, excited, pooled, squeeze_raw, squeezed,
        gating, gated, hat_c, scaling_c, hat_s, scaling_s, summed,
    ) = kept
    d_pre = d_out * mask_out * slope(summed)
    terms = [crop_sums(d_pre), crop_sums(d_pre * hat_c)]
    if short is not None:
        terms.append(crop_sums(d_pre * hat_s))
    tot_c = lax.psum(jnp.stack(terms, 1), "dp")
    d_proj = norm_back(d_pre, hat_c, scaling_c, gains[2], tot_c, n_out, mask_out)
    g_wc = px_outer(gated, d_proj)
    d_gated = px_back(d_proj, wc)
    d_gate = crop_sums(d_gated * excited)
    d_gate_raw = d_gate * gating * (1.0 - gating)
    g_wu = jnp.dot(squeezed.T, d_gate_raw, precision=HIGHEST)
    d_sq = jnp.dot(d_gate_raw, wu.T, precision=HIGHEST) * slope(squeeze_raw)
    g_wd = jnp.dot(pooled.T, d_sq, precision=HIGHEST)
    d_pool = jnp.dot(d_sq, wd.T, precision=HIGHEST) / crop_count
    d_exc = d_gated * gating[:, None, None] + d_pool[:, None, None]
    dz_b = d_exc * mask_out * slope(hat_b * gains[1] + shifts[1])
    tot_b = lax.psum(jnp.stack([crop_sums(dz_b), crop_sums(dz_b * hat_b)], 1), "dp")
    d_conv = norm_back(dz_b, hat_b, scaling_b, gains[1], tot_b, n_out, mask_out)
    back = jax.vjp(
        lambda x, k: conv(x, k, stride), activated.astype(F32), kernel.astype(F32)
    )[1]
    d_act, g_k = back(d_conv.astype(F32))
    dz_a = d_act * mask_u * slope(hat_a * gains[0] + shifts[0])
    tot_a = lax.psum(jnp.stack([crop_sums(dz_a), crop_sums(dz_a * hat_a)], 1), "dp")
    d_inner = norm_back(dz_a, hat_a, scaling_a, gains[0], tot_a, n_u, mask_u)
    g_wa = px_outer(u, d_inner)
    d_u = px_back(d_inner, wa)
    g_ws = None
    if short is not None:
        weight_s, gain_s, shift_s = short
        tot_s = jnp.stack([tot_c[:, 0], tot_c[:, 2]], 1)
        d_strided = norm_back(d_pre, hat_s, scaling_s, gain_s, tot_s, n_out, mask_out)
        g_ws = px_outer(u[:, ::2, ::2], d_strided)
        d_u = d_u.at[:, ::2, ::2].add(px_back(d_strided, weight_s))
    else:
        d_u = d_u + d_pre
    return d_u.astype(BF16), (g_wa, g_k, g_wc, g_wd, g_wu, g_ws), (tot_a, tot_b, tot_c)


def local(
    features, crop_side, upstream,
    entry_in, entry_group, entry_out, entry_down, entry_up, shortcut_weight,
    body_in, body_group, body_out, body_down, body_up,
    norm_gain, norm_shift, shortcut_gain, shortcut_shift,
):
    section = lax.axis_index("section")
    first = section == 0
    slots = features.shape[0]
    half = slots // 2
    swap = [(0, 1), (1, 0)]

    def halves_in(rows):
        sent = lax.dynamic_slice_in_dim(rows, (1 - section) * half, half, 0)
        kept = lax.dynamic_slice_in_dim(rows, section * half, half, 0)
        got = lax.ppermute(sent, "section", swap)
        return jnp.where(
            first, jnp.concatenate([kept, got], 1), jnp.concatenate([got, kept], 1)
        )

    def halves_out(whole):
        rows = whole.shape[1] // 2
        top, low = whole[:, :rows], whole[:, rows:]
        got = lax.ppermute(jnp.where(first, low, top), "section", swap)
        kept = jnp.where(first, top, low)
        return jnp.where(
            first, jnp.concatenate([kept, got], 0), jnp.concatenate([got, kept], 0)
        )

    u = halves_in(features).reshape(half, IN, IN, DIN)
    d_out = halves_in(upstream).reshape(half, OUT, OUT, D).astype(F32)
    shards = (
        entry_in, entry_group, entry_out, entry_down, entry_up, shortcut_weight,
        body_in, body_group, body_out, body_down, body_up,
    )
    shapes = (
        (DIN, D), (3, 3, GW, D), (D, D), (D, SE0), (SE0, D), (DIN, D),
        (D, D), (3, 3, GW, D), (D, D), (D, SE1), (SE1, D),
    )
    together = lax.all_gather(jnp.concatenate(shards), ("section", "dp"), axis=0, tiled=False)
    weights = []
    start = 0
    for shard, shape in zip(shards, shapes):
        weights.append(together[:, start : start + shard.shape[0]].reshape(shape))
        start += shard.shape[0]
    (w_in, w_group, w_out, w_down, w_up, w_short, b_in, b_group, b_out, b_down, b_up) = weights
    entry = (w_in, w_group, w_out, w_down.astype(F32), w_up.astype(F32))
    body = (b_in, b_group, b_out, b_down.astype(F32), b_up.astype(F32))
    gains, shifts, short_gain, short_shift = (
        lax.all_gather(part, "section", axis=0, tiled=True)
        for part in (norm_gain, norm_shift, shortcut_gain, shortcut_shift)
    )
    short = (w_short, short_gain.astype(F32), short_shift.astype(F32))
    side = lax.dynamic_slice_in_dim(crop_side, section * half, half, 0)

    def grid_mask(extent, bound):
        at = jnp.arange(extent, dtype=jnp.int32)
        inside = at[None] < bound[:, None]
        return (inside[:, :, None] & inside[:, None, :]).astype(F32)[..., None]

    mask_in = grid_mask(IN, side)
    mask_out = grid_mask(OUT, side // 2)
    crop_count = ((side // 2) * (side // 2)).astype(F32)[:, None]
    n_out = lax.psum(crop_count, "dp")
    n_in = n_out * 4.0

    hidden, kept0 = block_forward(
        u, entry, gains[0], shifts[0], mask_in, mask_out, n_in, n_out, crop_count, 2, short
    )
    output, kept1 = block_forward(
        hidden, body, gains[1], shifts[1], mask_out, mask_out, n_out, n_out, crop_count, 1, None
    )
    d_hidden, grads1, totals1 = block_backward(
        d_out, hidden, body, gains[1], shifts[1], mask_out, mask_out, n_out, n_out, crop_count, 1,
        None, kept1,
    )
    d_features, grads0, totals0 = block_backward(
        d_hidden.astype(F32), u, entry, gains[0], shifts[0], mask_in, mask_out, n_in, n_out,
        crop_count, 2, short, kept0,
    )
    order = (
        grads0[0], grads0[1], grads0[2], grads0[3], grads0[4], grads0[5],
        grads1[0], grads1[1], grads1[2], grads1[3], grads1[4],
    )
    devices = lax.axis_size("section") * lax.axis_size("dp")
    packed = jnp.concatenate([grad.reshape(devices, -1) for grad in order], 1)
    summed = lax.psum_scatter(packed, ("section", "dp"), scatter_dimension=0, tiled=False)
    weight_out = []
    start = 0
    for shard in shards:
        weight_out.append(summed[start : start + shard.shape[0]])
        start += shard.shape[0]

    norms = [
        jnp.stack(
            [
                jnp.stack([jnp.sum(totals[at][:, kind], 0) for at in range(3)])
                for totals in (totals0, totals1)
            ]
        )
        for kind in (1, 0)
    ]
    short_grads = jnp.stack([jnp.sum(totals0[2][:, 2], 0), jnp.sum(totals0[2][:, 0], 0)])
    norms = lax.psum(jnp.concatenate([norms[0], norms[1]], 1), "section")
    own = lax.dynamic_slice_in_dim(norms, section, 1, 0)
    short_grads = lax.psum(short_grads, "section")
    width = shortcut_gain.shape[0]
    own_short = lax.dynamic_slice_in_dim(short_grads, section * width, width, 1)
    return (
        halves_out(output.reshape(half, OUT, OUT * D)),
        halves_out(d_features.reshape(half, IN, IN * DIN)),
        *weight_out,
        own[:, :3],
        own[:, 3:],
        own_short[0],
        own_short[1],
    )


def solution(mesh):
    rows = P("dp", "section", None)
    flat = P(("section", "dp"))
    params = (P("section", None, None), P("section", None, None), P("section"), P("section"))
    return jax.shard_map(
        local,
        mesh=mesh,
        in_specs=(rows, P("dp"), rows) + (flat,) * 11 + params,
        out_specs=(rows, rows) + (flat,) * 11 + params,
        check_vma=False,
    )
```

```python
import functools

import jax
import jax.numpy as jnp
import numpy as np
from jax import lax
from jax.experimental import pallas as pl
from jax.experimental.pallas import tpu as pltpu
from jax.sharding import PartitionSpec as P

D = 896
DIN = 448
OUT = 14
IN = 28
SE0 = 112
SE1 = 224
EPSILON = 1e-05
F32 = jnp.float32
BF16 = jnp.bfloat16
MESH = pl.DeviceIdType.MESH
C = 1024
PX = 224
GUARD = 16
MEMBERS = 16
SHARDS = 32


def dot(a, b, dims):
    return lax.dot_general(a, b, ((dims[:1], dims[1:]), ((), ())), preferred_element_type=F32)


def nn(a, b):
    return dot(a, b, (1, 0))


def nt(a, b):
    return dot(a, b, (1, 1))


def tn(a, b):
    return dot(a, b, (0, 0))


def sig(z):
    return jnp.tanh(z * 0.5) * 0.5 + 0.5


def slope_of(z, s):
    return s * (1.0 + z * (1.0 - s))


def split_rows(rows):
    high = [r.astype(BF16).astype(F32) for r in rows]
    low = [r - h for r, h in zip(rows, high)]
    return high, low


def stacked(rows):
    pad = jnp.zeros((16 - len(rows), rows[0].shape[1]), F32)
    return jnp.concatenate(list(rows) + [pad], 0).astype(BF16)


def row_dot(row, weight, mul):
    high, low = split_rows([row])
    both = mul(stacked(high + low), weight)
    return both[0:1] + both[1:2]


def col(n, width=256):
    return pl.ds(pl.multiple_of(n * width, width), width)


def chunk(j, base=0):
    return pl.ds(pl.multiple_of(j * 16 + base, 16), 16)


def loop(count, body):
    def step(i, carry):
        body(i)
        return carry

    lax.fori_loop(0, count, step, 0)


def main_kernel(
    n_dp, features, upstream, side_ref, expand, wa0, ws, k0, wc0, wd0, wu0, wa1, k1, wc1, wd1,
    wu1, params, out, grad, g_wa0, g_ws, g_k0, g_wc0, g_wd0, g_wu0, g_wa1, g_k1, g_wc1, g_wd1,
    g_wu1, norms,
    inn, pool, u_buf, a0, a1, d_buf, ga, hid, dp_buf, ds_buf, x_buf, up_buf, fs, kd, kr, e_buf,
    wg, st, sv, cn, ng, ng_in, ar2, ar4, arv, asend, arecv, vsend, vrecv, xsend, xrecv, lsem,
):
    section = lax.axis_index("section")
    me = lax.axis_index("dp")
    v = n_dp // MEMBERS
    digit, rest = me // v, lax.rem(me, v)
    other = 1 - section

    def member(hop):
        return lax.rem(digit + hop, MEMBERS) * v + rest

    def near(hop):
        return digit * v + lax.rem(rest + hop, v)

    barrier = pltpu.get_barrier_semaphore()

    def greet(hop):
        pl.semaphore_signal(barrier, inc=1, device_id=(section, member(hop + 1)), device_id_type=MESH)

    def greet_near(hop):
        pl.semaphore_signal(barrier, inc=1, device_id=(section, near(hop + 1)), device_id_type=MESH)

    loop(MEMBERS - 1, greet)
    if v > 1:
        loop(v - 1, greet_near)
    pl.semaphore_signal(barrier, inc=1, device_id=(other, me), device_id_type=MESH)
    pl.semaphore_wait(barrier, MEMBERS + v - 1)

    def local_copy(src, dst, sem=0):
        return pltpu.make_async_copy(src, dst, lsem.at[sem])

    def to_sibling(src, dst, at):
        return pltpu.make_async_remote_copy(
            src_ref=src, dst_ref=dst, send_sem=xsend.at[at], recv_sem=xrecv.at[at],
            device_id=(other, me), device_id_type=MESH,
        )

    mine = pl.ds(2 * section, 2)
    theirs = pl.ds(2 * other, 2)
    copies = [
        to_sibling(features.at[theirs], x_buf.at[section], 0),
        to_sibling(upstream.at[theirs], up_buf.at[section], 1),
        local_copy(features.at[mine], x_buf.at[section], 0),
        local_copy(upstream.at[mine], up_buf.at[section], 1),
        local_copy(expand.at[0], e_buf, 2),
        local_copy(k0, kr, 3),
    ]
    for copy in copies:
        copy.start()

    fs[...] = jnp.zeros_like(fs)
    ng[...] = jnp.zeros_like(ng)
    guard = jnp.zeros((GUARD, C), BF16)
    for ref, count in ((a0, 4), (d_buf, 3)):
        for c in range(2):
            for k in range(count):
                ref[c, k, 0:GUARD] = guard
                ref[c, k, GUARD + PX :] = guard
    for c in range(2):
        a1[c, 0:GUARD] = guard
        a1[c, GUARD + PX :] = guard

    def half_side(c):
        return side_ref[2 * section + c] // 2

    def keep(c, j):
        half = half_side(c)
        bound = jnp.where(j < half, half, 0)
        tile = (lax.broadcasted_iota(jnp.int32, (16, 128), 0) < bound).astype(F32)
        return jnp.concatenate([tile] * (C // 128), 1)

    def crop_count(c):
        half = half_side(c)
        return (half * half).astype(F32)

    def ar_slots(rows, n):
        return (ar2 if rows == 2 else ar4).at[n % 2]

    def ar_start(n, c, rows):
        slots = ar_slots(len(rows), n).at[c]
        slots[digit] = jnp.concatenate(rows, 0)

        def send(hop):
            pltpu.make_async_remote_copy(
                src_ref=slots.at[digit], dst_ref=slots.at[digit], send_sem=asend.at[n % 2, c],
                recv_sem=arecv.at[n % 2, c], device_id=(section, member(hop + 1)),
                device_id_type=MESH,
            ).start()

        loop(MEMBERS - 1, send)

    def ar_wait(n, c, rows):
        slots = ar_slots(rows, n).at[c]
        arrived = slots.at[pl.ds(0, MEMBERS - 1)]
        pltpu.make_async_copy(arrived, arrived, asend.at[n % 2, c]).wait()
        pltpu.make_async_copy(arrived, arrived, arecv.at[n % 2, c]).wait()
        total = slots[0]
        for k in range(1, MEMBERS):
            total = total + slots[k]
        if v > 1:
            again = arv.at[n % 2, c]
            spare = [jnp.zeros((4 - rows, C), F32)] if rows < 4 else []
            again[rest] = jnp.concatenate([total] + spare, 0)

            def send(hop):
                pltpu.make_async_remote_copy(
                    src_ref=again.at[rest], dst_ref=again.at[rest], send_sem=vsend.at[n % 2, c],
                    recv_sem=vrecv.at[n % 2, c], device_id=(section, near(hop + 1)),
                    device_id_type=MESH,
                ).start()

            loop(v - 1, send)
            arrived = again.at[pl.ds(0, v - 1)]
            pltpu.make_async_copy(arrived, arrived, vsend.at[n % 2, c]).wait()
            pltpu.make_async_copy(arrived, arrived, vrecv.at[n % 2, c]).wait()
            total = again[0]
            for k in range(1, v):
                total = total + again[k]
        return [total[k : k + 1] for k in range(rows)]

    def down(sums):
        return jnp.sum(sums, axis=0, keepdims=True)

    def fold(value):
        return value[0:8] + value[8:16]

    def zeros(count):
        return tuple(jnp.zeros((8, C), F32) for _ in range(count))

    def each_column(count, body):
        sums = lax.fori_loop(0, 14, body, zeros(count))
        return [down(one) for one in sums]

    def moment_sums(c, value_of):
        def body(j, sums):
            value = value_of(j)
            weighted = value * keep(c, j)
            return (sums[0] + fold(weighted), sums[1] + fold(weighted * value))

        return each_column(2, body)

    def set_stats(c, index, totals, inverse, gain_row):
        center = totals[0] * inverse
        scaling = lax.rsqrt(totals[1] * inverse - center * center + EPSILON)
        gain = params[gain_row : gain_row + 1] * scaling
        shift_row = gain_row + 6 if gain_row < 6 else gain_row + 1
        st[c, index, 0:1] = center
        st[c, index, 1:2] = scaling
        st[c, index, 2:3] = gain
        st[c, index, 3:4] = params[shift_row : shift_row + 1] - center * gain

    def affine(c, index):
        return st[c, index, 2:3], st[c, index, 3:4]

    def hat_of(c, index):
        return st[c, index, 0:1], st[c, index, 1:2]

    def inverse_out(c):
        return cn[c, 1:2]

    def inverse_in(c):
        return cn[c, 2:3]

    def build_conv(raw):
        def shard(s):
            for k in range(2):
                fs[pl.ds(2048 * k + 63 * s, 64)] = raw[
                    pl.ds(pl.multiple_of(64 * s, 64), 64), 128 * k : 128 * k + 128
                ].astype(F32)

        loop(SHARDS, shard)
        lane = lax.broadcasted_iota(jnp.int32, (64, 256), 1) // 64

        def block(a):
            for tap in range(9):
                tiles = []
                for k in range(2):
                    at = 2048 * k + 224 * tap
                    tiles.append(
                        jnp.concatenate(
                            [
                                fs[pl.ds(at + a, 28, stride=4)],
                                jnp.zeros((4, 128), F32),
                                fs[pl.ds(at + 112 + a, 28, stride=4)],
                                jnp.zeros((4, 128), F32),
                            ],
                            0,
                        )
                    )
                dense = jnp.concatenate(tiles, 1)
                for g in range(4):
                    kd[a, 256 * tap + 64 * g : 256 * tap + 64 * g + 64] = jnp.where(
                        lane == g, dense, 0.0
                    ).astype(BF16)

        loop(4, block)

    def taps0():
        for a in range(3):
            for b in range(3):
                yield a * 3 + b, (0 if a == 1 else 1), (0 if b == 1 else 1), a, b

    def emit(dst, shape):
        copy = local_copy(wg.at[pl.ds(0, shape)], dst, 4)
        copy.start()
        copy.wait()

    def both(ref_of):
        return jnp.concatenate([ref_of(0), ref_of(1)], 0)

    def squeeze(c, b, pooled, wd, wu):
        width = wd.shape[1]
        raw = row_dot(pooled, wd[...], nn)
        squeezed = raw * sig(raw)
        gating = sig(row_dot(squeezed, wu[...], nn))
        sv[b, c, 0:1] = pooled
        sv[b, c, 1:2, 0:width] = raw
        sv[b, c, 2:3, 0:width] = squeezed
        sv[b, c, 3:4] = gating
        return gating

    def gate(c, b, index, conv_k, wd, wu, wc, proj_k):
        a, shift = affine(c, index)

        def pool_chunk(j, sums):
            z = pool[c, conv_k, chunk(j)] * a + shift
            excited = keep(c, j) * (z * sig(z))
            pool[c, 7, chunk(j)] = excited
            return (sums[0] + fold(excited),)

        pooled = each_column(1, pool_chunk)[0] / crop_count(c)
        gating = squeeze(c, b, pooled, wd, wu)

        def gate_chunk(j):
            ga[b, c, chunk(j)] = (pool[c, 7, chunk(j)] * gating).astype(BF16)

        loop(14, gate_chunk)

        def project(n):
            pool[c, proj_k, :, col(n)] = nn(ga[b, c], wc[:, col(n)])

        loop(4, project)
        return moment_sums(c, lambda j: pool[c, proj_k, chunk(j)])

    def ungate(c, b, index, conv_k, wd, wu, wc):
        width = wd.shape[1]

        def back(n):
            pool[c, 7, :, col(n)] = nt(dp_buf[c], wc[col(n)])

        loop(4, back)
        a, shift = affine(c, index)

        def gate_chunk(j, sums):
            z = pool[c, conv_k, chunk(j)] * a + shift
            excited = keep(c, j) * (z * sig(z))
            return (sums[0] + fold(pool[c, 7, chunk(j)] * excited),)

        d_gate = each_column(1, gate_chunk)[0]
        gating = sv[b, c, 3:4]
        d_raw = d_gate * gating * (1.0 - gating)
        raw = sv[b, c, 1:2, 0:width]
        d_squeeze = row_dot(d_raw, wu[...], nt) * slope_of(raw, sig(raw))
        d_pool = row_dot(d_squeeze, wd[...], nt) / crop_count(c)
        sv[b, c, 4:5] = d_raw
        sv[b, c, 5:6, 0:width] = d_squeeze
        center, scaling = hat_of(c, index)

        def slope_chunk(j, sums):
            value = pool[c, conv_k, chunk(j)]
            z = value * a + shift
            d = (pool[c, 7, chunk(j)] * gating + d_pool) * (keep(c, j) * slope_of(z, sig(z)))
            pool[c, 7, chunk(j)] = d
            return (sums[0] + fold(d), sums[1] + fold(d * ((value - center) * scaling)))

        return each_column(2, slope_chunk)

    def small_grads(b, wd, g_wd, g_wu):
        width = wd.shape[1]

        def pairs(x_row, x_width, y_row, y_width):
            xs, ys = [], []
            for c in range(2):
                xh, xl = split_rows([sv[b, c, x_row : x_row + 1, 0:x_width]])
                yh, yl = split_rows([sv[b, c, y_row : y_row + 1, 0:y_width]])
                xs += [xh[0], xh[0], xl[0]]
                ys += [yh[0], yl[0], yh[0]]
            return tn(stacked(xs), stacked(ys))

        wg[:, 0:width] = pairs(0, C, 5, width).astype(BF16)
        copy = local_copy(wg.at[:, pl.ds(0, width)], g_wd, 4)
        copy.start()
        grad_up = pairs(2, width, 4, C)
        rows = SE0 if b == 0 else SE1
        per = 2 * rows // SHARDS
        for h in range(2):
            for k in range(4):
                fs[pl.ds(512 * k + h, rows, stride=2)] = grad_up[
                    0:rows, 512 * h + 128 * k : 512 * h + 128 * k + 128
                ]
        copy.wait()
        for s in range(SHARDS):
            for k in range(4):
                wg[16 * s : 16 * s + 16, 128 * k : 128 * k + 128] = fs[
                    512 * k + per * s : 512 * k + per * s + 16
                ].astype(BF16)
        copy = local_copy(wg.at[pl.ds(0, 512), pl.ds(0, 512)], g_wu, 4)
        copy.start()
        copy.wait()

    def norm_coefficients(c, index, totals, inverse, gain_row, kind):
        center, scaling = hat_of(c, index)
        ng[gain_row : gain_row + 1] += totals[1]
        shift_row = gain_row + 6 if gain_row < 6 else gain_row + 1
        ng[shift_row : shift_row + 1] += totals[0]
        a = st[c, index, 2:3]
        slope = -a * scaling * (totals[1] * inverse)
        offset = -a * (totals[0] * inverse) - slope * center
        return a, slope, offset

    def conv_grad(act_of, v_of, dst):
        lane = lax.broadcasted_iota(jnp.int32, (64, 256), 1) // 64

        def block(a):
            for tap in range(9):
                dense = tn(
                    both(lambda c: act_of(c, tap, col(a))), both(lambda c: v_of(c, tap, col(a)))
                )
                own = jnp.where(lane == 0, dense[0:64], 0.0)
                for g in range(1, 4):
                    own = own + jnp.where(lane == g, dense[64 * g : 64 * g + 64], 0.0)
                for k in range(2):
                    at = 2048 * k + 224 * tap
                    fs[pl.ds(at + a, 28, stride=4)] = own[0:28, 128 * k : 128 * k + 128]
                    fs[pl.ds(at + 112 + a, 28, stride=4)] = own[32:60, 128 * k : 128 * k + 128]

        loop(4, block)

        def shard(s):
            for k in range(2):
                kr[pl.ds(pl.multiple_of(64 * s, 64), 64), 128 * k : 128 * k + 128] = fs[
                    pl.ds(2048 * k + 63 * s, 64)
                ].astype(BF16)

        loop(SHARDS, shard)
        copy = local_copy(kr, dst, 3)
        copy.start()
        copy.wait()

    def outer(left_of, right_of, tiles, dst):
        def tile(m):
            wg[col(m)] = tn(both(lambda c: left_of(c, col(m))), both(right_of)).astype(BF16)

        loop(tiles, tile)
        emit(dst, tiles * 256)

    for copy in copies:
        copy.wait()

    def gather_slices(ref, rows):
        pad = jnp.zeros((16 - rows, D), BF16)
        return jnp.concatenate(
            [
                jnp.concatenate([ref[:, D * j : D * j + D], pad], 0)
                for j in range(OUT)
            ],
            0,
        )

    def phases(c):
        for h in range(2):
            x = gather_slices(x_buf.at[h, c], 14)
            for n in range(4):
                y = nn(x, e_buf[:, 256 * n : 256 * n + 256])
                for j in range(OUT):
                    for k in range(2):
                        fs[pl.ds(512 * (2 * n + k) + 32 * j + 14 * h, 14)] = y[
                            16 * j : 16 * j + 14, 128 * k : 128 * k + 128
                        ]
        for q in range(2):
            def take(j):
                for k in range(8):
                    u_buf[c, q, chunk(j), 128 * k : 128 * k + 128] = fs[
                        pl.ds(512 * k + 32 * j + q, 16, stride=2)
                    ].astype(BF16)

            loop(14, take)

        for q in range(2):
            for r in range(2):
                def product(n):
                    inn[c, 2 * q + r, :, col(n)] = nn(
                        u_buf[c, q, :, 512 * r : 512 * r + 512], wa0[:, col(n)]
                    )

                loop(4, product)

        def body(j, sums):
            mask = keep(c, j)
            first, second = sums
            for k in range(4):
                value = inn[c, k, chunk(j)]
                weighted = value * mask
                first = first + fold(weighted)
                second = second + fold(weighted * value)
            return (first, second)

        sums = each_column(2, body)
        own = jnp.zeros((1, C), F32) + crop_count(c)
        ar_start(0, c, [sums[0], sums[1], own, own])

    loop(2, phases)
    load = local_copy(expand.at[1], e_buf, 2)
    load.start()
    build_conv(kr)
    again = local_copy(k1, kr, 3)
    again.start()
    load.wait()

    def cotangent(c):
        for h in range(2):
            x = gather_slices(up_buf.at[h, c], 7)
            for n in range(4):
                y = nn(x, e_buf[:, 256 * n : 256 * n + 256])
                for j in range(OUT):
                    count = 16 if h == 0 else 7
                    pool[c, 3, 16 * j + 7 * h : 16 * j + 7 * h + count, 256 * n : 256 * n + 256] = y[
                        16 * j : 16 * j + count
                    ]

    loop(2, cotangent)

    def entry_conv(c):
        totals = ar_wait(0, c, 4)
        cn[c, 0:1] = totals[2]
        cn[c, 1:2] = 1.0 / totals[2]
        cn[c, 2:3] = 0.25 / totals[2]
        set_stats(c, 0, totals, inverse_in(c), 0)
        a, shift = affine(c, 0)

        def activate(j):
            mask = keep(c, j)
            for q in range(2):
                for r in range(2):
                    z = inn[c, 2 * q + r, chunk(j)] * a + shift
                    act = mask * (z * sig(z))
                    a0[c, 2 * q + r, chunk(j, GUARD)] = act.astype(BF16)
                    if q == 1:
                        d_buf[c, r, chunk(j, GUARD)] = pltpu.roll(act, 1, 0).astype(BF16)

        loop(14, activate)

        def convolve(n):
            patches = []
            for tap, q, r, ta, tb in taps0():
                at = GUARD - 16 if tb == 0 else GUARD
                src = d_buf.at[c, r] if ta == 0 else a0.at[c, 2 * q + r]
                patches.append(src[at : at + PX, col(n)])
            pool[c, 0, :, col(n)] = nn(jnp.concatenate(patches, 1), kd[n])

        loop(4, convolve)
        ar_start(1, c, moment_sums(c, lambda j: pool[c, 0, chunk(j)]))

    loop(2, entry_conv)

    def strided(c):
        def product(n):
            pool[c, 2, :, col(n)] = nn(u_buf[c, 0, :, 0:512], ws[:, col(n)])

        loop(4, product)

    loop(2, strided)
    again.wait()

    def entry_gate(c):
        totals = ar_wait(1, c, 2)
        set_stats(c, 1, totals, inverse_out(c), 1)
        sums = gate(c, 0, 1, 0, wd0, wu0, wc0, 1)
        ar_start(2, c, sums + moment_sums(c, lambda j: pool[c, 2, chunk(j)]))

    loop(2, entry_gate)
    build_conv(kr)

    def entry_pre(c, j):
        a, shift = affine(c, 2)
        short_a, short_shift = affine(c, 3)
        return (
            pool[c, 1, chunk(j)] * a + pool[c, 2, chunk(j)] * short_a + (shift + short_shift)
        )

    def entry_out(c):
        totals = ar_wait(2, c, 4)
        set_stats(c, 2, totals[0:2], inverse_out(c), 2)
        set_stats(c, 3, totals[2:4], inverse_out(c), 12)

        def finish(j):
            z = entry_pre(c, j)
            hid[c, chunk(j)] = (keep(c, j) * (z * sig(z))).astype(BF16)

        loop(14, finish)

        def product(n):
            pool[c, 4, :, col(n)] = nn(hid[c], wa1[:, col(n)])

        loop(4, product)
        ar_start(3, c, moment_sums(c, lambda j: pool[c, 4, chunk(j)]))

    loop(2, entry_out)

    def body_conv(c):
        set_stats(c, 4, ar_wait(3, c, 2), inverse_out(c), 3)
        a, shift = affine(c, 4)

        def activate(j):
            z = pool[c, 4, chunk(j)] * a + shift
            act = keep(c, j) * (z * sig(z))
            a1[c, chunk(j, GUARD)] = act.astype(BF16)
            d_buf[c, 0, chunk(j, GUARD)] = pltpu.roll(act, 1, 0).astype(BF16)
            d_buf[c, 1, chunk(j, GUARD)] = pltpu.roll(act, 15, 0).astype(BF16)

        loop(14, activate)

        def convolve(n):
            rows = (d_buf.at[c, 0], a1.at[c], d_buf.at[c, 1])
            patches = [
                rows[ta][16 * tb : 16 * tb + PX, col(n)] for ta in range(3) for tb in range(3)
            ]
            pool[c, 5, :, col(n)] = nn(jnp.concatenate(patches, 1), kd[n])

        loop(4, convolve)
        ar_start(4, c, moment_sums(c, lambda j: pool[c, 5, chunk(j)]))

    loop(2, body_conv)

    def body_gate(c):
        set_stats(c, 5, ar_wait(4, c, 2), inverse_out(c), 4)
        ar_start(5, c, gate(c, 1, 5, 5, wd1, wu1, wc1, 6))

    loop(2, body_gate)

    def body_out(c):
        set_stats(c, 6, ar_wait(5, c, 2), inverse_out(c), 5)
        a, shift = affine(c, 6)
        center, scaling = hat_of(c, 6)

        def finish(j, sums):
            value = pool[c, 6, chunk(j)]
            z = value * a + shift + hid[c, chunk(j)].astype(F32)
            mask = keep(c, j)
            s = sig(z)
            dp_buf[c, chunk(j)] = (mask * (z * s)).astype(BF16)
            d_pre = pool[c, 3, chunk(j)] * (mask * slope_of(z, s))
            pool[c, 3, chunk(j)] = d_pre
            return (sums[0] + fold(d_pre), sums[1] + fold(d_pre * ((value - center) * scaling)))

        ar_start(6, c, each_column(2, finish))

    loop(2, body_out)

    def narrow(value, store):
        for start, width in ((0, 256), (256, 256), (512, 256), (768, 128)):
            store(start, width, nt(value, e_buf[start : start + width]))

    def body_emit(c):
        def store(start, width, y):
            for j in range(OUT):
                for h in range(2):
                    up_buf[h, c, :, D * j + start : D * j + start + width] = y[
                        16 * j + 7 * h : 16 * j + 7 * h + 7
                    ].astype(BF16)

        narrow(dp_buf[c], store)

    loop(2, body_emit)
    out_copies = [
        to_sibling(up_buf.at[other], out.at[mine], 2),
        local_copy(up_buf.at[section], out.at[mine], 1),
        local_copy(expand.at[0], e_buf, 2),
    ]
    for copy in out_copies:
        copy.start()

    def body_back_out(c):
        a, slope, offset = norm_coefficients(c, 6, ar_wait(6, c, 2), inverse_out(c), 5, 0)

        def project(j):
            value = pool[c, 6, chunk(j)]
            dp_buf[c, chunk(j)] = (
                keep(c, j) * (a * pool[c, 3, chunk(j)] + slope * value + offset)
            ).astype(BF16)

        loop(14, project)
        ar_start(7, c, ungate(c, 1, 5, 5, wd1, wu1, wc1))

    loop(2, body_back_out)
    outer(lambda c, l: ga[1, c, :, l], lambda c: dp_buf[c], 4, g_wc1)
    small_grads(1, wd1, g_wd1, g_wu1)

    def conv_cotangent(c, index, conv_k, a, slope, offset, versions):
        def body(j):
            d = keep(c, j) * (a * pool[c, 7, chunk(j)] + slope * pool[c, conv_k, chunk(j)] + offset)
            d_buf[c, 0, chunk(j, GUARD)] = d.astype(BF16)
            d_buf[c, 1, chunk(j, GUARD)] = pltpu.roll(d, 15, 0).astype(BF16)
            if versions == 3:
                d_buf[c, 2, chunk(j, GUARD)] = pltpu.roll(d, 1, 0).astype(BF16)

        loop(14, body)

    def v_body(c, tap, lanes):
        ta, tb = tap // 3, tap % 3
        return d_buf[c, (1, 0, 2)[ta], 32 - 16 * tb : 32 - 16 * tb + PX, lanes]

    def v_entry(c, tap, lanes):
        ta, tb = tap // 3, tap % 3
        at = 32 if tb == 0 else 16
        return d_buf[c, 1 if ta == 0 else 0, at : at + PX, lanes]

    def body_back_conv(c):
        a, slope, offset = norm_coefficients(c, 5, ar_wait(7, c, 2), inverse_out(c), 4, 0)
        conv_cotangent(c, 5, 5, a, slope, offset, 3)

        def back(n):
            total = nt(v_body(c, 0, col(n)), kd[n, 0:256])
            for tap in range(1, 9):
                total = total + nt(v_body(c, tap, col(n)), kd[n, 256 * tap : 256 * tap + 256])
            pool[c, 7, :, col(n)] = total

        loop(4, back)
        a, shift = affine(c, 4)
        center, scaling = hat_of(c, 4)

        def body(j, sums):
            value = pool[c, 4, chunk(j)]
            z = value * a + shift
            d = pool[c, 7, chunk(j)] * (keep(c, j) * slope_of(z, sig(z)))
            pool[c, 7, chunk(j)] = d
            return (sums[0] + fold(d), sums[1] + fold(d * ((value - center) * scaling)))

        ar_start(8, c, each_column(2, body))

    loop(2, body_back_conv)
    again = local_copy(k0, kr, 3)
    conv_grad(lambda c, tap, l: a1[c, GUARD : GUARD + PX, l], v_body, g_k1)
    again.start()

    def body_back_in(c):
        a, slope, offset = norm_coefficients(c, 4, ar_wait(8, c, 2), inverse_out(c), 3, 0)

        def body(j):
            dp_buf[c, chunk(j)] = (
                keep(c, j) * (a * pool[c, 7, chunk(j)] + slope * pool[c, 4, chunk(j)] + offset)
            ).astype(BF16)

        loop(14, body)

        def back(n):
            pool[c, 3, :, col(n)] = (
                (nt(dp_buf[c], wa1[col(n)]) + pool[c, 3, :, col(n)]).astype(BF16).astype(F32)
            )

        loop(4, back)
        center, scaling = hat_of(c, 2)
        short_center, short_scaling = hat_of(c, 3)

        def pre(j, sums):
            z = entry_pre(c, j)
            d = pool[c, 3, chunk(j)] * (keep(c, j) * slope_of(z, sig(z)))
            pool[c, 3, chunk(j)] = d
            return (
                sums[0] + fold(d),
                sums[1] + fold(d * ((pool[c, 1, chunk(j)] - center) * scaling)),
                sums[2] + fold(d * ((pool[c, 2, chunk(j)] - short_center) * short_scaling)),
            )

        sums = each_column(3, pre)
        ar_start(9, c, sums + [sums[0]])

    loop(2, body_back_in)
    outer(lambda c, l: hid[c, :, l], lambda c: dp_buf[c], 4, g_wa1)
    again.wait()
    build_conv(kr)

    def entry_back_out(c):
        totals = ar_wait(9, c, 4)
        a, slope, offset = norm_coefficients(c, 2, totals[0:2], inverse_out(c), 2, 0)
        short = norm_coefficients(c, 3, [totals[0], totals[2]], inverse_out(c), 12, 0)

        def project(j):
            mask = keep(c, j)
            d = pool[c, 3, chunk(j)]
            dp_buf[c, chunk(j)] = (
                mask * (a * d + slope * pool[c, 1, chunk(j)] + offset)
            ).astype(BF16)
            ds_buf[c, chunk(j)] = (
                mask * (short[0] * d + short[1] * pool[c, 2, chunk(j)] + short[2])
            ).astype(BF16)

        loop(14, project)
        ar_start(10, c, ungate(c, 0, 1, 0, wd0, wu0, wc0))

    loop(2, entry_back_out)
    outer(lambda c, l: ga[0, c, :, l], lambda c: dp_buf[c], 4, g_wc0)
    outer(lambda c, l: u_buf[c, 0, :, l], lambda c: ds_buf[c], 2, g_ws)
    small_grads(0, wd0, g_wd0, g_wu0)

    def entry_back_conv(c):
        a, slope, offset = norm_coefficients(c, 1, ar_wait(10, c, 2), inverse_out(c), 1, 0)
        conv_cotangent(c, 1, 0, a, slope, offset, 2)
        for q in range(2):
            for r in range(2):
                def back(n):
                    total = None
                    for tap, tq, tr, ta, tb in taps0():
                        if (tq, tr) == (q, r):
                            term = nt(v_entry(c, tap, col(n)), kd[n, 256 * tap : 256 * tap + 256])
                            total = term if total is None else total + term
                    pool[c, 4 + 2 * q + r, :, col(n)] = total

                loop(4, back)
        a, shift = affine(c, 0)
        center, scaling = hat_of(c, 0)

        def body(j, sums):
            mask = keep(c, j)
            first, second = sums
            for k in range(4):
                value = inn[c, k, chunk(j)]
                z = value * a + shift
                d = pool[c, 4 + k, chunk(j)] * (mask * slope_of(z, sig(z)))
                pool[c, 4 + k, chunk(j)] = d
                first = first + fold(d)
                second = second + fold(d * ((value - center) * scaling))
            return (first, second)

        ar_start(11, c, each_column(2, body))

    loop(2, entry_back_conv)

    def act_entry(c, tap, lanes):
        q = 0 if tap // 3 == 1 else 1
        r = 0 if tap % 3 == 1 else 1
        return a0[c, 2 * q + r, GUARD : GUARD + PX, lanes]

    conv_grad(act_entry, v_entry, g_k0)
    for copy in out_copies:
        copy.wait()

    def entry_back_in(c):
        a, slope, offset = norm_coefficients(c, 0, ar_wait(11, c, 2), inverse_in(c), 0, 0)

        def body(j):
            mask = keep(c, j)
            for k in range(4):
                a0[c, k, chunk(j, GUARD)] = (
                    mask * (a * pool[c, 4 + k, chunk(j)] + slope * inn[c, k, chunk(j)] + offset)
                ).astype(BF16)

        loop(14, body)
        for q in range(2):
            for r in range(2):
                def back(n):
                    total = nt(a0[c, 2 * q + r, GUARD : GUARD + PX], wa0[col(n)])
                    if q == 0 and r == 0:
                        total = total + nt(ds_buf[c], ws[col(n)])
                    at = pl.ds(pl.multiple_of(512 * r + 256 * n, 256), 256)
                    ga[0, c, :, at] = total.astype(BF16)

                loop(2, back)

            def store(start, width, y):
                for j in range(OUT):
                    for k in range(width // 128):
                        fs[pl.ds(512 * (start // 128 + k) + 32 * j + q, 14, stride=2)] = y[
                            16 * j : 16 * j + 14, 128 * k : 128 * k + 128
                        ]

            narrow(ga[0, c], store)
        for h in range(2):
            for j in range(OUT):
                for k in range(7):
                    x_buf[h, c, :, D * j + 128 * k : D * j + 128 * k + 128] = fs[
                        512 * k + 32 * j + 14 * h : 512 * k + 32 * j + 14 * h + 14
                    ].astype(BF16)

    loop(2, entry_back_in)
    last = [
        to_sibling(x_buf.at[other], grad.at[mine], 4),
        local_copy(x_buf.at[section], grad.at[mine], 0),
        to_sibling(ng, ng_in, 3),
    ]
    for copy in last:
        copy.start()

    def input_grad(m):
        total = None
        for q in range(2):
            for r in range(2):
                at = pl.ds(pl.multiple_of(512 * r + 256 * m, 256), 256)
                term = tn(
                    both(lambda c: u_buf[c, q, :, at]),
                    both(lambda c: a0[c, 2 * q + r, GUARD : GUARD + PX]),
                )
                total = term if total is None else total + term
        wg[col(m)] = total.astype(BF16)

    loop(2, input_grad)
    emit(g_wa0, 512)
    for copy in last:
        copy.wait()
    norms[...] = ng[...] + ng_in[...]


def lane_maps():
    at = np.arange(D)
    first = np.zeros((D, C), np.float32)
    first[at, at // 14 * 16 + at % 14] = 1
    second = np.zeros((D, C), np.float32)
    second[at, at // 28 * 32 + at % 28] = 1
    return np.stack([first, second])


def main_call(n_dp, *args):
    v = n_dp // MEMBERS
    any_space = pl.BlockSpec(memory_space=pl.ANY)
    vmem = pl.BlockSpec(memory_space=pltpu.VMEM)
    smem = pl.BlockSpec(memory_space=pltpu.SMEM)
    shape = lambda *s, dtype=BF16: jax.ShapeDtypeStruct(s, dtype)
    in_specs = [any_space, any_space, smem, any_space] + [
        vmem, vmem, any_space, vmem, vmem, vmem, vmem, any_space, vmem, vmem, vmem, vmem
    ]
    outs = [
        shape(4, 7, 12544), shape(4, 14, 12544),
        shape(512, C), shape(512, C), shape(2048, 256), shape(C, C), shape(C, 128), shape(512, 512),
        shape(C, C), shape(2048, 256), shape(C, C), shape(C, 256), shape(512, 512),
        shape(16, C, dtype=F32),
    ]
    dma = pltpu.SemaphoreType.DMA
    scratch = [
        pltpu.VMEM((2, 4, PX, C), F32),
        pltpu.VMEM((2, 8, PX, C), F32),
        pltpu.VMEM((2, 2, PX, C), BF16),
        pltpu.VMEM((2, 4, PX + 2 * GUARD, C), BF16),
        pltpu.VMEM((2, PX + 2 * GUARD, C), BF16),
        pltpu.VMEM((2, 3, PX + 2 * GUARD, C), BF16),
        pltpu.VMEM((2, 2, PX, C), BF16),
        pltpu.VMEM((2, PX, C), BF16),
        pltpu.VMEM((2, PX, C), BF16),
        pltpu.VMEM((2, PX, C), BF16),
        pltpu.VMEM((2, 2, 14, 12544), BF16),
        pltpu.VMEM((2, 2, 7, 12544), BF16),
        pltpu.VMEM((4096, 128), F32),
        pltpu.VMEM((4, 2304, 256), BF16),
        pltpu.VMEM((2048, 256), BF16),
        pltpu.VMEM((D, C), BF16),
        pltpu.VMEM((C, C), BF16),
        pltpu.VMEM((2, 7, 8, C), F32),
        pltpu.VMEM((2, 2, 8, C), F32),
        pltpu.VMEM((2, 8, C), F32),
        pltpu.VMEM((16, C), F32),
        pltpu.VMEM((16, C), F32),
        pltpu.VMEM((2, 2, MEMBERS, 2, C), F32),
        pltpu.VMEM((2, 2, MEMBERS, 4, C), F32),
        pltpu.VMEM((2, 2, v, 4, C), F32),
        dma((2, 2)), dma((2, 2)), dma((2, 2)), dma((2, 2)), dma((5,)), dma((5,)), dma((5,)),
    ]
    return pl.pallas_call(
        functools.partial(main_kernel, n_dp),
        out_shape=outs,
        in_specs=in_specs,
        out_specs=[any_space] * 13 + [vmem],
        scratch_shapes=scratch,
        compiler_params=pltpu.CompilerParams(
            collective_id=1, has_side_effects=True, vmem_limit_bytes=64 << 20
        ),
    )(*args)


def widen(values):
    shape = values.shape
    values = values.reshape(shape[:-1] + (shape[-1] // 28, 28))
    values = jnp.pad(values, [(0, 0)] * len(shape) + [(0, 4)])
    return values.reshape(shape[:-1] + (-1,))


def rows_to(values, count):
    return jnp.pad(values, ((0, count - values.shape[0]), (0, 0)))


def pack_wu(values):
    parts = values.reshape(-1, 448)
    return rows_to(widen(parts), 16)


SHAPES = (
    (DIN, D), (9 * 56, D), (D, D), (D, SE0), (SE0, D), (DIN, D), (D, D), (9 * 56, D), (D, D),
    (D, SE1), (SE1, D),
)


def pack_rows(values):
    wide = widen(values.reshape(SHARDS, -1, D))
    rows = wide.shape[1]
    return jnp.pad(wide, ((0, 0), (0, -rows % 16), (0, 0))).reshape(-1, C)


def pack_conv(values):
    wide = widen(values.reshape(SHARDS, 63, 224))
    return jnp.pad(wide, ((0, 0), (0, 1), (0, 0))).reshape(-1, 256)


def pack_down(values, width):
    narrow = values.reshape(SHARDS, 28, width)
    return jnp.pad(narrow, ((0, 0), (0, 4), (0, -width % 128))).reshape(C, -1)


def pack_up(values, rows):
    return rows_to(widen(values.reshape(rows, D)), rows + -rows % 128)


def unwiden(values):
    shape = values.shape
    return values.reshape(shape[:-1] + (shape[-1] // 32, 32))[..., :28].reshape(shape[:-1] + (-1,))


def unpack_rows(values, rows):
    return unwiden(values.reshape(SHARDS, -1, C)[:, :rows]).reshape(-1)


def unpack_conv(values):
    return unwiden(values.reshape(SHARDS, 64, 256)[:, :63]).reshape(-1)


def unpack_down(values, width):
    return values.reshape(SHARDS, 32, -1)[:, :28, :width].reshape(-1)


def unpack_up(values, rows):
    return unwiden(values.reshape(SHARDS, 16, 512)[:, : 2 * rows // SHARDS]).reshape(-1)


def local(
    features, crop_side, upstream,
    entry_in, entry_group, entry_out, entry_down, entry_up, shortcut_weight,
    body_in, body_group, body_out, body_down, body_up,
    norm_gain, norm_shift, shortcut_gain, shortcut_shift,
):
    section = lax.axis_index("section")
    n_dp = lax.axis_size("dp")
    shards = (
        entry_in, entry_group, entry_out, entry_down, entry_up, shortcut_weight,
        body_in, body_group, body_out, body_down, body_up,
    )
    together = lax.all_gather(jnp.concatenate(shards), ("section", "dp"), axis=0, tiled=False)
    whole = []
    start = 0
    for shard in shards:
        whole.append(together[:, start : start + shard.shape[0]])
        start += shard.shape[0]
    gains, shifts, short_gain, short_shift = (
        lax.all_gather(part, "section", axis=0, tiled=True)
        for part in (norm_gain, norm_shift, shortcut_gain, shortcut_shift)
    )
    params = jnp.concatenate(
        [
            gains.reshape(6, D), shifts.reshape(6, D), short_gain.astype(F32)[None],
            short_shift.astype(F32)[None], jnp.zeros((2, D), F32),
        ]
    )
    expand = jnp.asarray(lane_maps(), BF16)
    (
        output, d_features, g_wa0, g_ws, g_k0, g_wc0, g_wd0, g_wu0, g_wa1, g_k1, g_wc1, g_wd1,
        g_wu1, norms,
    ) = main_call(
        n_dp, features, upstream, crop_side, expand, pack_rows(whole[0]), pack_rows(whole[5]),
        pack_conv(whole[1]), pack_rows(whole[2]), pack_down(whole[3], SE0),
        pack_up(whole[4], SE0), pack_rows(whole[6]), pack_conv(whole[7]), pack_rows(whole[8]),
        pack_down(whole[9], SE1), pack_up(whole[10], SE1), widen(params),
    )
    order = (
        unpack_rows(g_wa0, 14), unpack_conv(g_k0), unpack_rows(g_wc0, 28),
        unpack_down(g_wd0, SE0), unpack_up(g_wu0, SE0), unpack_rows(g_ws, 14),
        unpack_rows(g_wa1, 28), unpack_conv(g_k1), unpack_rows(g_wc1, 28),
        unpack_down(g_wd1, SE1), unpack_up(g_wu1, SE1),
    )
    devices = 2 * n_dp
    packed = jnp.concatenate([one.reshape(devices, -1) for one in order], 1).astype(F32)
    summed = lax.psum_scatter(packed, ("section", "dp"), scatter_dimension=0, tiled=False)
    weight_out = []
    start = 0
    for shard in shards:
        weight_out.append(summed[start : start + shard.shape[0]])
        start += shard.shape[0]
    rows = unwiden(norms)
    own = lambda at: lax.dynamic_slice_in_dim(rows, at + 3 * section, 3, 0)[None]
    width = shortcut_gain.shape[0]
    short = lax.dynamic_slice_in_dim(rows[12:14], section * width, width, 1)
    return (output, d_features, *weight_out, own(0), own(6), short[0], short[1])


def solution(mesh):
    rows = P("dp", "section", None)
    flat = P(("section", "dp"))
    params = (P("section", None, None), P("section", None, None), P("section"), P("section"))
    return jax.shard_map(
        local,
        mesh=mesh,
        in_specs=(rows, P("dp"), rows) + (flat,) * 11 + params,
        out_specs=(rows, rows) + (flat,) * 11 + params,
        check_vma=False,
    )
```

```python
import functools

import jax
import jax.numpy as jnp
import numpy as np
from jax import lax
from jax.experimental import pallas as pl
from jax.experimental.pallas import tpu as pltpu
from jax.sharding import PartitionSpec as P

D = 896
DIN = 448
OUT = 14
IN = 28
SE0 = 112
SE1 = 224
EPSILON = 1e-05
F32 = jnp.float32
BF16 = jnp.bfloat16
MESH = pl.DeviceIdType.MESH
C = 1024
PX = 224
GUARD = 16
MEMBERS = 16
SHARDS = 32
ROWS = {
    "wa0": (0, 16), "k0": (16, 16), "ws": (32, 16), "misc0": (48, 16), "wc0": (64, 32),
    "wa1": (96, 32), "k1": (128, 16), "misc1": (144, 16), "wc1": (160, 32),
}
ORDER = ("wa0", "k0", "ws", "wd0", "wu0", "wc0", "wa1", "k1", "wd1", "wu1", "wc1")
LINES = (98, 112, 98, 28, 28, 196, 196, 112, 49, 49, 196)
GATHERS = ((0, 16), (16, 48), (48, 96), (96, 144), (144, 192))
SCATTERS = ((144, 192), (96, 144), (32, 96), (16, 32), (0, 16))


def dot(a, b, dims):
    return lax.dot_general(a, b, ((dims[:1], dims[1:]), ((), ())), preferred_element_type=F32)


def nn(a, b):
    return dot(a, b, (1, 0))


def nt(a, b):
    return dot(a, b, (1, 1))


def tn(a, b):
    return dot(a, b, (0, 0))


def sig(z):
    return jnp.tanh(z * 0.5) * 0.5 + 0.5


def slope_of(z, s):
    return s * (1.0 + z * (1.0 - s))


def split_rows(rows):
    high = [r.astype(BF16).astype(F32) for r in rows]
    low = [r - h for r, h in zip(rows, high)]
    return high, low


def stacked(rows):
    pad = jnp.zeros((16 - len(rows), rows[0].shape[1]), F32)
    return jnp.concatenate(list(rows) + [pad], 0).astype(BF16)


def row_dot(row, weight, mul):
    high, low = split_rows([row])
    both = mul(stacked(high + low), weight)
    return both[0:1] + both[1:2]


def col(n, width=256):
    return pl.ds(pl.multiple_of(n * width, width), width)


def chunk(j, base=0):
    return pl.ds(pl.multiple_of(j * 16 + base, 16), 16)


def loop(count, body):
    def step(i, carry):
        body(i)
        return carry

    lax.fori_loop(0, count, step, 0)


def main_kernel(
    n_dp, features, upstream, side_ref, expand, gain_in, shift_in, short_gain_in, short_shift_in,
    l_wa0, l_k0, l_ws, l_wd0, l_wu0, l_wc0, l_wa1, l_k1, l_wd1, l_wu1, l_wc1,
    out, grad, o_wa0, o_k0, o_ws, o_wd0, o_wu0, o_wc0, o_wa1, o_k1, o_wd1, o_wu1, o_wc1,
    gain_out, shift_out, short_gain_out, short_shift_out, land_d, land_c, land_b, land_a,
    inn, pool, u_buf, a0, a1, d_buf, ga, hid, dp_buf, x_buf, up_buf, fs, kd, e_buf,
    w, wd0, wu0, wd1, wu1, stage, params, pair, st, sv, cn, ng, ng_in, ar2, ar4, arv,
    asend, arecv, vsend, vrecv, xsend, xrecv, lsem, gsend, grecv, rsend, rrecv,
):
    section = lax.axis_index("section")
    me = lax.axis_index("dp")
    v = n_dp // MEMBERS
    digit, rest = me // v, lax.rem(me, v)
    other = 1 - section

    def member(hop):
        return lax.rem(digit + hop, MEMBERS) * v + rest

    def near(hop):
        return digit * v + lax.rem(rest + hop, v)

    barrier = pltpu.get_barrier_semaphore()

    def greet(hop):
        pl.semaphore_signal(barrier, inc=1, device_id=(section, member(hop + 1)), device_id_type=MESH)

    def greet_near(hop):
        pl.semaphore_signal(barrier, inc=1, device_id=(section, near(hop + 1)), device_id_type=MESH)

    loop(MEMBERS - 1, greet)
    if v > 1:
        loop(v - 1, greet_near)
    pl.semaphore_signal(barrier, inc=1, device_id=(other, me), device_id_type=MESH)
    pl.semaphore_wait(barrier, MEMBERS + v - 1)

    def local_copy(src, dst, sem=0):
        return pltpu.make_async_copy(src, dst, lsem.at[sem])

    def to_sibling(src, dst, at):
        return pltpu.make_async_remote_copy(
            src_ref=src, dst_ref=dst, send_sem=xsend.at[at], recv_sem=xrecv.at[at],
            device_id=(other, me), device_id_type=MESH,
        )

    mine = pl.ds(2 * section, 2)
    theirs = pl.ds(2 * other, 2)
    load_map = local_copy(expand.at[1], e_buf, 2)
    copies = [
        to_sibling(features.at[theirs], x_buf.at[section], 0),
        to_sibling(upstream.at[theirs], up_buf.at[section], 1),
        local_copy(features.at[mine], x_buf.at[section], 0),
        local_copy(upstream.at[mine], up_buf.at[section], 1),
    ]
    load_map.start()
    for copy in copies:
        copy.start()

    fs[...] = jnp.zeros_like(fs)
    ng[...] = jnp.zeros_like(ng)
    guard = jnp.zeros((GUARD, C), BF16)
    for ref, count in ((a0, 4), (d_buf, 2)):
        for c in range(2):
            for k in range(count):
                ref[c, k, 0:GUARD] = guard
                ref[c, k, GUARD + PX :] = guard
    for c in range(2):
        for ref in (a1, dp_buf):
            ref[c, 0:GUARD] = guard
            ref[c, GUARD + PX :] = guard

    def dp_of(c):
        return dp_buf[c, GUARD : GUARD + PX]

    def half_side(c):
        return side_ref[2 * section + c] // 2

    def keep(c, j):
        half = half_side(c)
        bound = jnp.where(j < half, half, 0)
        tile = (lax.broadcasted_iota(jnp.int32, (16, 128), 0) < bound).astype(F32)
        return jnp.concatenate([tile] * (C // 128), 1)

    def crop_count(c):
        half = half_side(c)
        return (half * half).astype(F32)

    def ar_slots(rows, n):
        return ar2.at[n % 2] if rows == 2 else ar4

    def ar_start(n, c, rows):
        slots = ar_slots(len(rows), n).at[c]
        slots[digit] = jnp.concatenate(rows, 0)

        def send(hop):
            pltpu.make_async_remote_copy(
                src_ref=slots.at[digit], dst_ref=slots.at[digit], send_sem=asend.at[n % 2, c],
                recv_sem=arecv.at[n % 2, c], device_id=(section, member(hop + 1)),
                device_id_type=MESH,
            ).start()

        loop(MEMBERS - 1, send)

    def ar_wait(n, c, rows):
        slots = ar_slots(rows, n).at[c]
        arrived = slots.at[pl.ds(0, MEMBERS - 1)]
        pltpu.make_async_copy(arrived, arrived, asend.at[n % 2, c]).wait()
        pltpu.make_async_copy(arrived, arrived, arecv.at[n % 2, c]).wait()
        total = slots[0]
        for k in range(1, MEMBERS):
            total = total + slots[k]
        if v > 1:
            again = arv.at[n % 2, c]
            spare = [jnp.zeros((4 - rows, C), F32)] if rows < 4 else []
            again[rest] = jnp.concatenate([total] + spare, 0)

            def send(hop):
                pltpu.make_async_remote_copy(
                    src_ref=again.at[rest], dst_ref=again.at[rest], send_sem=vsend.at[n % 2, c],
                    recv_sem=vrecv.at[n % 2, c], device_id=(section, near(hop + 1)),
                    device_id_type=MESH,
                ).start()

            loop(v - 1, send)
            arrived = again.at[pl.ds(0, v - 1)]
            pltpu.make_async_copy(arrived, arrived, vsend.at[n % 2, c]).wait()
            pltpu.make_async_copy(arrived, arrived, vrecv.at[n % 2, c]).wait()
            total = again[0]
            for k in range(1, v):
                total = total + again[k]
        return [total[k : k + 1] for k in range(rows)]

    def down(sums):
        return jnp.sum(sums, axis=0, keepdims=True)

    def fold(value):
        return value[0:8] + value[8:16]

    def zeros(count):
        return tuple(jnp.zeros((8, C), F32) for _ in range(count))

    def each_column(count, body):
        sums = lax.fori_loop(0, 14, body, zeros(count))
        return [down(one) for one in sums]

    def moment_sums(c, value_of):
        def body(j, sums):
            value = value_of(j)
            weighted = value * keep(c, j)
            return (sums[0] + fold(weighted), sums[1] + fold(weighted * value))

        return each_column(2, body)

    def set_stats(c, index, totals, inverse, gain_row):
        center = totals[0] * inverse
        scaling = lax.rsqrt(totals[1] * inverse - center * center + EPSILON)
        gain = params[gain_row : gain_row + 1] * scaling
        shift_row = gain_row + 6 if gain_row < 6 else gain_row + 1
        st[c, index, 0:1] = center
        st[c, index, 1:2] = scaling
        st[c, index, 2:3] = gain
        st[c, index, 3:4] = params[shift_row : shift_row + 1] - center * gain

    def affine(c, index):
        return st[c, index, 2:3], st[c, index, 3:4]

    def hat_of(c, index):
        return st[c, index, 0:1], st[c, index, 1:2]

    def inverse_out(c):
        return cn[c, 1:2]

    def inverse_in(c):
        return cn[c, 2:3]

    def place(shard):
        return shard // 16, lax.rem(shard // 4, 4), lax.rem(shard, 4)

    def cols_of(name, lanes):
        at, count = ROWS[name]
        value = w[:, :, :, at : at + count, lanes]
        return value.reshape(SHARDS * count, value.shape[-1])

    def rows_index(name, n):
        at, count = ROWS[name]
        if count == 16:
            return (n, slice(None), slice(None), slice(at, at + 16))
        return (n // 2, pl.ds(2 * lax.rem(n, 2), 2), slice(None), slice(at, at + 32))

    def rows_of(name, n):
        return w[rows_index(name, n)].reshape(256, C)

    def put_rows(name, n, value):
        shape = (4, 4, 16, C) if ROWS[name][1] == 16 else (2, 4, 32, C)
        w[rows_index(name, n)] = value.astype(BF16).reshape(shape)

    def shard_rows(name, shard):
        at, count = ROWS[name]
        return w[(*place(shard), slice(at, at + count))].astype(F32)

    def put_shard(name, shard, value):
        at, count = ROWS[name]
        w[(*place(shard), slice(at, at + count))] = value.astype(BF16)

    def tile(k):
        return slice(128 * k, 128 * k + 128)

    def build_conv(name):
        def shard(s):
            rows = shard_rows(name, s)
            for a in range(4):
                for k in range(2):
                    fs[pl.ds(2048 * k + 63 * s + a, 16, stride=4)] = rows[:, tile(2 * a + k)]

        loop(SHARDS, shard)
        lane = lax.broadcasted_iota(jnp.int32, (64, 256), 1) // 64

        def block(a):
            for tap in range(9):
                tiles = []
                for k in range(2):
                    at = 2048 * k + 224 * tap
                    tiles.append(
                        jnp.concatenate(
                            [
                                fs[pl.ds(at + a, 28, stride=4)],
                                jnp.zeros((4, 128), F32),
                                fs[pl.ds(at + 112 + a, 28, stride=4)],
                                jnp.zeros((4, 128), F32),
                            ],
                            0,
                        )
                    )
                dense = jnp.concatenate(tiles, 1)
                for g in range(4):
                    kd[a, 256 * tap + 64 * g : 256 * tap + 64 * g + 64] = jnp.where(
                        lane == g, dense, 0.0
                    ).astype(BF16)

        loop(4, block)

    def build_small(b):
        wd, wu = (wd0, wu0) if b == 0 else (wd1, wu1)
        fs[...] = jnp.zeros_like(fs)

        def shard(s):
            rows = shard_rows("misc0" if b == 0 else "misc1", s)
            if b == 0:
                for k in range(8):
                    fs[pl.ds(32 * s + k, 4, stride=8)] = rows[0:4, tile(k)]
                    fs[pl.ds(1024 + 256 * (k % 4) + 7 * s + k // 4, 4, stride=2)] = rows[
                        8:12, tile(k)
                    ]
            else:
                for k in range(8):
                    fs[pl.ds(1024 * (k % 2) + 32 * s + k // 2, 7, stride=4)] = rows[0:7, tile(k)]
                    fs[pl.ds(2048 + 256 * k + 7 * s, 7)] = rows[8:15, tile(k)]

        loop(SHARDS, shard)
        for k in range(1 + b):
            wd[:, tile(k)] = fs[1024 * k : 1024 * k + 1024].astype(BF16)
        gap = jnp.zeros((4, 128), F32)
        for g in range(4 + 4 * b):
            for k in range(8):
                if b == 0:
                    start = 1024 + 256 * (k % 4) + 56 * g + k // 4
                    part = fs[pl.ds(start, 28, stride=2)]
                else:
                    start = 2048 + 256 * k + 28 * g
                    part = fs[start : start + 28]
                wu[32 * g : 32 * g + 32, tile(k)] = jnp.concatenate([part, gap], 0).astype(BF16)

    def taps0():
        for a in range(3):
            for b in range(3):
                yield a * 3 + b, (0 if a == 1 else 1), (0 if b == 1 else 1), a, b

    def both(ref_of):
        return jnp.concatenate([ref_of(0), ref_of(1)], 0)

    def squeeze(c, b, pooled, wd, wu):
        width = wd.shape[1]
        raw = row_dot(pooled, wd[...], nn)
        squeezed = raw * sig(raw)
        gating = sig(row_dot(squeezed, wu[...], nn))
        sv[b, c, 0:1] = pooled
        sv[b, c, 1:2, 0:width] = raw
        sv[b, c, 2:3, 0:width] = squeezed
        sv[b, c, 3:4] = gating
        return gating

    def gate(c, b, index, conv_k, wd, wu, name, proj_k):
        a, shift = affine(c, index)

        def pool_chunk(j, sums):
            z = pool[c, conv_k, chunk(j)] * a + shift
            excited = keep(c, j) * (z * sig(z))
            pool[c, 7, chunk(j)] = excited
            return (sums[0] + fold(excited),)

        pooled = each_column(1, pool_chunk)[0] / crop_count(c)
        gating = squeeze(c, b, pooled, wd, wu)

        def gate_chunk(j):
            ga[b, c, chunk(j)] = (pool[c, 7, chunk(j)] * gating).astype(BF16)

        loop(14, gate_chunk)

        def project(n):
            pool[c, proj_k, :, col(n)] = nn(ga[b, c], cols_of(name, col(n)))

        loop(4, project)
        return moment_sums(c, lambda j: pool[c, proj_k, chunk(j)])

    def ungate(c, b, index, conv_k, wd, wu, name):
        width = wd.shape[1]

        def back(n):
            pool[c, 7, :, col(n)] = nt(dp_of(c), rows_of(name, n))

        loop(4, back)
        a, shift = affine(c, index)

        def gate_chunk(j, sums):
            z = pool[c, conv_k, chunk(j)] * a + shift
            excited = keep(c, j) * (z * sig(z))
            return (sums[0] + fold(pool[c, 7, chunk(j)] * excited),)

        d_gate = each_column(1, gate_chunk)[0]
        gating = sv[b, c, 3:4]
        d_raw = d_gate * gating * (1.0 - gating)
        raw = sv[b, c, 1:2, 0:width]
        d_squeeze = row_dot(d_raw, wu[...], nt) * slope_of(raw, sig(raw))
        d_pool = row_dot(d_squeeze, wd[...], nt) / crop_count(c)
        sv[b, c, 4:5] = d_raw
        sv[b, c, 5:6, 0:width] = d_squeeze
        center, scaling = hat_of(c, index)

        def slope_chunk(j, sums):
            value = pool[c, conv_k, chunk(j)]
            z = value * a + shift
            d = (pool[c, 7, chunk(j)] * gating + d_pool) * (keep(c, j) * slope_of(z, sig(z)))
            pool[c, 7, chunk(j)] = d
            return (sums[0] + fold(d), sums[1] + fold(d * ((value - center) * scaling)))

        return each_column(2, slope_chunk)

    def small_grads(b):
        width = 128 + 128 * b

        def pairs(x_row, x_width, y_row, y_width):
            xs, ys = [], []
            for c in range(2):
                xh, xl = split_rows([sv[b, c, x_row : x_row + 1, 0:x_width]])
                yh, yl = split_rows([sv[b, c, y_row : y_row + 1, 0:y_width]])
                xs += [xh[0], xh[0], xl[0]]
                ys += [yh[0], yl[0], yh[0]]
            return tn(stacked(xs), stacked(ys))

        grad_down = pairs(0, C, 5, width)
        for k in range(1 + b):
            fs[1024 * k : 1024 * k + 1024] = grad_down[:, tile(k)]
        grad_up = pairs(2, width, 4, C)
        for g in range(4 + 4 * b):
            for k in range(8):
                part = grad_up[32 * g : 32 * g + 28, tile(k)]
                if b == 0:
                    fs[pl.ds(1024 + 256 * (k % 4) + 56 * g + k // 4, 28, stride=2)] = part
                else:
                    fs[2048 + 256 * k + 28 * g : 2048 + 256 * k + 28 * g + 28] = part

        def shard(s):
            tiles = []
            for k in range(8):
                if b == 0:
                    count = 4
                    first = fs[pl.ds(32 * s + k, 4, stride=8)]
                    second = fs[pl.ds(1024 + 256 * (k % 4) + 7 * s + k // 4, 4, stride=2)]
                else:
                    count = 7
                    first = fs[pl.ds(1024 * (k % 2) + 32 * s + k // 2, 7, stride=4)]
                    second = fs[pl.ds(2048 + 256 * k + 7 * s, 7)]
                gap = jnp.zeros((8 - count, 128), F32)
                tiles.append(jnp.concatenate([first, gap, second, gap], 0))
            put_shard("misc0" if b == 0 else "misc1", s, jnp.concatenate(tiles, 1))

        loop(SHARDS, shard)

    def norm_coefficients(c, index, totals, inverse, gain_row, kind):
        center, scaling = hat_of(c, index)
        ng[gain_row : gain_row + 1] += totals[1]
        shift_row = gain_row + 6 if gain_row < 6 else gain_row + 1
        ng[shift_row : shift_row + 1] += totals[0]
        a = st[c, index, 2:3]
        slope = -a * scaling * (totals[1] * inverse)
        offset = -a * (totals[0] * inverse) - slope * center
        return a, slope, offset

    def conv_grad(act_of, v_of, name):
        lane = lax.broadcasted_iota(jnp.int32, (64, 256), 1) // 64

        def block(a):
            for tap in range(9):
                dense = tn(
                    both(lambda c: act_of(c, tap, col(a))), both(lambda c: v_of(c, tap, col(a)))
                )
                own = jnp.where(lane == 0, dense[0:64], 0.0)
                for g in range(1, 4):
                    own = own + jnp.where(lane == g, dense[64 * g : 64 * g + 64], 0.0)
                for k in range(2):
                    at = 2048 * k + 224 * tap
                    fs[pl.ds(at + a, 28, stride=4)] = own[0:28, 128 * k : 128 * k + 128]
                    fs[pl.ds(at + 112 + a, 28, stride=4)] = own[32:60, 128 * k : 128 * k + 128]

        loop(4, block)

        def shard(s):
            tiles = [
                fs[pl.ds(2048 * k + 63 * s + a, 16, stride=4)] for a in range(4) for k in range(2)
            ]
            put_shard(name, s, jnp.concatenate(tiles, 1))

        loop(SHARDS, shard)

    def outer(left_of, right_of, name):
        def block(m):
            put_rows(name, m, tn(both(lambda c: left_of(c, col(m))), both(right_of)))

        loop(SHARDS * ROWS[name][1] // 256, block)

    z, yx = digit // 4, lax.rem(digit, 4)
    bits = (1 + section, 2 - section)

    def flip(bit):
        return yx + bit * (1 - 2 * lax.rem(yx // bit, 2))

    def push(src, dst, to, sends, recvs):
        pltpu.make_async_remote_copy(
            src_ref=src, dst_ref=dst, send_sem=sends, recv_sem=recvs,
            device_id=(section, to * v + rest), device_id_type=MESH,
        ).start()

    def push_sibling(src, dst, sends, recvs):
        pltpu.make_async_remote_copy(
            src_ref=src, dst_ref=dst, send_sem=sends, recv_sem=recvs,
            device_id=(other, me), device_id_type=MESH,
        ).start()

    def arrive(ref, sem):
        pltpu.make_async_copy(ref, ref, sem).wait()

    def gather(k, phase):
        start, stop = GATHERS[k]
        rows = pl.ds(start, stop - start)
        sent = w.at[section, :, :, rows]
        if phase > 0:
            sem = grecv.at[k, phase - 1]
            if phase == 1:
                arrive(w.at[section, pl.ds(0, 3), 0, rows], sem)
            elif phase == 2:
                arrive(sent.at[:, 0], sem)
            elif phase == 3:
                arrive(sent.at[:, pl.ds(0, 2)], sem)
            else:
                arrive(sent, sem)
        if phase == 4:
            arrive(w.at[section, pl.ds(0, 3), 0, rows], gsend.at[k, 0])
            arrive(sent.at[:, 0], gsend.at[k, 1])
            arrive(sent.at[:, pl.ds(0, 2)], gsend.at[k, 2])
            arrive(sent, gsend.at[k, 3])
            return
        sems = (gsend.at[k, phase], grecv.at[k, phase])
        if phase == 0:
            own = w.at[section, z, yx, rows]
            for hop in range(1, 4):
                push(own, own, lax.rem(z + hop, 4) * 4 + yx, *sems)
        elif phase == 1:
            push(sent.at[:, yx], sent.at[:, yx], z * 4 + flip(bits[0]), *sems)
        elif phase == 2:
            for at in (yx, flip(bits[0])):
                push(sent.at[:, at], sent.at[:, at], z * 4 + flip(bits[1]), *sems)
        else:
            push_sibling(sent, sent, *sems)

    def add_landed(land, rows, blocks, start, count):
        def fetch(at):
            return local_copy(
                land.at[pl.ds(2 * at, 2), rows],
                stage.at[pl.ds(2 * (at % 2), 2), pl.ds(0, count)], 3 + at % 2,
            )

        fetch(0).start()
        for at in range(len(blocks) // 2):
            if 2 * at + 2 < len(blocks):
                fetch(at + 1).start()
            fetch(at).wait()
            for near in range(2):
                def strip(i):
                    here = pl.ds(pl.multiple_of(start + 16 * i, 16), 16)
                    there = pl.ds(pl.multiple_of(16 * i, 16), 16)
                    index = (section, *blocks[2 * at + near], here)
                    w[index] = (
                        w[index].astype(F32) + stage[2 * (at % 2) + near, there].astype(F32)
                    ).astype(BF16)

                loop(count // 16, strip)

    def scatter(k, phase):
        start, stop = SCATTERS[k]
        count = stop - start
        rows = pl.ds(start, count)
        part = w.at[section, :, :, rows]
        first, second = flip(bits[1]), flip(bits[0])
        if phase == 1:
            arrive(land_d.at[:, rows], rrecv.at[k, 0])
            blocks = [(zz, near) for zz in range(4) for near in range(4)]
            add_landed(land_d, rows, blocks, start, count)
        elif phase == 2:
            arrive(land_c.at[:, rows], rrecv.at[k, 1])
            blocks = [(zz, near) for zz in range(4) for near in (yx, second)]
            add_landed(land_c, rows, blocks, start, count)
        elif phase == 3:
            arrive(land_b.at[:, rows], rrecv.at[k, 2])
            add_landed(land_b, rows, [(zz, yx) for zz in range(4)], start, count)
        elif phase == 4:
            arrive(land_a.at[pl.ds(0, 3), rows], rrecv.at[k, 3])
            copies = [
                local_copy(land_a.at[at, rows], stage.at[at, pl.ds(0, count)], 3 + at)
                for at in range(3)
            ]
            for copy in copies:
                copy.start()
            total = w[section, z, yx, start:stop].astype(F32)
            for at in range(3):
                copies[at].wait()
                total = total + stage[at, 0:count].astype(F32)
            pool[0, 4, start:stop] = total
            arrive(land_d.at[:, rows], rsend.at[k, 0])
            arrive(land_c.at[:, rows], rsend.at[k, 1])
            arrive(land_b.at[:, rows], rsend.at[k, 2])
            arrive(land_a.at[pl.ds(0, 3), rows], rsend.at[k, 3])
            return
        sems = (rsend.at[k, phase], rrecv.at[k, phase])
        if phase == 0:
            for zz in range(4):
                push_sibling(w.at[other, zz, :, rows], land_d.at[pl.ds(4 * zz, 4), rows], *sems)
        elif phase == 1:
            for zz in range(4):
                to = z * 4 + first
                push(w.at[section, zz, first, rows], land_c.at[2 * zz, rows], to, *sems)
                push(
                    w.at[section, zz, first + second - yx, rows], land_c.at[2 * zz + 1, rows], to,
                    *sems,
                )
        elif phase == 2:
            push(part.at[:, second], land_b.at[:, rows], z * 4 + second, *sems)
        else:
            for hop in range(1, 4):
                to = lax.rem(z + hop, 4)
                push(
                    w.at[section, to, yx, rows], land_a.at[hop - 1, rows], to * 4 + yx, *sems
                )

    shares = {}
    at = 0
    for name, ref, count in (
        ("wa0", l_wa0, 14), ("k0", l_k0, 16), ("ws", l_ws, 14), ("wd0", l_wd0, 4),
        ("wu0", l_wu0, 4), ("wc0", l_wc0, 28), ("wa1", l_wa1, 28), ("k1", l_k1, 16),
        ("wd1", l_wd1, 7), ("wu1", l_wu1, 7), ("wc1", l_wc1, 28),
    ):
        fs[at : at + ref.shape[0]] = ref[...].astype(F32)
        value = jnp.concatenate([fs[pl.ds(at + k, count, stride=7)] for k in range(7)], 1)
        room = 8 if count < 8 else count + -count % 16
        if room > count:
            value = jnp.concatenate([value, jnp.zeros((room - count, D), F32)], 0)
        shares[name] = value
        at += ref.shape[0] + -ref.shape[0] % 8
    load_map.wait()
    own_rows = jnp.concatenate([shares[name] for name in ORDER], 0).astype(BF16)
    for n in range(4):
        lanes = slice(256 * n, 256 * n + 256)
        w[section, z, yx, :, lanes] = nn(own_rows, e_buf[:, lanes]).astype(BF16)
    gather(0, 0)
    gather(1, 0)

    halves = jnp.concatenate(
        [short_gain_in[...].astype(F32), short_shift_in[...].astype(F32)], 1
    )
    pair[section] = jnp.concatenate(
        [gain_in[0], shift_in[0], halves, jnp.zeros((1, D), F32)], 0
    )
    swap = to_sibling(pair.at[section], pair.at[section], 3)
    swap.start()
    swap.wait()
    first, second = pair[0], pair[1]
    short_gain_row = jnp.concatenate([first[6:7, 0:DIN], second[6:7, 0:DIN]], 1)
    short_shift_row = jnp.concatenate([first[6:7, DIN:], second[6:7, DIN:]], 1)
    rows = jnp.concatenate(
        [
            first[0:3], second[0:3], first[3:6], second[3:6], short_gain_row, short_shift_row,
            jnp.zeros((2, D), F32),
        ],
        0,
    )

    def thirds(value):
        high = value.astype(BF16)
        left = value - high.astype(F32)
        middle = left.astype(BF16)
        return jnp.concatenate([high, middle, (left - middle.astype(F32)).astype(BF16)], 0)

    wide = nn(thirds(rows), e_buf[...])
    params[...] = wide[0:16] + wide[16:32] + wide[32:48]
    gather(0, 1)
    gather(2, 0)

    for copy in copies:
        copy.wait()

    def gather_slices(ref, rows):
        pad = jnp.zeros((16 - rows, D), BF16)
        return jnp.concatenate(
            [jnp.concatenate([ref[:, D * j : D * j + D], pad], 0) for j in range(OUT)], 0
        )

    def cotangent(c):
        for h in range(2):
            x = gather_slices(up_buf.at[h, c], 7)
            for n in range(4):
                y = nn(x, e_buf[:, 256 * n : 256 * n + 256])
                for j in range(OUT):
                    count = 16 if h == 0 else 7
                    pool[c, 3, 16 * j + 7 * h : 16 * j + 7 * h + count, 256 * n : 256 * n + 256] = y[
                        16 * j : 16 * j + count
                    ]

    loop(2, cotangent)
    load_map = local_copy(expand.at[0], e_buf, 2)
    load_map.start()
    gather(0, 2)
    gather(1, 1)
    fs[...] = jnp.zeros_like(fs)
    load_map.wait()

    def phases(c):
        for h in range(2):
            x = gather_slices(x_buf.at[h, c], 14)
            for n in range(4):
                y = nn(x, e_buf[:, 256 * n : 256 * n + 256])
                for j in range(OUT):
                    for k in range(2):
                        fs[pl.ds(512 * (2 * n + k) + 32 * j + 14 * h, 14)] = y[
                            16 * j : 16 * j + 14, 128 * k : 128 * k + 128
                        ]
        for q in range(2):
            def take(j):
                for k in range(8):
                    u_buf[c, q, chunk(j), 128 * k : 128 * k + 128] = fs[
                        pl.ds(512 * k + 32 * j + q, 16, stride=2)
                    ].astype(BF16)

            loop(14, take)

    phases(0)
    gather(0, 3)
    gather(1, 2)
    gather(3, 0)
    phases(1)
    load_map = local_copy(expand.at[1], e_buf, 2)
    load_map.start()
    gather(0, 4)
    gather(1, 3)
    gather(2, 1)

    def entry_inner(c):
        for q in range(2):
            for r in range(2):
                def product(n):
                    inn[c, 2 * q + r, :, col(n)] = nn(
                        u_buf[c, q, :, 512 * r : 512 * r + 512], cols_of("wa0", col(n))
                    )

                loop(4, product)

        def body(j, sums):
            mask = keep(c, j)
            first, second = sums
            for k in range(4):
                value = inn[c, k, chunk(j)]
                weighted = value * mask
                first = first + fold(weighted)
                second = second + fold(weighted * value)
            return (first, second)

        sums = each_column(2, body)
        own = jnp.zeros((1, C), F32) + crop_count(c)
        ar_start(0, c, [sums[0], sums[1], own, own])

    loop(2, entry_inner)
    gather(2, 2)
    gather(4, 0)
    gather(1, 4)
    build_conv("k0")
    gather(2, 3)
    gather(3, 1)

    def entry_conv(c):
        totals = ar_wait(0, c, 4)
        cn[c, 0:1] = totals[2]
        cn[c, 1:2] = 1.0 / totals[2]
        cn[c, 2:3] = 0.25 / totals[2]
        set_stats(c, 0, totals, inverse_in(c), 0)
        a, shift = affine(c, 0)

        def activate(j):
            mask = keep(c, j)
            for q in range(2):
                for r in range(2):
                    z = inn[c, 2 * q + r, chunk(j)] * a + shift
                    act = mask * (z * sig(z))
                    a0[c, 2 * q + r, chunk(j, GUARD)] = act.astype(BF16)
                    if q == 1:
                        d_buf[c, r, chunk(j, GUARD)] = pltpu.roll(act, 1, 0).astype(BF16)

        loop(14, activate)

        def convolve(n):
            patches = []
            for tap, q, r, ta, tb in taps0():
                at = GUARD - 16 if tb == 0 else GUARD
                src = d_buf.at[c, r] if ta == 0 else a0.at[c, 2 * q + r]
                patches.append(src[at : at + PX, col(n)])
            pool[c, 0, :, col(n)] = nn(jnp.concatenate(patches, 1), kd[n])

        loop(4, convolve)
        ar_start(1, c, moment_sums(c, lambda j: pool[c, 0, chunk(j)]))

    loop(2, entry_conv)

    def strided(c):
        def product(n):
            pool[c, 2, :, col(n)] = nn(u_buf[c, 0, :, 0:512], cols_of("ws", col(n)))

        loop(4, product)

    loop(2, strided)
    gather(2, 4)
    gather(3, 2)
    gather(4, 1)
    build_small(0)

    def entry_gate(c):
        totals = ar_wait(1, c, 2)
        set_stats(c, 1, totals, inverse_out(c), 1)
        sums = gate(c, 0, 1, 0, wd0, wu0, "wc0", 1)
        ar_start(2, c, sums + moment_sums(c, lambda j: pool[c, 2, chunk(j)]))

    loop(2, entry_gate)
    gather(3, 3)
    gather(4, 2)
    gather(3, 4)
    build_conv("k1")

    def entry_pre(c, j):
        a, shift = affine(c, 2)
        short_a, short_shift = affine(c, 3)
        return (
            pool[c, 1, chunk(j)] * a + pool[c, 2, chunk(j)] * short_a + (shift + short_shift)
        )

    def entry_out(c):
        totals = ar_wait(2, c, 4)
        set_stats(c, 2, totals[0:2], inverse_out(c), 2)
        set_stats(c, 3, totals[2:4], inverse_out(c), 12)

        def finish(j):
            z = entry_pre(c, j)
            hid[c, chunk(j)] = (keep(c, j) * (z * sig(z))).astype(BF16)

        loop(14, finish)

        def product(n):
            pool[c, 4, :, col(n)] = nn(hid[c], cols_of("wa1", col(n)))

        loop(4, product)
        ar_start(3, c, moment_sums(c, lambda j: pool[c, 4, chunk(j)]))

    loop(2, entry_out)

    def body_conv(c):
        set_stats(c, 4, ar_wait(3, c, 2), inverse_out(c), 3)
        a, shift = affine(c, 4)

        def activate(j):
            z = pool[c, 4, chunk(j)] * a + shift
            act = keep(c, j) * (z * sig(z))
            a1[c, chunk(j, GUARD)] = act.astype(BF16)
            d_buf[c, 0, chunk(j, GUARD)] = pltpu.roll(act, 1, 0).astype(BF16)
            d_buf[c, 1, chunk(j, GUARD)] = pltpu.roll(act, 15, 0).astype(BF16)

        loop(14, activate)

        def convolve(n):
            rows = (d_buf.at[c, 0], a1.at[c], d_buf.at[c, 1])
            patches = [
                rows[ta][16 * tb : 16 * tb + PX, col(n)] for ta in range(3) for tb in range(3)
            ]
            pool[c, 5, :, col(n)] = nn(jnp.concatenate(patches, 1), kd[n])

        loop(4, convolve)
        ar_start(4, c, moment_sums(c, lambda j: pool[c, 5, chunk(j)]))

    loop(2, body_conv)
    gather(4, 3)
    gather(4, 4)
    build_small(1)

    def body_gate(c):
        set_stats(c, 5, ar_wait(4, c, 2), inverse_out(c), 4)
        ar_start(5, c, gate(c, 1, 5, 5, wd1, wu1, "wc1", 6))

    loop(2, body_gate)

    def body_out(c):
        set_stats(c, 6, ar_wait(5, c, 2), inverse_out(c), 5)
        a, shift = affine(c, 6)
        center, scaling = hat_of(c, 6)

        def finish(j, sums):
            value = pool[c, 6, chunk(j)]
            z = value * a + shift + hid[c, chunk(j)].astype(F32)
            mask = keep(c, j)
            s = sig(z)
            dp_buf[c, chunk(j, GUARD)] = (mask * (z * s)).astype(BF16)
            d_pre = pool[c, 3, chunk(j)] * (mask * slope_of(z, s))
            pool[c, 3, chunk(j)] = d_pre
            return (sums[0] + fold(d_pre), sums[1] + fold(d_pre * ((value - center) * scaling)))

        ar_start(6, c, each_column(2, finish))

    loop(2, body_out)
    load_map.wait()

    def narrow(value, store):
        for start, width in ((0, 256), (256, 256), (512, 256), (768, 128)):
            store(start, width, nt(value, e_buf[start : start + width]))

    def body_emit(c):
        def store(start, width, y):
            for j in range(OUT):
                for h in range(2):
                    up_buf[h, c, :, D * j + start : D * j + start + width] = y[
                        16 * j + 7 * h : 16 * j + 7 * h + 7
                    ].astype(BF16)

        narrow(dp_of(c), store)

    loop(2, body_emit)
    out_copies = [
        to_sibling(up_buf.at[other], out.at[mine], 2),
        local_copy(up_buf.at[section], out.at[mine], 1),
        local_copy(expand.at[0], e_buf, 2),
    ]
    for copy in out_copies:
        copy.start()

    def body_back_out(c):
        a, slope, offset = norm_coefficients(c, 6, ar_wait(6, c, 2), inverse_out(c), 5, 0)

        def project(j):
            value = pool[c, 6, chunk(j)]
            dp_buf[c, chunk(j, GUARD)] = (
                keep(c, j) * (a * pool[c, 3, chunk(j)] + slope * value + offset)
            ).astype(BF16)

        loop(14, project)
        ar_start(7, c, ungate(c, 1, 5, 5, wd1, wu1, "wc1"))

    loop(2, body_back_out)
    outer(lambda c, l: ga[1, c, :, l], dp_of, "wc1")
    small_grads(1)
    scatter(0, 0)

    def conv_cotangent(c, index, conv_k, a, slope, offset, versions):
        def body(j):
            d = keep(c, j) * (a * pool[c, 7, chunk(j)] + slope * pool[c, conv_k, chunk(j)] + offset)
            d_buf[c, 0, chunk(j, GUARD)] = d.astype(BF16)
            d_buf[c, 1, chunk(j, GUARD)] = pltpu.roll(d, 15, 0).astype(BF16)
            if versions == 3:
                dp_buf[c, chunk(j, GUARD)] = pltpu.roll(d, 1, 0).astype(BF16)

        loop(14, body)

    def v_body(c, tap, lanes):
        ta, tb = tap // 3, tap % 3
        ref = (d_buf.at[c, 1], d_buf.at[c, 0], dp_buf.at[c])[ta]
        return ref[32 - 16 * tb : 32 - 16 * tb + PX, lanes]

    def v_entry(c, tap, lanes):
        ta, tb = tap // 3, tap % 3
        at = 32 if tb == 0 else 16
        return d_buf[c, 1 if ta == 0 else 0, at : at + PX, lanes]

    def body_back_conv(c):
        a, slope, offset = norm_coefficients(c, 5, ar_wait(7, c, 2), inverse_out(c), 4, 0)
        conv_cotangent(c, 5, 5, a, slope, offset, 3)

        def back(n):
            total = nt(v_body(c, 0, col(n)), kd[n, 0:256])
            for tap in range(1, 9):
                total = total + nt(v_body(c, tap, col(n)), kd[n, 256 * tap : 256 * tap + 256])
            pool[c, 7, :, col(n)] = total

        loop(4, back)
        a, shift = affine(c, 4)
        center, scaling = hat_of(c, 4)

        def body(j, sums):
            value = pool[c, 4, chunk(j)]
            z = value * a + shift
            d = pool[c, 7, chunk(j)] * (keep(c, j) * slope_of(z, sig(z)))
            pool[c, 7, chunk(j)] = d
            return (sums[0] + fold(d), sums[1] + fold(d * ((value - center) * scaling)))

        ar_start(8, c, each_column(2, body))

    loop(2, body_back_conv)
    conv_grad(lambda c, tap, l: a1[c, GUARD : GUARD + PX, l], v_body, "k1")
    scatter(0, 1)

    def body_back_in(c):
        a, slope, offset = norm_coefficients(c, 4, ar_wait(8, c, 2), inverse_out(c), 3, 0)

        def body(j):
            dp_buf[c, chunk(j, GUARD)] = (
                keep(c, j) * (a * pool[c, 7, chunk(j)] + slope * pool[c, 4, chunk(j)] + offset)
            ).astype(BF16)

        loop(14, body)

        def back(n):
            pool[c, 3, :, col(n)] = (
                (nt(dp_of(c), rows_of("wa1", n)) + pool[c, 3, :, col(n)]).astype(BF16).astype(F32)
            )

        loop(4, back)
        center, scaling = hat_of(c, 2)
        short_center, short_scaling = hat_of(c, 3)

        def pre(j, sums):
            z = entry_pre(c, j)
            d = pool[c, 3, chunk(j)] * (keep(c, j) * slope_of(z, sig(z)))
            pool[c, 3, chunk(j)] = d
            return (
                sums[0] + fold(d),
                sums[1] + fold(d * ((pool[c, 1, chunk(j)] - center) * scaling)),
                sums[2] + fold(d * ((pool[c, 2, chunk(j)] - short_center) * short_scaling)),
            )

        sums = each_column(3, pre)
        ar_start(9, c, sums + [sums[0]])

    loop(2, body_back_in)
    outer(lambda c, l: hid[c, :, l], dp_of, "wa1")
    scatter(1, 0)
    scatter(0, 2)
    build_conv("k0")

    def entry_back_out(c):
        totals = ar_wait(9, c, 4)
        a, slope, offset = norm_coefficients(c, 2, totals[0:2], inverse_out(c), 2, 0)
        short = norm_coefficients(c, 3, [totals[0], totals[2]], inverse_out(c), 12, 0)

        def project(j):
            mask = keep(c, j)
            d = pool[c, 3, chunk(j)]
            dp_buf[c, chunk(j, GUARD)] = (
                mask * (a * d + slope * pool[c, 1, chunk(j)] + offset)
            ).astype(BF16)
            hid[c, chunk(j)] = (
                mask * (short[0] * d + short[1] * pool[c, 2, chunk(j)] + short[2])
            ).astype(BF16)

        loop(14, project)

        def back(n):
            pool[c, 2, :, col(n)] = nt(hid[c], rows_of("ws", n))

        loop(2, back)
        ar_start(10, c, ungate(c, 0, 1, 0, wd0, wu0, "wc0"))

    loop(2, entry_back_out)
    outer(lambda c, l: ga[0, c, :, l], dp_of, "wc0")
    outer(lambda c, l: u_buf[c, 0, :, l], lambda c: hid[c], "ws")
    small_grads(0)
    scatter(2, 0)
    scatter(1, 1)
    scatter(0, 3)

    def entry_back_conv(c):
        a, slope, offset = norm_coefficients(c, 1, ar_wait(10, c, 2), inverse_out(c), 1, 0)
        conv_cotangent(c, 1, 0, a, slope, offset, 2)
        for q in range(2):
            for r in range(2):
                def back(n):
                    total = None
                    for tap, tq, tr, ta, tb in taps0():
                        if (tq, tr) == (q, r):
                            term = nt(v_entry(c, tap, col(n)), kd[n, 256 * tap : 256 * tap + 256])
                            total = term if total is None else total + term
                    pool[c, 4 + 2 * q + r, :, col(n)] = total

                loop(4, back)
        a, shift = affine(c, 0)
        center, scaling = hat_of(c, 0)

        def body(j, sums):
            mask = keep(c, j)
            first, second = sums
            for k in range(4):
                value = inn[c, k, chunk(j)]
                z = value * a + shift
                d = pool[c, 4 + k, chunk(j)] * (mask * slope_of(z, sig(z)))
                pool[c, 4 + k, chunk(j)] = d
                first = first + fold(d)
                second = second + fold(d * ((value - center) * scaling))
            return (first, second)

        ar_start(11, c, each_column(2, body))

    loop(2, entry_back_conv)

    def act_entry(c, tap, lanes):
        q = 0 if tap // 3 == 1 else 1
        r = 0 if tap % 3 == 1 else 1
        return a0[c, 2 * q + r, GUARD : GUARD + PX, lanes]

    conv_grad(act_entry, v_entry, "k0")
    scatter(3, 0)
    scatter(2, 1)
    scatter(1, 2)
    for copy in out_copies:
        copy.wait()

    def entry_back_in(c):
        a, slope, offset = norm_coefficients(c, 0, ar_wait(11, c, 2), inverse_in(c), 0, 0)

        def body(j):
            mask = keep(c, j)
            for k in range(4):
                a0[c, k, chunk(j, GUARD)] = (
                    mask * (a * pool[c, 4 + k, chunk(j)] + slope * inn[c, k, chunk(j)] + offset)
                ).astype(BF16)

        loop(14, body)

    loop(2, entry_back_in)
    scatter(0, 4)
    swap = to_sibling(ng, ng_in, 3)
    swap.start()

    def input_grad(m):
        total = None
        for q in range(2):
            for r in range(2):
                at = pl.ds(pl.multiple_of(512 * r + 256 * m, 256), 256)
                term = tn(
                    both(lambda c: u_buf[c, q, :, at]),
                    both(lambda c: a0[c, 2 * q + r, GUARD : GUARD + PX]),
                )
                total = term if total is None else total + term
        return total

    def entry_back_input(c):
        for q in range(2):
            for r in range(2):
                def back(n):
                    total = nt(a0[c, 2 * q + r, GUARD : GUARD + PX], rows_of("wa0", n))
                    if q == 0 and r == 0:
                        total = total + pool[c, 2, :, col(n)]
                    at = pl.ds(pl.multiple_of(512 * r + 256 * n, 256), 256)
                    d_buf[c, q, 0:PX, at] = total.astype(BF16)

                loop(2, back)

    loop(2, entry_back_input)

    def input_block(m):
        put_rows("wa0", m, input_grad(m))

    loop(2, input_block)
    scatter(4, 0)
    scatter(3, 1)

    def entry_emit(c):
        for q in range(2):
            def store(start, width, y):
                for j in range(OUT):
                    for k in range(width // 128):
                        fs[pl.ds(512 * (start // 128 + k) + 32 * j + q, 14, stride=2)] = y[
                            16 * j : 16 * j + 14, 128 * k : 128 * k + 128
                        ]

            narrow(d_buf[c, q, 0:PX], store)
        for h in range(2):
            for j in range(OUT):
                for k in range(7):
                    x_buf[h, c, :, D * j + 128 * k : D * j + 128 * k + 128] = fs[
                        512 * k + 32 * j + 14 * h : 512 * k + 32 * j + 14 * h + 14
                    ].astype(BF16)

    entry_emit(0)
    scatter(4, 1)
    scatter(3, 2)
    scatter(2, 2)
    scatter(1, 3)
    entry_emit(1)
    load_map = local_copy(expand.at[1], e_buf, 2)
    load_map.start()
    last = [
        to_sibling(x_buf.at[other], grad.at[mine], 4),
        local_copy(x_buf.at[section], grad.at[mine], 0),
    ]
    for copy in last:
        copy.start()
    scatter(4, 2)
    scatter(3, 3)
    scatter(2, 3)
    scatter(1, 4)
    scatter(4, 3)
    scatter(2, 4)
    scatter(3, 4)
    scatter(4, 4)
    load_map.wait()
    swap.wait()
    total = thirds(ng[...] + ng_in[...])
    total = nt(total, e_buf[...])
    total = total[0:16] + total[16:32] + total[32:48]

    def own(top, low):
        return jnp.where(section == 0, top, low)

    gain_out[0] = own(total[0:3], total[3:6])
    shift_out[0] = own(total[6:9], total[9:12])
    short_gain_out[...] = own(total[12:13, 0:DIN], total[12:13, DIN:])
    short_shift_out[...] = own(total[13:14, 0:DIN], total[13:14, DIN:])
    total = pool[0, 4, 0:192]
    high = total.astype(BF16)
    low = (total - high.astype(F32)).astype(BF16)
    final = nt(high, e_buf[...]) + nt(low, e_buf[...])
    for name, ref, count in (
        ("wa0", o_wa0, 14), ("k0", o_k0, 16), ("ws", o_ws, 14), ("wd0", o_wd0, 4),
        ("wu0", o_wu0, 4), ("wc0", o_wc0, 28), ("wa1", o_wa1, 28), ("k1", o_k1, 16),
        ("wd1", o_wd1, 7), ("wu1", o_wu1, 7), ("wc1", o_wc1, 28),
    ):
        if name[1] in "du":
            at = ROWS["misc" + name[2]][0] + (8 if name[1] == "u" else 0)
        else:
            at = ROWS[name][0]
        for k in range(7):
            ref[pl.ds(k, count, stride=7)] = final[at : at + count, 128 * k : 128 * k + 128]
    for copy in last:
        copy.wait()


def lane_maps():
    at = np.arange(D)
    first = np.zeros((D, C), np.float32)
    first[at, at // 14 * 16 + at % 14] = 1
    second = np.zeros((D, C), np.float32)
    second[at, at // 28 * 32 + at % 28] = 1
    return np.stack([first, second])


def main_call(n_dp, *args):
    v = n_dp // MEMBERS
    any_space = pl.BlockSpec(memory_space=pl.ANY)
    vmem = pl.BlockSpec(memory_space=pltpu.VMEM)
    smem = pl.BlockSpec(memory_space=pltpu.SMEM)
    shape = lambda *s, dtype=BF16: jax.ShapeDtypeStruct(s, dtype)
    flat = [shape(count, 128, dtype=F32) for count in LINES]
    outs = [
        shape(4, 7, 12544), shape(4, 14, 12544), *flat,
        shape(1, 3, D, dtype=F32), shape(1, 3, D, dtype=F32),
        shape(1, DIN, dtype=F32), shape(1, DIN, dtype=F32),
        shape(16, 192, C), shape(8, 192, C), shape(4, 192, C), shape(3, 192, C),
    ]
    dma = pltpu.SemaphoreType.DMA
    scratch = [
        pltpu.VMEM((2, 4, PX, C), F32),
        pltpu.VMEM((2, 8, PX, C), F32),
        pltpu.VMEM((2, 2, PX, C), BF16),
        pltpu.VMEM((2, 4, PX + 2 * GUARD, C), BF16),
        pltpu.VMEM((2, PX + 2 * GUARD, C), BF16),
        pltpu.VMEM((2, 2, PX + 2 * GUARD, C), BF16),
        pltpu.VMEM((2, 2, PX, C), BF16),
        pltpu.VMEM((2, PX, C), BF16),
        pltpu.VMEM((2, PX + 2 * GUARD, C), BF16),
        pltpu.VMEM((2, 2, 14, 12544), BF16),
        pltpu.VMEM((2, 2, 7, 12544), BF16),
        pltpu.VMEM((4096, 128), F32),
        pltpu.VMEM((4, 2304, 256), BF16),
        pltpu.VMEM((D, C), BF16),
        pltpu.VMEM((2, 4, 4, 192, C), BF16),
        pltpu.VMEM((C, 128), BF16),
        pltpu.VMEM((128, C), BF16),
        pltpu.VMEM((C, 256), BF16),
        pltpu.VMEM((256, C), BF16),
        pltpu.VMEM((4, 64, C), BF16),
        pltpu.VMEM((16, C), F32),
        pltpu.VMEM((2, 8, D), F32),
        pltpu.VMEM((2, 7, 8, C), F32),
        pltpu.VMEM((2, 2, 8, C), F32),
        pltpu.VMEM((2, 8, C), F32),
        pltpu.VMEM((16, C), F32),
        pltpu.VMEM((16, C), F32),
        pltpu.VMEM((2, 2, MEMBERS, 2, C), F32),
        pltpu.VMEM((2, MEMBERS, 4, C), F32),
        pltpu.VMEM((2, 2, v, 4, C), F32),
        dma((2, 2)), dma((2, 2)), dma((2, 2)), dma((2, 2)), dma((5,)), dma((5,)), dma((6,)),
        dma((5, 4)), dma((5, 4)), dma((5, 4)), dma((5, 4)),
    ]
    return pl.pallas_call(
        functools.partial(main_kernel, n_dp),
        out_shape=outs,
        in_specs=[any_space, any_space, smem, any_space] + [vmem] * 15,
        out_specs=[any_space] * 2 + [vmem] * 15 + [any_space] * 4,
        scratch_shapes=scratch,
        compiler_params=pltpu.CompilerParams(
            collective_id=1, has_side_effects=True, vmem_limit_bytes=64 << 20
        ),
    )(*args)


def local(
    features, crop_side, upstream,
    entry_in, entry_group, entry_out, entry_down, entry_up, shortcut_weight,
    body_in, body_group, body_out, body_down, body_up,
    norm_gain, norm_shift, shortcut_gain, shortcut_shift,
):
    n_dp = lax.axis_size("dp")
    v = n_dp // MEMBERS
    groups = [[v * member + k for k in range(v)] for member in range(MEMBERS)]
    shards = (
        entry_in, entry_group, shortcut_weight, entry_down, entry_up, entry_out,
        body_in, body_group, body_down, body_up, body_out,
    )

    def lines(shard, count):
        if v > 1:
            shard = lax.all_gather(shard, "dp", axis_index_groups=groups, axis=0, tiled=True)
        return jnp.pad(shard, (0, 128 * count - shard.shape[0])).reshape(count, 128)

    results = main_call(
        n_dp, features, upstream, crop_side, jnp.asarray(lane_maps(), BF16), norm_gain,
        norm_shift, shortcut_gain[None], shortcut_shift[None],
        *(lines(shard, count) for shard, count in zip(shards, LINES)),
    )
    output, d_features = results[:2]

    def share(values, shard):
        values = values.reshape(-1)[: v * shard.shape[0]]
        if v > 1:
            values = lax.psum_scatter(
                values, "dp", scatter_dimension=0, axis_index_groups=groups, tiled=True
            )
        return values

    wa0, k0, ws, wd0, wu0, wc0, wa1, k1, wd1, wu1, wc1 = (
        share(values, shard) for values, shard in zip(results[2:13], shards)
    )
    gains, shifts, short_gain, short_shift = results[13:17]
    return (
        output, d_features, wa0, k0, wc0, wd0, wu0, ws, wa1, k1, wc1, wd1, wu1, gains, shifts,
        short_gain[0], short_shift[0],
    )


def solution(mesh):
    rows = P("dp", "section", None)
    flat = P(("section", "dp"))
    params = (P("section", None, None), P("section", None, None), P("section"), P("section"))
    return jax.shard_map(
        local,
        mesh=mesh,
        in_specs=(rows, P("dp"), rows) + (flat,) * 11 + params,
        out_specs=(rows, rows) + (flat,) * 11 + params,
        check_vma=False,
    )
```

```python
import functools

import jax
import jax.numpy as jnp
import numpy as np
from jax import lax
from jax.experimental import pallas as pl
from jax.experimental.pallas import tpu as pltpu
from jax.sharding import PartitionSpec as P

D = 896
DIN = 448
OUT = 14
IN = 28
SE0 = 112
SE1 = 224
EPSILON = 1e-05
F32 = jnp.float32
BF16 = jnp.bfloat16
MESH = pl.DeviceIdType.MESH
C = 1024
PX = 224
GUARD = 16
MEMBERS = 16
SHARDS = 32
ROWS = {
    "wa0": (0, 16), "k0": (16, 16), "ws": (32, 16), "misc0": (48, 16), "wc0": (64, 32),
    "k1": (96, 16), "wa1": (112, 32), "misc1": (144, 16), "wc1": (160, 32),
}
ORDER = ("wa0", "k0", "ws", "wd0", "wu0", "wc0", "k1", "wa1", "wd1", "wu1", "wc1")
LINES = (98, 112, 98, 28, 28, 196, 196, 112, 49, 49, 196)
GATHERS = ((0, 16), (16, 32), (32, 64), (64, 96), (96, 112), (112, 144), (144, 192))
SCATTERS = (
    (144, 192), (96, 112), (112, 144), (64, 96), (32, 64), (16, 32), (0, 16)
)
CHAINED = 5
GATHER_PLAN = {
    "own": ((0, 0), (1, 0), (2, 0)),
    "ph1": ((0, 1), (3, 0)),
    "need_wa0": ((0, 2), (1, 1), (0, 3), (2, 1), (4, 0), (5, 0), (0, 4), (1, 2)),
    "in0b": ((6, 0),),
    "in0": ((3, 1),),
    "in1a": ((2, 2),),
    "in1b": ((4, 1),),
    "in1": ((1, 3),),
    "need_k0": ((1, 4),),
    "bk0": ((3, 2),),
    "conv0a": ((5, 1),),
    "conv1a": ((2, 3),),
    "conv1": ((4, 2),),
    "need_ws": ((2, 4),),
    "str1": ((6, 1),),
    "need_wc0": ((3, 3), (3, 4), (5, 2)),
    "gate0": ((4, 3),),
    "gate1": ((6, 2),),
    "need_k1": ((4, 4),),
    "need_wa1": ((5, 3), (5, 4)),
    "bconv0": ((6, 3),),
    "need_wc1": ((6, 4),),
}
SCATTER_PLAN = {
    "small1": ((0, 0),),
    "bback0": ((0, 1),),
    "k1": ((1, 0),),
    "bin1a": ((0, 2), (1, 1)),
    "wa1": ((2, 0),),
    "eback0": ((0, 3),),
    "eback1a": ((1, 2), (2, 1)),
    "wc0": ((3, 0),),
    "small0": ((4, 0),),
    "econv0b": ((1, 3),),
    "econv0": ((0, 4), (2, 2), (3, 1)),
    "econv1b": ((1, 4),),
    "econv1": ((2, 3),),
    "k0": ((5, 0),),
    "wa0": ((5, 1), (3, 2), (4, 1), (6, 0)),
    "input0": ((3, 3),),
    "input1a": ((6, 1),),
    "emit0": ((2, 4),),
    "emit1a": ((5, 2),),
    "tail": (
        (4, 2), (6, 2), (5, 3), (3, 4), (4, 3), (6, 3), (5, 4), (4, 4), (6, 4),
    ),
}


def dot(a, b, dims):
    return lax.dot_general(a, b, ((dims[:1], dims[1:]), ((), ())), preferred_element_type=F32)


def nn(a, b):
    return dot(a, b, (1, 0))


def nt(a, b):
    return dot(a, b, (1, 1))


def tn(a, b):
    return dot(a, b, (0, 0))


def sig(z):
    return jnp.tanh(z * 0.5) * 0.5 + 0.5


def slope_of(z, s):
    return s * (1.0 + z * (1.0 - s))


def split_rows(rows):
    high = [r.astype(BF16).astype(F32) for r in rows]
    low = [r - h for r, h in zip(rows, high)]
    return high, low


def stacked(rows):
    pad = jnp.zeros((16 - len(rows), rows[0].shape[1]), F32)
    return jnp.concatenate(list(rows) + [pad], 0).astype(BF16)


def row_dot(row, weight, mul):
    high, low = split_rows([row])
    both = mul(stacked(high + low), weight)
    return both[0:1] + both[1:2]


def col(n, width=256):
    return pl.ds(pl.multiple_of(n * width, width), width)


def chunk(j, base=0):
    return pl.ds(pl.multiple_of(j * 16 + base, 16), 16)


def loop(count, body):
    def step(i, carry):
        body(i)
        return carry

    lax.fori_loop(0, count, step, 0)


def main_kernel(
    n_dp, features, upstream, side_ref, expand, gain_in, shift_in, short_gain_in, short_shift_in,
    l_wa0, l_k0, l_ws, l_wd0, l_wu0, l_wc0, l_wa1, l_k1, l_wd1, l_wu1, l_wc1,
    out, grad, o_wa0, o_k0, o_ws, o_wd0, o_wu0, o_wc0, o_wa1, o_k1, o_wd1, o_wu1, o_wc1,
    gain_out, shift_out, short_gain_out, short_shift_out,
    inn, pool, u_buf, a0, a1, d_buf, ga, hid, dp_buf, x_buf, up_buf, fs, kd, e_buf,
    w, wd0, wu0, wd1, wu1, stage, params, pair, st, sv, cn, ng, ng_in, ar2, ar4, arv,
    asend, arecv, vsend, vrecv, xsend, xrecv, lsem, gsend, grecv, rsend, rrecv, free,
):
    section = lax.axis_index("section")
    me = lax.axis_index("dp")
    v = n_dp // MEMBERS
    digit, rest = me // v, lax.rem(me, v)
    other = 1 - section

    def member(hop):
        return lax.rem(digit + hop, MEMBERS) * v + rest

    def near(hop):
        return digit * v + lax.rem(rest + hop, v)

    barrier = pltpu.get_barrier_semaphore()

    def greet(hop):
        pl.semaphore_signal(barrier, inc=1, device_id=(section, member(hop + 1)), device_id_type=MESH)

    def greet_near(hop):
        pl.semaphore_signal(barrier, inc=1, device_id=(section, near(hop + 1)), device_id_type=MESH)

    loop(MEMBERS - 1, greet)
    if v > 1:
        loop(v - 1, greet_near)
    pl.semaphore_signal(barrier, inc=1, device_id=(other, me), device_id_type=MESH)
    def local_copy(src, dst, sem=0):
        return pltpu.make_async_copy(src, dst, lsem.at[sem])

    def to_sibling(src, dst, at):
        return pltpu.make_async_remote_copy(
            src_ref=src, dst_ref=dst, send_sem=xsend.at[at], recv_sem=xrecv.at[at],
            device_id=(other, me), device_id_type=MESH,
        )

    mine = pl.ds(2 * section, 2)
    theirs = pl.ds(2 * other, 2)
    load_map = local_copy(expand.at[1], e_buf, 2)
    copies = [
        local_copy(features.at[mine], x_buf.at[section], 0),
        local_copy(upstream.at[mine], up_buf.at[section], 1),
    ]
    for copy in [load_map] + copies:
        copy.start()

    def dp_of(c):
        return dp_buf[c, GUARD : GUARD + PX]

    def half_side(c):
        return side_ref[2 * section + c] // 2

    def keep(c, j):
        half = half_side(c)
        bound = jnp.where(j < half, half, 0)
        tile = (lax.broadcasted_iota(jnp.int32, (16, 128), 0) < bound).astype(F32)
        return jnp.concatenate([tile] * (C // 128), 1)

    def crop_count(c):
        half = half_side(c)
        return (half * half).astype(F32)

    def ar_slots(rows, n):
        return ar2.at[n % 2] if rows == 2 else ar4

    def ar_start(n, c, rows):
        slots = ar_slots(len(rows), n).at[c]
        slots[digit] = jnp.concatenate(rows, 0)

        def send(hop):
            pltpu.make_async_remote_copy(
                src_ref=slots.at[digit], dst_ref=slots.at[digit], send_sem=asend.at[n % 2, c],
                recv_sem=arecv.at[n % 2, c], device_id=(section, member(hop + 1)),
                device_id_type=MESH,
            ).start()

        loop(MEMBERS - 1, send)

    def ar_wait(n, c, rows):
        slots = ar_slots(rows, n).at[c]
        arrived = slots.at[pl.ds(0, MEMBERS - 1)]
        pltpu.make_async_copy(arrived, arrived, asend.at[n % 2, c]).wait()
        pltpu.make_async_copy(arrived, arrived, arecv.at[n % 2, c]).wait()
        total = slots[0]
        for k in range(1, MEMBERS):
            total = total + slots[k]
        if v > 1:
            again = arv.at[n % 2, c]
            spare = [jnp.zeros((4 - rows, C), F32)] if rows < 4 else []
            again[rest] = jnp.concatenate([total] + spare, 0)

            def send(hop):
                pltpu.make_async_remote_copy(
                    src_ref=again.at[rest], dst_ref=again.at[rest], send_sem=vsend.at[n % 2, c],
                    recv_sem=vrecv.at[n % 2, c], device_id=(section, near(hop + 1)),
                    device_id_type=MESH,
                ).start()

            loop(v - 1, send)
            arrived = again.at[pl.ds(0, v - 1)]
            pltpu.make_async_copy(arrived, arrived, vsend.at[n % 2, c]).wait()
            pltpu.make_async_copy(arrived, arrived, vrecv.at[n % 2, c]).wait()
            total = again[0]
            for k in range(1, v):
                total = total + again[k]
        return [total[k : k + 1] for k in range(rows)]

    def down(sums):
        return jnp.sum(sums, axis=0, keepdims=True)

    def fold(value):
        return value[0:8] + value[8:16]

    def zeros(count):
        return tuple(jnp.zeros((8, C), F32) for _ in range(count))

    def each_column(count, body):
        sums = lax.fori_loop(0, 14, body, zeros(count))
        return [down(one) for one in sums]

    def moment_sums(c, value_of):
        def body(j, sums):
            value = value_of(j)
            weighted = value * keep(c, j)
            return (sums[0] + fold(weighted), sums[1] + fold(weighted * value))

        return each_column(2, body)

    def set_stats(c, index, totals, inverse, gain_row):
        center = totals[0] * inverse
        scaling = lax.rsqrt(totals[1] * inverse - center * center + EPSILON)
        gain = params[gain_row : gain_row + 1] * scaling
        shift_row = gain_row + 6 if gain_row < 6 else gain_row + 1
        st[c, index, 0:1] = center
        st[c, index, 1:2] = scaling
        st[c, index, 2:3] = gain
        st[c, index, 3:4] = params[shift_row : shift_row + 1] - center * gain

    def affine(c, index):
        return st[c, index, 2:3], st[c, index, 3:4]

    def hat_of(c, index):
        return st[c, index, 0:1], st[c, index, 1:2]

    def inverse_out(c):
        return cn[c, 1:2]

    def inverse_in(c):
        return cn[c, 2:3]

    def place(shard):
        return shard // 16, lax.rem(shard // 4, 4), lax.rem(shard, 4)

    def cols_of(name, lanes):
        at, count = ROWS[name]
        value = w[:, :, :, at : at + count, lanes]
        return value.reshape(SHARDS * count, value.shape[-1])

    def rows_index(name, n):
        at, count = ROWS[name]
        if count == 16:
            return (n, slice(None), slice(None), slice(at, at + 16))
        return (n // 2, pl.ds(2 * lax.rem(n, 2), 2), slice(None), slice(at, at + 32))

    def rows_of(name, n):
        return w[rows_index(name, n)].reshape(256, C)

    def put_rows(name, n, value):
        shape = (4, 4, 16, C) if ROWS[name][1] == 16 else (2, 4, 32, C)
        w[rows_index(name, n)] = value.astype(BF16).reshape(shape)

    def shard_rows(name, shard):
        at, count = ROWS[name]
        return w[(*place(shard), slice(at, at + count))].astype(F32)

    def put_shard(name, shard, value):
        at, count = ROWS[name]
        w[(*place(shard), slice(at, at + count))] = value.astype(BF16)

    def tile(k):
        return slice(128 * k, 128 * k + 128)

    def build_conv(name):
        def shard(s):
            rows = shard_rows(name, s)
            for a in range(4):
                for k in range(2):
                    fs[pl.ds(2048 * k + 63 * s + a, 16, stride=4)] = rows[:, tile(2 * a + k)]

        loop(SHARDS, shard)
        lane = lax.broadcasted_iota(jnp.int32, (64, 256), 1) // 64

        def block(a):
            for tap in range(9):
                tiles = []
                for k in range(2):
                    at = 2048 * k + 224 * tap
                    tiles.append(
                        jnp.concatenate(
                            [
                                fs[pl.ds(at + a, 28, stride=4)],
                                jnp.zeros((4, 128), F32),
                                fs[pl.ds(at + 112 + a, 28, stride=4)],
                                jnp.zeros((4, 128), F32),
                            ],
                            0,
                        )
                    )
                dense = jnp.concatenate(tiles, 1)
                for g in range(4):
                    kd[a, 256 * tap + 64 * g : 256 * tap + 64 * g + 64] = jnp.where(
                        lane == g, dense, 0.0
                    ).astype(BF16)

        loop(4, block)

    def build_small(b):
        wd, wu = (wd0, wu0) if b == 0 else (wd1, wu1)
        fs[...] = jnp.zeros_like(fs)

        def shard(s):
            rows = shard_rows("misc0" if b == 0 else "misc1", s)
            if b == 0:
                for k in range(8):
                    fs[pl.ds(32 * s + k, 4, stride=8)] = rows[0:4, tile(k)]
                    fs[pl.ds(1024 + 256 * (k % 4) + 7 * s + k // 4, 4, stride=2)] = rows[
                        8:12, tile(k)
                    ]
            else:
                for k in range(8):
                    fs[pl.ds(1024 * (k % 2) + 32 * s + k // 2, 7, stride=4)] = rows[0:7, tile(k)]
                    fs[pl.ds(2048 + 256 * k + 7 * s, 7)] = rows[8:15, tile(k)]

        loop(SHARDS, shard)
        for k in range(1 + b):
            wd[:, tile(k)] = fs[1024 * k : 1024 * k + 1024].astype(BF16)
        gap = jnp.zeros((4, 128), F32)
        for g in range(4 + 4 * b):
            for k in range(8):
                if b == 0:
                    start = 1024 + 256 * (k % 4) + 56 * g + k // 4
                    part = fs[pl.ds(start, 28, stride=2)]
                else:
                    start = 2048 + 256 * k + 28 * g
                    part = fs[start : start + 28]
                wu[32 * g : 32 * g + 32, tile(k)] = jnp.concatenate([part, gap], 0).astype(BF16)

    def taps0():
        for a in range(3):
            for b in range(3):
                yield a * 3 + b, (0 if a == 1 else 1), (0 if b == 1 else 1), a, b

    def both(ref_of):
        return jnp.concatenate([ref_of(0), ref_of(1)], 0)

    def squeeze(c, b, pooled, wd, wu):
        width = wd.shape[1]
        raw = row_dot(pooled, wd[...], nn)
        squeezed = raw * sig(raw)
        gating = sig(row_dot(squeezed, wu[...], nn))
        sv[b, c, 0:1] = pooled
        sv[b, c, 1:2, 0:width] = raw
        sv[b, c, 2:3, 0:width] = squeezed
        sv[b, c, 3:4] = gating
        return gating

    def gate(c, b, index, conv_k, wd, wu, name, proj_k):
        a, shift = affine(c, index)

        def pool_chunk(j, sums):
            z = pool[c, conv_k, chunk(j)] * a + shift
            excited = keep(c, j) * (z * sig(z))
            pool[c, 7, chunk(j)] = excited
            return (sums[0] + fold(excited),)

        pooled = each_column(1, pool_chunk)[0] / crop_count(c)
        gating = squeeze(c, b, pooled, wd, wu)

        def gate_chunk(j):
            ga[b, c, chunk(j)] = (pool[c, 7, chunk(j)] * gating).astype(BF16)

        loop(14, gate_chunk)

        def project(n):
            pool[c, proj_k, :, col(n)] = nn(ga[b, c], cols_of(name, col(n)))

        loop(4, project)
        return moment_sums(c, lambda j: pool[c, proj_k, chunk(j)])

    def ungate(c, b, index, conv_k, wd, wu, name):
        width = wd.shape[1]

        def back(n):
            pool[c, 7, :, col(n)] = nt(dp_of(c), rows_of(name, n))

        loop(4, back)
        a, shift = affine(c, index)

        def gate_chunk(j, sums):
            z = pool[c, conv_k, chunk(j)] * a + shift
            excited = keep(c, j) * (z * sig(z))
            return (sums[0] + fold(pool[c, 7, chunk(j)] * excited),)

        d_gate = each_column(1, gate_chunk)[0]
        poll_crop(c, ("eback" if b == 0 else "bout", "a"))
        gating = sv[b, c, 3:4]
        d_raw = d_gate * gating * (1.0 - gating)
        raw = sv[b, c, 1:2, 0:width]
        d_squeeze = row_dot(d_raw, wu[...], nt) * slope_of(raw, sig(raw))
        d_pool = row_dot(d_squeeze, wd[...], nt) / crop_count(c)
        sv[b, c, 4:5] = d_raw
        sv[b, c, 5:6, 0:width] = d_squeeze
        center, scaling = hat_of(c, index)

        def slope_chunk(j, sums):
            value = pool[c, conv_k, chunk(j)]
            z = value * a + shift
            d = (pool[c, 7, chunk(j)] * gating + d_pool) * (keep(c, j) * slope_of(z, sig(z)))
            pool[c, 7, chunk(j)] = d
            return (sums[0] + fold(d), sums[1] + fold(d * ((value - center) * scaling)))

        return each_column(2, slope_chunk)

    def small_grads(b):
        width = 128 + 128 * b

        def pairs(x_row, x_width, y_row, y_width):
            xs, ys = [], []
            for c in range(2):
                xh, xl = split_rows([sv[b, c, x_row : x_row + 1, 0:x_width]])
                yh, yl = split_rows([sv[b, c, y_row : y_row + 1, 0:y_width]])
                xs += [xh[0], xh[0], xl[0]]
                ys += [yh[0], yl[0], yh[0]]
            return tn(stacked(xs), stacked(ys))

        grad_down = pairs(0, C, 5, width)
        for k in range(1 + b):
            fs[1024 * k : 1024 * k + 1024] = grad_down[:, tile(k)]
        grad_up = pairs(2, width, 4, C)
        for g in range(4 + 4 * b):
            for k in range(8):
                part = grad_up[32 * g : 32 * g + 28, tile(k)]
                if b == 0:
                    fs[pl.ds(1024 + 256 * (k % 4) + 56 * g + k // 4, 28, stride=2)] = part
                else:
                    fs[2048 + 256 * k + 28 * g : 2048 + 256 * k + 28 * g + 28] = part

        def shard(s):
            tiles = []
            for k in range(8):
                if b == 0:
                    count = 4
                    first = fs[pl.ds(32 * s + k, 4, stride=8)]
                    second = fs[pl.ds(1024 + 256 * (k % 4) + 7 * s + k // 4, 4, stride=2)]
                else:
                    count = 7
                    first = fs[pl.ds(1024 * (k % 2) + 32 * s + k // 2, 7, stride=4)]
                    second = fs[pl.ds(2048 + 256 * k + 7 * s, 7)]
                gap = jnp.zeros((8 - count, 128), F32)
                tiles.append(jnp.concatenate([first, gap, second, gap], 0))
            put_shard("misc0" if b == 0 else "misc1", s, jnp.concatenate(tiles, 1))

        loop(SHARDS, shard)

    def norm_coefficients(c, index, totals, inverse, gain_row, kind):
        center, scaling = hat_of(c, index)
        ng[gain_row : gain_row + 1] += totals[1]
        shift_row = gain_row + 6 if gain_row < 6 else gain_row + 1
        ng[shift_row : shift_row + 1] += totals[0]
        a = st[c, index, 2:3]
        slope = -a * scaling * (totals[1] * inverse)
        offset = -a * (totals[0] * inverse) - slope * center
        return a, slope, offset

    def conv_grad(act_of, v_of, name):
        lane = lax.broadcasted_iota(jnp.int32, (64, 256), 1) // 64

        def block(a):
            for tap in range(9):
                dense = tn(
                    both(lambda c: act_of(c, tap, col(a))), both(lambda c: v_of(c, tap, col(a)))
                )
                own = jnp.where(lane == 0, dense[0:64], 0.0)
                for g in range(1, 4):
                    own = own + jnp.where(lane == g, dense[64 * g : 64 * g + 64], 0.0)
                for k in range(2):
                    at = 2048 * k + 224 * tap
                    fs[pl.ds(at + a, 28, stride=4)] = own[0:28, 128 * k : 128 * k + 128]
                    fs[pl.ds(at + 112 + a, 28, stride=4)] = own[32:60, 128 * k : 128 * k + 128]

        loop(4, block)

        def shard(s):
            tiles = [
                fs[pl.ds(2048 * k + 63 * s + a, 16, stride=4)] for a in range(4) for k in range(2)
            ]
            put_shard(name, s, jnp.concatenate(tiles, 1))

        loop(SHARDS, shard)

    def outer(left_of, right_of, name):
        def block(m):
            put_rows(name, m, tn(both(lambda c: left_of(c, col(m))), both(right_of)))

        loop(SHARDS * ROWS[name][1] // 256, block)

    z, yx = digit // 4, lax.rem(digit, 4)
    bits = (1 + section, 2 - section)

    def flip(bit):
        return yx + bit * (1 - 2 * lax.rem(yx // bit, 2))

    def push(src, dst, to, sends, recvs):
        pltpu.make_async_remote_copy(
            src_ref=src, dst_ref=dst, send_sem=sends, recv_sem=recvs,
            device_id=(section, to * v + rest), device_id_type=MESH,
        ).start()

    def push_sibling(src, dst, sends, recvs):
        pltpu.make_async_remote_copy(
            src_ref=src, dst_ref=dst, send_sem=sends, recv_sem=recvs,
            device_id=(other, me), device_id_type=MESH,
        ).start()

    def arrive(ref, sem):
        pltpu.make_async_copy(ref, ref, sem).wait()

    def gather(k, phase):
        start, stop = GATHERS[k]
        rows = pl.ds(start, stop - start)
        sent = w.at[section, :, :, rows]
        if phase > 0:
            sem = grecv.at[k, phase - 1]
            if phase == 1:
                arrive(w.at[section, pl.ds(0, 3), 0, rows], sem)
            elif phase == 2:
                arrive(sent.at[:, 0], sem)
            elif phase == 3:
                arrive(sent.at[:, pl.ds(0, 2)], sem)
            else:
                arrive(sent, sem)
        if phase == 4:
            arrive(w.at[section, pl.ds(0, 3), 0, rows], gsend.at[k, 0])
            arrive(sent.at[:, 0], gsend.at[k, 1])
            arrive(sent.at[:, pl.ds(0, 2)], gsend.at[k, 2])
            arrive(sent, gsend.at[k, 3])
            return
        sems = (gsend.at[k, phase], grecv.at[k, phase])
        if phase == 0:
            own = w.at[section, z, yx, rows]
            for hop in range(1, 4):
                push(own, own, lax.rem(z + hop, 4) * 4 + yx, *sems)
        elif phase == 1:
            push(sent.at[:, yx], sent.at[:, yx], z * 4 + flip(bits[0]), *sems)
        elif phase == 2:
            for at in (yx, flip(bits[0])):
                push(sent.at[:, at], sent.at[:, at], z * 4 + flip(bits[1]), *sems)
        else:
            push_sibling(sent, sent, *sems)

    def poll(point):
        for k, phase in GATHER_PLAN.get(point, ()):
            gather(k, phase)
        for k, phase in SCATTER_PLAN.get(point, ()):
            scatter(k, phase)

    def poll_crop(c, point):
        for one in range(2):
            name = point[0] + str(one) + point[1]
            if name in GATHER_PLAN or name in SCATTER_PLAN:
                pl.when(c == one)(lambda: poll(name))

    def crops(body, point=None):
        def run(c):
            body(c)
            if point is not None:
                poll_crop(c, (point, ""))

        loop(2, run)

    def landing(k, phase, block, count):
        last = k - CHAINED
        if phase == 0:
            if k < 4:
                return e_buf.at[pl.ds(pl.multiple_of(block * count, 16), count)]
            ref = a1 if k == 4 else hid if last == 0 else ga.at[0]
            return ref.at[
                block // 8, pl.ds(pl.multiple_of(lax.rem(block, 8) * count, 16), count)
            ]
        if phase == 1:
            if last < 0:
                return ga.at[1, block // 4, pl.ds(block % 4 * count, count)]
            ref = hid if last == 0 else ga.at[0]
            return ref.at[block // 4, pl.ds(128 + block % 4 * 16, 16)]
        if phase == 2:
            if last < 0:
                return wu1.at[pl.ds(block * count, count)]
            ref = ga.at[0] if last == 0 else hid
            return ref.at[block // 2, pl.ds(192 + block % 2 * 16, 16)]
        if last >= 0:
            return wu0.at[pl.ds(64 * last + 16 * block, 16)]
        if k % 2:
            return wu1.at[pl.ds(160 + block * count, count)]
        return stage.at[block, pl.ds(0, count)]

    def landed(k, phase, count):
        return w.at[section, pl.ds(0, (4, 2, 1, 1)[phase]), pl.ds(0, (4, 4, 4, 3)[phase]), pl.ds(0, count)]

    def add_landed(k, phase, block, place_of, start, count):
        ref = landing(k, phase, block, count)
        index = (section, *place_of(block), pl.ds(start, count))
        w[index] = (w[index].astype(F32) + ref[...].astype(F32)).astype(BF16)

    def credit(at, to):
        pl.semaphore_signal(
            free.at[at], inc=1, device_id=(section, to * v + rest), device_id_type=MESH
        )

    def credit_sibling(at):
        pl.semaphore_signal(free.at[at], inc=1, device_id=(other, me), device_id_type=MESH)

    def credit_z(at):
        for hop in range(1, 4):
            credit(at, lax.rem(z + hop, 4) * 4 + yx)

    def scatter(k, phase):
        start, stop = SCATTERS[k]
        count = stop - start
        rows = pl.ds(start, count)
        first, second = flip(bits[1]), flip(bits[0])
        more = k + 1 < CHAINED
        if phase > 0:
            arrive(landed(k, phase - 1, count), rrecv.at[k, phase - 1])
        if phase == 1:
            loop(16, lambda b: add_landed(k, 0, b, lambda b: (b // 4, lax.rem(b, 4)), start, count))
            if k < 3:
                credit_sibling(0)
        elif phase == 2:
            for b in range(8):
                add_landed(k, 1, b, lambda b: (b // 2, yx if b % 2 == 0 else second), start, count)
            if more:
                credit(1, z * 4 + first)
        elif phase == 3:
            for b in range(4):
                add_landed(k, 2, b, lambda b: (b, yx), start, count)
            if more:
                credit(2, z * 4 + second)
            if k == 0:
                credit_z(5)
        elif phase == 4:
            total = w[section, z, yx, start:stop].astype(F32)
            for b in range(3):
                total = total + landing(k, 3, b, count)[...].astype(F32)
            pool[0, 1, start:stop] = total
            if k + 2 < CHAINED:
                credit_z(5 if k % 2 else 3)
            for sent in range(4):
                arrive(landed(k, sent, count), rsend.at[k, sent])
            return
        sems = (rsend.at[k, phase], rrecv.at[k, phase])
        if phase == 0:
            if k < 4 or k == CHAINED:
                pl.semaphore_wait(free.at[0 if k < 4 else 4], 1)

            def send(b):
                push_sibling(
                    w.at[other, b // 4, lax.rem(b, 4), rows], landing(k, 0, b, count), *sems
                )

            loop(16, send)
        elif phase == 1:
            if k < CHAINED:
                pl.semaphore_wait(free.at[1], 1)
            for b in range(8):
                to = first if b % 2 == 0 else first + second - yx
                push(
                    w.at[section, b // 2, to, rows], landing(k, 1, b, count), z * 4 + first, *sems
                )
        elif phase == 2:
            if k < CHAINED:
                pl.semaphore_wait(free.at[2], 1)
            for b in range(4):
                push(
                    w.at[section, b, second, rows], landing(k, 2, b, count), z * 4 + second, *sems
                )
        else:
            if k < CHAINED:
                pl.semaphore_wait(free.at[5 if k % 2 else 3], 3)
            for hop in range(1, 4):
                to = lax.rem(z + hop, 4)
                push(w.at[section, to, yx, rows], landing(k, 3, hop - 1, count), to * 4 + yx, *sems)

    shares = {}
    at = 0
    for name, ref, count in (
        ("wa0", l_wa0, 14), ("k0", l_k0, 16), ("ws", l_ws, 14), ("wd0", l_wd0, 4),
        ("wu0", l_wu0, 4), ("wc0", l_wc0, 28), ("wa1", l_wa1, 28), ("k1", l_k1, 16),
        ("wd1", l_wd1, 7), ("wu1", l_wu1, 7), ("wc1", l_wc1, 28),
    ):
        fs[at : at + ref.shape[0]] = ref[...].astype(F32)
        value = jnp.concatenate([fs[pl.ds(at + k, count, stride=7)] for k in range(7)], 1)
        room = 8 if count < 8 else count + -count % 16
        if room > count:
            value = jnp.concatenate([value, jnp.zeros((room - count, D), F32)], 0)
        shares[name] = value
        at += ref.shape[0] + -ref.shape[0] % 8
    load_map.wait()
    own_rows = jnp.concatenate([shares[name] for name in ORDER], 0).astype(BF16)
    for n in range(4):
        lanes = slice(256 * n, 256 * n + 256)
        w[section, z, yx, :, lanes] = nn(own_rows, e_buf[:, lanes]).astype(BF16)
    pl.semaphore_wait(barrier, MEMBERS + v - 1)
    poll("own")
    exchange = [
        to_sibling(upstream.at[theirs], up_buf.at[section], 1),
        to_sibling(features.at[theirs], x_buf.at[section], 0),
    ]
    for copy in exchange:
        copy.start()
    copies = exchange + copies
    ng[...] = jnp.zeros_like(ng)
    guard = jnp.zeros((GUARD, C), BF16)
    for ref, count in ((a0, 4), (d_buf, 2)):
        for c in range(2):
            for k in range(count):
                ref[c, k, 0:GUARD] = guard
                ref[c, k, GUARD + PX :] = guard
    for c in range(2):
        for ref in (a1, dp_buf):
            ref[c, 0:GUARD] = guard
            ref[c, GUARD + PX :] = guard

    halves = jnp.concatenate(
        [short_gain_in[...].astype(F32), short_shift_in[...].astype(F32)], 1
    )
    pair[section] = jnp.concatenate(
        [gain_in[k] for k in range(3)] + [shift_in[k] for k in range(3)]
        + [halves, jnp.zeros((1, D), F32)],
        0,
    )
    swap = to_sibling(pair.at[section], pair.at[section], 3)
    swap.start()
    swap.wait()
    first, second = pair[0], pair[1]
    short_gain_row = jnp.concatenate([first[6:7, 0:DIN], second[6:7, 0:DIN]], 1)
    short_shift_row = jnp.concatenate([first[6:7, DIN:], second[6:7, DIN:]], 1)
    rows = jnp.concatenate(
        [
            first[0:3], second[0:3], first[3:6], second[3:6], short_gain_row, short_shift_row,
            jnp.zeros((2, D), F32),
        ],
        0,
    )

    def thirds(value):
        high = value.astype(BF16)
        left = value - high.astype(F32)
        middle = left.astype(BF16)
        return jnp.concatenate([high, middle, (left - middle.astype(F32)).astype(BF16)], 0)

    wide = nn(thirds(rows), e_buf[...])
    params[...] = wide[0:16] + wide[16:32] + wide[32:48]
    poll("params")

    for copy in copies:
        copy.wait()

    def gather_slices(ref, rows):
        pad = jnp.zeros((16 - rows, D), BF16)
        return jnp.concatenate(
            [jnp.concatenate([ref[:, D * j : D * j + D], pad], 0) for j in range(OUT)], 0
        )

    def cotangent(c):
        for h in range(2):
            x = gather_slices(up_buf.at[h, c], 7)
            for n in range(4):
                y = nn(x, e_buf[:, 256 * n : 256 * n + 256])
                for j in range(OUT):
                    count = 16 if h == 0 else 7
                    pool[c, 3, 16 * j + 7 * h : 16 * j + 7 * h + count, 256 * n : 256 * n + 256] = y[
                        16 * j : 16 * j + count
                    ]

    crops(cotangent, "cot")
    load_map = local_copy(expand.at[0], e_buf, 2)
    load_map.start()
    fs[...] = jnp.zeros_like(fs)
    load_map.wait()

    def phases(c):
        for h in range(2):
            x = gather_slices(x_buf.at[h, c], 14)
            for n in range(4):
                y = nn(x, e_buf[:, 256 * n : 256 * n + 256])
                for j in range(OUT):
                    for k in range(2):
                        fs[pl.ds(512 * (2 * n + k) + 32 * j + 14 * h, 14)] = y[
                            16 * j : 16 * j + 14, 128 * k : 128 * k + 128
                        ]
        for q in range(2):
            def take(j):
                for k in range(8):
                    u_buf[c, q, chunk(j), 128 * k : 128 * k + 128] = fs[
                        pl.ds(512 * k + 32 * j + q, 16, stride=2)
                    ].astype(BF16)

            loop(14, take)

    crops(phases, "ph")
    load_map = local_copy(expand.at[1], e_buf, 2)
    load_map.start()
    poll("need_wa0")

    def entry_inner(c):
        for q in range(2):
            for r in range(2):
                def product(n):
                    inn[c, 2 * q + r, :, col(n)] = nn(
                        u_buf[c, q, :, 512 * r : 512 * r + 512], cols_of("wa0", col(n))
                    )

                loop(4, product)
            poll_crop(c, ("in", "ab"[q]))

        def body(j, sums):
            mask = keep(c, j)
            first, second = sums
            for k in range(4):
                value = inn[c, k, chunk(j)]
                weighted = value * mask
                first = first + fold(weighted)
                second = second + fold(weighted * value)
            return (first, second)

        sums = each_column(2, body)
        own = jnp.zeros((1, C), F32) + crop_count(c)
        ar_start(0, c, [sums[0], sums[1], own, own])

    crops(entry_inner, "in")
    poll("need_k0")
    build_conv("k0")
    poll("bk0")

    def entry_conv(c):
        totals = ar_wait(0, c, 4)
        cn[c, 0:1] = totals[2]
        cn[c, 1:2] = 1.0 / totals[2]
        cn[c, 2:3] = 0.25 / totals[2]
        set_stats(c, 0, totals, inverse_in(c), 0)
        a, shift = affine(c, 0)

        def activate(j):
            mask = keep(c, j)
            for q in range(2):
                for r in range(2):
                    z = inn[c, 2 * q + r, chunk(j)] * a + shift
                    act = mask * (z * sig(z))
                    a0[c, 2 * q + r, chunk(j, GUARD)] = act.astype(BF16)
                    if q == 1:
                        d_buf[c, r, chunk(j, GUARD)] = pltpu.roll(act, 1, 0).astype(BF16)

        loop(14, activate)

        poll_crop(c, ("conv", "a"))

        def convolve(n):
            patches = []
            for tap, q, r, ta, tb in taps0():
                at = GUARD - 16 if tb == 0 else GUARD
                src = d_buf.at[c, r] if ta == 0 else a0.at[c, 2 * q + r]
                patches.append(src[at : at + PX, col(n)])
            pool[c, 0, :, col(n)] = nn(jnp.concatenate(patches, 1), kd[n])

        loop(4, convolve)
        ar_start(1, c, moment_sums(c, lambda j: pool[c, 0, chunk(j)]))

    crops(entry_conv, "conv")
    poll("need_ws")

    def strided(c):
        def product(n):
            pool[c, 2, :, col(n)] = nn(u_buf[c, 0, :, 0:512], cols_of("ws", col(n)))

        loop(4, product)

    crops(strided, "str")
    build_small(0)
    poll("need_wc0")

    def entry_gate(c):
        totals = ar_wait(1, c, 2)
        set_stats(c, 1, totals, inverse_out(c), 1)
        sums = gate(c, 0, 1, 0, wd0, wu0, "wc0", 1)
        ar_start(2, c, sums + moment_sums(c, lambda j: pool[c, 2, chunk(j)]))

    crops(entry_gate, "gate")
    poll("need_k1")
    build_conv("k1")
    poll("need_wa1")

    def entry_pre(c, j):
        a, shift = affine(c, 2)
        short_a, short_shift = affine(c, 3)
        return (
            pool[c, 1, chunk(j)] * a + pool[c, 2, chunk(j)] * short_a + (shift + short_shift)
        )

    def entry_out(c):
        totals = ar_wait(2, c, 4)
        set_stats(c, 2, totals[0:2], inverse_out(c), 2)
        set_stats(c, 3, totals[2:4], inverse_out(c), 12)

        def finish(j):
            z = entry_pre(c, j)
            hid[c, chunk(j)] = (keep(c, j) * (z * sig(z))).astype(BF16)

        loop(14, finish)

        def product(n):
            pool[c, 4, :, col(n)] = nn(hid[c], cols_of("wa1", col(n)))

        loop(4, product)
        ar_start(3, c, moment_sums(c, lambda j: pool[c, 4, chunk(j)]))

    crops(entry_out, "out")

    def body_conv(c):
        set_stats(c, 4, ar_wait(3, c, 2), inverse_out(c), 3)
        a, shift = affine(c, 4)

        def activate(j):
            z = pool[c, 4, chunk(j)] * a + shift
            act = keep(c, j) * (z * sig(z))
            a1[c, chunk(j, GUARD)] = act.astype(BF16)
            d_buf[c, 0, chunk(j, GUARD)] = pltpu.roll(act, 1, 0).astype(BF16)
            d_buf[c, 1, chunk(j, GUARD)] = pltpu.roll(act, 15, 0).astype(BF16)

        loop(14, activate)

        def convolve(n):
            rows = (d_buf.at[c, 0], a1.at[c], d_buf.at[c, 1])
            patches = [
                rows[ta][16 * tb : 16 * tb + PX, col(n)] for ta in range(3) for tb in range(3)
            ]
            pool[c, 5, :, col(n)] = nn(jnp.concatenate(patches, 1), kd[n])

        loop(4, convolve)
        ar_start(4, c, moment_sums(c, lambda j: pool[c, 5, chunk(j)]))

    crops(body_conv, "bconv")
    poll("need_wc1")
    build_small(1)

    def body_gate(c):
        set_stats(c, 5, ar_wait(4, c, 2), inverse_out(c), 4)
        ar_start(5, c, gate(c, 1, 5, 5, wd1, wu1, "wc1", 6))

    loop(2, body_gate)

    def body_out(c):
        set_stats(c, 6, ar_wait(5, c, 2), inverse_out(c), 5)
        a, shift = affine(c, 6)
        center, scaling = hat_of(c, 6)

        def finish(j, sums):
            value = pool[c, 6, chunk(j)]
            z = value * a + shift + hid[c, chunk(j)].astype(F32)
            mask = keep(c, j)
            s = sig(z)
            dp_buf[c, chunk(j, GUARD)] = (mask * (z * s)).astype(BF16)
            d_pre = pool[c, 3, chunk(j)] * (mask * slope_of(z, s))
            pool[c, 3, chunk(j)] = d_pre
            return (sums[0] + fold(d_pre), sums[1] + fold(d_pre * ((value - center) * scaling)))

        ar_start(6, c, each_column(2, finish))

    loop(2, body_out)
    load_map.wait()

    def narrow(value, store):
        for start, width in ((0, 256), (256, 256), (512, 256), (768, 128)):
            store(start, width, nt(value, e_buf[start : start + width]))

    def body_emit(c):
        def store(start, width, y):
            for j in range(OUT):
                for h in range(2):
                    up_buf[h, c, :, D * j + start : D * j + start + width] = y[
                        16 * j + 7 * h : 16 * j + 7 * h + 7
                    ].astype(BF16)

        narrow(dp_of(c), store)

    loop(2, body_emit)
    out_copies = [
        to_sibling(up_buf.at[other], out.at[mine], 2),
        local_copy(up_buf.at[section], out.at[mine], 1),
    ]
    for copy in out_copies:
        copy.start()

    credit_sibling(0)

    def body_back_out(c):
        a, slope, offset = norm_coefficients(c, 6, ar_wait(6, c, 2), inverse_out(c), 5, 0)

        def project(j):
            value = pool[c, 6, chunk(j)]
            dp_buf[c, chunk(j, GUARD)] = (
                keep(c, j) * (a * pool[c, 3, chunk(j)] + slope * value + offset)
            ).astype(BF16)

        loop(14, project)
        ar_start(7, c, ungate(c, 1, 5, 5, wd1, wu1, "wc1"))

    crops(body_back_out, "bout")
    credit(2, z * 4 + flip(bits[0]))
    credit_z(3)
    outer(lambda c, l: ga[1, c, :, l], dp_of, "wc1")
    credit(1, z * 4 + flip(bits[1]))
    small_grads(1)
    poll("small1")

    def conv_cotangent(c, index, conv_k, a, slope, offset, versions):
        def body(j):
            d = keep(c, j) * (a * pool[c, 7, chunk(j)] + slope * pool[c, conv_k, chunk(j)] + offset)
            d_buf[c, 0, chunk(j, GUARD)] = d.astype(BF16)
            d_buf[c, 1, chunk(j, GUARD)] = pltpu.roll(d, 15, 0).astype(BF16)
            if versions == 3:
                dp_buf[c, chunk(j, GUARD)] = pltpu.roll(d, 1, 0).astype(BF16)

        loop(14, body)

    def v_body(c, tap, lanes):
        ta, tb = tap // 3, tap % 3
        ref = (d_buf.at[c, 1], d_buf.at[c, 0], dp_buf.at[c])[ta]
        return ref[32 - 16 * tb : 32 - 16 * tb + PX, lanes]

    def v_entry(c, tap, lanes):
        ta, tb = tap // 3, tap % 3
        at = 32 if tb == 0 else 16
        return d_buf[c, 1 if ta == 0 else 0, at : at + PX, lanes]

    def body_back_conv(c):
        a, slope, offset = norm_coefficients(c, 5, ar_wait(7, c, 2), inverse_out(c), 4, 0)
        conv_cotangent(c, 5, 5, a, slope, offset, 3)

        def back(n):
            total = nt(v_body(c, 0, col(n)), kd[n, 0:256])
            for tap in range(1, 9):
                total = total + nt(v_body(c, tap, col(n)), kd[n, 256 * tap : 256 * tap + 256])
            pool[c, 7, :, col(n)] = total

        loop(4, back)
        poll_crop(c, ("bback", "a"))
        a, shift = affine(c, 4)
        center, scaling = hat_of(c, 4)

        def body(j, sums):
            value = pool[c, 4, chunk(j)]
            z = value * a + shift
            d = pool[c, 7, chunk(j)] * (keep(c, j) * slope_of(z, sig(z)))
            pool[c, 7, chunk(j)] = d
            return (sums[0] + fold(d), sums[1] + fold(d * ((value - center) * scaling)))

        ar_start(8, c, each_column(2, body))

    crops(body_back_conv, "bback")
    conv_grad(lambda c, tap, l: a1[c, GUARD : GUARD + PX, l], v_body, "k1")
    poll("k1")

    def body_back_in(c):
        a, slope, offset = norm_coefficients(c, 4, ar_wait(8, c, 2), inverse_out(c), 3, 0)

        def body(j):
            dp_buf[c, chunk(j, GUARD)] = (
                keep(c, j) * (a * pool[c, 7, chunk(j)] + slope * pool[c, 4, chunk(j)] + offset)
            ).astype(BF16)

        loop(14, body)

        def back(n):
            pool[c, 3, :, col(n)] = (
                (nt(dp_of(c), rows_of("wa1", n)) + pool[c, 3, :, col(n)]).astype(BF16).astype(F32)
            )

        loop(4, back)
        poll_crop(c, ("bin", "a"))
        center, scaling = hat_of(c, 2)
        short_center, short_scaling = hat_of(c, 3)

        def pre(j, sums):
            z = entry_pre(c, j)
            d = pool[c, 3, chunk(j)] * (keep(c, j) * slope_of(z, sig(z)))
            pool[c, 3, chunk(j)] = d
            return (
                sums[0] + fold(d),
                sums[1] + fold(d * ((pool[c, 1, chunk(j)] - center) * scaling)),
                sums[2] + fold(d * ((pool[c, 2, chunk(j)] - short_center) * short_scaling)),
            )

        sums = each_column(3, pre)
        ar_start(9, c, sums + [sums[0]])

    crops(body_back_in, "bin")
    outer(lambda c, l: hid[c, :, l], dp_of, "wa1")
    poll("wa1")
    build_conv("k0")

    def entry_back_out(c):
        totals = ar_wait(9, c, 4)
        a, slope, offset = norm_coefficients(c, 2, totals[0:2], inverse_out(c), 2, 0)
        short = norm_coefficients(c, 3, [totals[0], totals[2]], inverse_out(c), 12, 0)

        def project(j):
            mask = keep(c, j)
            d = pool[c, 3, chunk(j)]
            dp_buf[c, chunk(j, GUARD)] = (
                mask * (a * d + slope * pool[c, 1, chunk(j)] + offset)
            ).astype(BF16)
            hid[c, chunk(j)] = (
                mask * (short[0] * d + short[1] * pool[c, 2, chunk(j)] + short[2])
            ).astype(BF16)

        loop(14, project)

        def back(n):
            pool[c, 2, :, col(n)] = nt(hid[c], rows_of("ws", n))

        loop(2, back)
        ar_start(10, c, ungate(c, 0, 1, 0, wd0, wu0, "wc0"))

    crops(entry_back_out, "eback")
    outer(lambda c, l: ga[0, c, :, l], dp_of, "wc0")
    poll("wc0")
    outer(lambda c, l: u_buf[c, 0, :, l], lambda c: hid[c], "ws")
    credit_sibling(4)
    small_grads(0)
    poll("small0")

    def entry_back_conv(c):
        a, slope, offset = norm_coefficients(c, 1, ar_wait(10, c, 2), inverse_out(c), 1, 0)
        conv_cotangent(c, 1, 0, a, slope, offset, 2)
        for q in range(2):
            for r in range(2):
                def back(n):
                    total = None
                    for tap, tq, tr, ta, tb in taps0():
                        if (tq, tr) == (q, r):
                            term = nt(v_entry(c, tap, col(n)), kd[n, 256 * tap : 256 * tap + 256])
                            total = term if total is None else total + term
                    pool[c, 4 + 2 * q + r, :, col(n)] = total

                loop(4, back)
            poll_crop(c, ("econv", "ab"[q]))
        a, shift = affine(c, 0)
        center, scaling = hat_of(c, 0)

        def body(j, sums):
            mask = keep(c, j)
            first, second = sums
            for k in range(4):
                value = inn[c, k, chunk(j)]
                z = value * a + shift
                d = pool[c, 4 + k, chunk(j)] * (mask * slope_of(z, sig(z)))
                pool[c, 4 + k, chunk(j)] = d
                first = first + fold(d)
                second = second + fold(d * ((value - center) * scaling))
            return (first, second)

        ar_start(11, c, each_column(2, body))

    crops(entry_back_conv, "econv")

    def act_entry(c, tap, lanes):
        q = 0 if tap // 3 == 1 else 1
        r = 0 if tap % 3 == 1 else 1
        return a0[c, 2 * q + r, GUARD : GUARD + PX, lanes]

    conv_grad(act_entry, v_entry, "k0")
    poll("k0")
    load_map = local_copy(expand.at[0], e_buf, 2)
    load_map.start()
    for copy in out_copies:
        copy.wait()

    def entry_back_in(c):
        a, slope, offset = norm_coefficients(c, 0, ar_wait(11, c, 2), inverse_in(c), 0, 0)

        def body(j):
            mask = keep(c, j)
            for k in range(4):
                a0[c, k, chunk(j, GUARD)] = (
                    mask * (a * pool[c, 4 + k, chunk(j)] + slope * inn[c, k, chunk(j)] + offset)
                ).astype(BF16)

        loop(14, body)

    loop(2, entry_back_in)
    swap = to_sibling(ng, ng_in, 3)
    swap.start()

    def input_grad(m):
        total = None
        for q in range(2):
            for r in range(2):
                at = pl.ds(pl.multiple_of(512 * r + 256 * m, 256), 256)
                term = tn(
                    both(lambda c: u_buf[c, q, :, at]),
                    both(lambda c: a0[c, 2 * q + r, GUARD : GUARD + PX]),
                )
                total = term if total is None else total + term
        return total

    def input_block(m):
        dp_buf[m] = rows_of("wa0", m)
        put_rows("wa0", m, input_grad(m))

    loop(2, input_block)
    poll("wa0")

    def entry_back_input(c):
        for q in range(2):
            for r in range(2):
                def back(n):
                    total = nt(a0[c, 2 * q + r, GUARD : GUARD + PX], dp_buf[n])
                    if q == 0 and r == 0:
                        total = total + pool[c, 2, :, col(n)]
                    at = pl.ds(pl.multiple_of(512 * r + 256 * n, 256), 256)
                    d_buf[c, q, 0:PX, at] = total.astype(BF16)

                loop(2, back)
            if q == 0:
                poll_crop(c, ("input", "a"))

    crops(entry_back_input, "input")

    def entry_emit(c):
        for q in range(2):
            def store(start, width, y):
                for j in range(OUT):
                    for k in range(width // 128):
                        fs[pl.ds(512 * (start // 128 + k) + 32 * j + q, 14, stride=2)] = y[
                            16 * j : 16 * j + 14, 128 * k : 128 * k + 128
                        ]

            narrow(d_buf[c, q, 0:PX], store)
        poll_crop(c, ("emit", "a"))
        for h in range(2):
            for j in range(OUT):
                for k in range(7):
                    x_buf[h, c, :, D * j + 128 * k : D * j + 128 * k + 128] = fs[
                        512 * k + 32 * j + 14 * h : 512 * k + 32 * j + 14 * h + 14
                    ].astype(BF16)

    load_map.wait()
    crops(entry_emit, "emit")
    load_map = local_copy(expand.at[1], e_buf, 2)
    load_map.start()
    last = [
        to_sibling(x_buf.at[other], grad.at[mine], 4),
        local_copy(x_buf.at[section], grad.at[mine], 0),
    ]
    for copy in last:
        copy.start()
    poll("tail")
    load_map.wait()
    swap.wait()
    total = thirds(ng[...] + ng_in[...])
    total = nt(total, e_buf[...])
    total = total[0:16] + total[16:32] + total[32:48]

    def own(top, low):
        return jnp.where(section == 0, top, low)

    for k in range(3):
        gain_out[k] = own(total[k : k + 1], total[k + 3 : k + 4])
        shift_out[k] = own(total[k + 6 : k + 7], total[k + 9 : k + 10])
    short_gain_out[...] = own(total[12:13, 0:DIN], total[12:13, DIN:])
    short_shift_out[...] = own(total[13:14, 0:DIN], total[13:14, DIN:])
    total = pool[0, 1, 0:192]
    high = total.astype(BF16)
    low = (total - high.astype(F32)).astype(BF16)
    final = nt(high, e_buf[...]) + nt(low, e_buf[...])
    for name, ref, count in (
        ("wa0", o_wa0, 14), ("k0", o_k0, 16), ("ws", o_ws, 14), ("wd0", o_wd0, 4),
        ("wu0", o_wu0, 4), ("wc0", o_wc0, 28), ("wa1", o_wa1, 28), ("k1", o_k1, 16),
        ("wd1", o_wd1, 7), ("wu1", o_wu1, 7), ("wc1", o_wc1, 28),
    ):
        if name[1] in "du":
            at = ROWS["misc" + name[2]][0] + (8 if name[1] == "u" else 0)
        else:
            at = ROWS[name][0]
        for k in range(7):
            ref[pl.ds(k, count, stride=7)] = final[at : at + count, 128 * k : 128 * k + 128]
    for copy in last:
        copy.wait()


def lane_maps():
    at = np.arange(D)
    first = np.zeros((D, C), np.float32)
    first[at, at // 14 * 16 + at % 14] = 1
    second = np.zeros((D, C), np.float32)
    second[at, at // 28 * 32 + at % 28] = 1
    return np.stack([first, second])


def main_call(n_dp, *args):
    v = n_dp // MEMBERS
    any_space = pl.BlockSpec(memory_space=pl.ANY)
    vmem = pl.BlockSpec(memory_space=pltpu.VMEM)
    smem = pl.BlockSpec(memory_space=pltpu.SMEM)
    shape = lambda *s, dtype=BF16: jax.ShapeDtypeStruct(s, dtype)
    flat = [shape(count, 128, dtype=F32) for count in LINES]
    outs = [
        shape(4, 7, 12544), shape(4, 14, 12544), *flat,
        shape(3, 1, D, dtype=F32), shape(3, 1, D, dtype=F32),
        shape(1, DIN, dtype=F32), shape(1, DIN, dtype=F32),
    ]
    dma = pltpu.SemaphoreType.DMA
    scratch = [
        pltpu.VMEM((2, 4, PX, C), F32),
        pltpu.VMEM((2, 8, PX, C), F32),
        pltpu.VMEM((2, 2, PX, C), BF16),
        pltpu.VMEM((2, 4, PX + 2 * GUARD, C), BF16),
        pltpu.VMEM((2, PX + 2 * GUARD, C), BF16),
        pltpu.VMEM((2, 2, PX + 2 * GUARD, C), BF16),
        pltpu.VMEM((2, 2, PX, C), BF16),
        pltpu.VMEM((2, PX, C), BF16),
        pltpu.VMEM((2, PX + 2 * GUARD, C), BF16),
        pltpu.VMEM((2, 2, 14, 12544), BF16),
        pltpu.VMEM((2, 2, 7, 12544), BF16),
        pltpu.VMEM((4096, 128), F32),
        pltpu.VMEM((4, 2304, 256), BF16),
        pltpu.VMEM((D, C), BF16),
        pltpu.VMEM((2, 4, 4, 192, C), BF16),
        pltpu.VMEM((C, 128), BF16),
        pltpu.VMEM((128, C), BF16),
        pltpu.VMEM((C, 256), BF16),
        pltpu.VMEM((256, C), BF16),
        pltpu.VMEM((3, 48, C), BF16),
        pltpu.VMEM((16, C), F32),
        pltpu.VMEM((2, 8, D), F32),
        pltpu.VMEM((2, 7, 8, C), F32),
        pltpu.VMEM((2, 2, 8, C), F32),
        pltpu.VMEM((2, 8, C), F32),
        pltpu.VMEM((16, C), F32),
        pltpu.VMEM((16, C), F32),
        pltpu.VMEM((2, 2, MEMBERS, 2, C), F32),
        pltpu.VMEM((2, MEMBERS, 4, C), F32),
        pltpu.VMEM((2, 2, v, 4, C), F32),
        dma((2, 2)), dma((2, 2)), dma((2, 2)), dma((2, 2)), dma((5,)), dma((5,)), dma((4,)),
        dma((7, 4)), dma((7, 4)), dma((7, 4)), dma((7, 4)), pltpu.SemaphoreType.REGULAR((6,)),
    ]
    return pl.pallas_call(
        functools.partial(main_kernel, n_dp),
        out_shape=outs,
        in_specs=[any_space, any_space, smem, any_space] + [vmem] * 15,
        out_specs=[any_space] * 2 + [vmem] * 15,
        scratch_shapes=scratch,
        compiler_params=pltpu.CompilerParams(
            collective_id=1, has_side_effects=True, vmem_limit_bytes=64 << 20
        ),
    )(*args)


def local(
    features, crop_side, upstream,
    entry_in, entry_group, entry_out, entry_down, entry_up, shortcut_weight,
    body_in, body_group, body_out, body_down, body_up,
    norm_gain, norm_shift, shortcut_gain, shortcut_shift,
):
    n_dp = lax.axis_size("dp")
    v = n_dp // MEMBERS
    groups = [[v * member + k for k in range(v)] for member in range(MEMBERS)]
    shards = (
        entry_in, entry_group, shortcut_weight, entry_down, entry_up, entry_out,
        body_in, body_group, body_down, body_up, body_out,
    )

    def lines(shard, count):
        if v > 1:
            shard = lax.all_gather(shard, "dp", axis_index_groups=groups, axis=0, tiled=True)
        return jnp.pad(shard, (0, 128 * count - shard.shape[0])).reshape(count, 128)

    results = main_call(
        n_dp, features, upstream, crop_side, jnp.asarray(lane_maps(), BF16),
        norm_gain.transpose(1, 0, 2), norm_shift.transpose(1, 0, 2), shortcut_gain[None],
        shortcut_shift[None],
        *(lines(shard, count) for shard, count in zip(shards, LINES)),
    )
    output, d_features = results[:2]

    def share(values, shard):
        values = values.reshape(-1)[: v * shard.shape[0]]
        if v > 1:
            values = lax.psum_scatter(
                values, "dp", scatter_dimension=0, axis_index_groups=groups, tiled=True
            )
        return values

    wa0, k0, ws, wd0, wu0, wc0, wa1, k1, wd1, wu1, wc1 = (
        share(values, shard) for values, shard in zip(results[2:13], shards)
    )
    gains, shifts, short_gain, short_shift = results[13:17]
    return (
        output, d_features, wa0, k0, wc0, wd0, wu0, ws, wa1, k1, wc1, wd1, wu1,
        gains.transpose(1, 0, 2), shifts.transpose(1, 0, 2),
        short_gain[0], short_shift[0],
    )


def solution(mesh):
    rows = P("dp", "section", None)
    flat = P(("section", "dp"))
    params = (P("section", None, None), P("section", None, None), P("section"), P("section"))
    return jax.shard_map(
        local,
        mesh=mesh,
        in_specs=(rows, P("dp"), rows) + (flat,) * 11 + params,
        out_specs=(rows, rows) + (flat,) * 11 + params,
        check_vma=False,
    )
```

```python
import functools

import jax
import jax.numpy as jnp
import numpy as np
from jax import lax
from jax.experimental import pallas as pl
from jax.experimental.pallas import tpu as pltpu
from jax.sharding import PartitionSpec as P

D = 896
DIN = 448
OUT = 14
IN = 28
SE0 = 112
SE1 = 224
EPSILON = 1e-05
F32 = jnp.float32
BF16 = jnp.bfloat16
MESH = pl.DeviceIdType.MESH
C = 1024
PX = 224
GUARD = 16
MEMBERS = 16
SHARDS = 32
ROWS = {
    "wa0": (0, 16), "k0": (16, 16), "ws": (32, 16), "misc0": (48, 16), "wc0": (64, 32),
    "k1": (96, 16), "wa1": (112, 32), "misc1": (144, 16), "wc1": (160, 32),
}
ORDER = ("wa0", "k0", "ws", "wd0", "wu0", "wc0", "k1", "wa1", "wd1", "wu1", "wc1")
LINES = (98, 112, 98, 28, 28, 196, 196, 112, 49, 49, 196)
GATHERS = ((0, 16), (16, 32), (32, 64), (64, 96), (96, 112), (112, 144), (144, 192))
SCATTERS = (
    (144, 192), (96, 112), (112, 144), (64, 96), (32, 64), (16, 32), (0, 16)
)
CHAINED = 5
GATHER_PLAN = {
    "own": ((0, 0), (1, 0), (2, 0)),
    "ph1": ((0, 1), (3, 0)),
    "need_wa0": ((0, 2), (1, 1), (0, 3), (2, 1), (4, 0), (5, 0), (0, 4), (1, 2)),
    "in0b": ((6, 0),),
    "in0": ((3, 1),),
    "in1a": ((2, 2),),
    "in1b": ((4, 1),),
    "in1": ((1, 3),),
    "need_k0": ((1, 4),),
    "bk0": ((3, 2),),
    "conv0a": ((5, 1),),
    "conv1a": ((2, 3),),
    "conv1": ((4, 2),),
    "need_ws": ((2, 4),),
    "str1": ((6, 1),),
    "need_wc0": ((3, 3), (3, 4), (5, 2)),
    "gate0": ((4, 3),),
    "gate1": ((6, 2),),
    "need_k1": ((4, 4),),
    "need_wa1": ((5, 3), (5, 4)),
    "bconv0": ((6, 3),),
    "need_wc1": ((6, 4),),
}
SCATTER_PLAN = {
    "small1": ((0, 0),),
    "bback0": ((0, 1),),
    "k1": ((1, 0),),
    "bin1a": ((0, 2), (1, 1)),
    "wa1": ((2, 0),),
    "eback0": ((0, 3),),
    "eback1a": ((1, 2), (2, 1)),
    "wc0": ((3, 0),),
    "small0": ((4, 0),),
    "econv0b": ((1, 3),),
    "econv0": ((0, 4), (2, 2), (3, 1)),
    "econv1b": ((1, 4),),
    "econv1": ((2, 3),),
    "k0": ((5, 0),),
    "wa0": ((5, 1), (3, 2), (4, 1), (6, 0)),
    "input0": ((3, 3),),
    "input1a": ((6, 1),),
    "emit0": ((2, 4),),
    "emit1a": ((5, 2),),
    "tail": (
        (4, 2), (6, 2), (5, 3), (3, 4), (4, 3), (6, 3), (5, 4), (4, 4), (6, 4),
    ),
}


def dot(a, b, dims):
    return lax.dot_general(a, b, ((dims[:1], dims[1:]), ((), ())), preferred_element_type=F32)


def nn(a, b):
    return dot(a, b, (1, 0))


def nt(a, b):
    return dot(a, b, (1, 1))


def tn(a, b):
    return dot(a, b, (0, 0))


def sig(z):
    return jnp.tanh(z * 0.5) * 0.5 + 0.5


def slope_of(z, s):
    return s * (1.0 + z * (1.0 - s))


def split_rows(rows):
    high = [r.astype(BF16).astype(F32) for r in rows]
    low = [r - h for r, h in zip(rows, high)]
    return high, low


def stacked(rows):
    pad = jnp.zeros((16 - len(rows), rows[0].shape[1]), F32)
    return jnp.concatenate(list(rows) + [pad], 0).astype(BF16)


def row_dot(row, weight, mul):
    high, low = split_rows([row])
    both = mul(stacked(high + low), weight)
    return both[0:1] + both[1:2]


def col(n, width=256):
    return pl.ds(pl.multiple_of(n * width, width), width)


def chunk(j, base=0):
    return pl.ds(pl.multiple_of(j * 16 + base, 16), 16)


def loop(count, body):
    def step(i, carry):
        body(i)
        return carry

    lax.fori_loop(0, count, step, 0)


def main_kernel(
    n_dp, features, upstream, side_ref, expand, gain_in, shift_in, short_in,
    l_wa0, l_k0, l_ws, l_wd0, l_wu0, l_wc0, l_wa1, l_k1, l_wd1, l_wu1, l_wc1,
    out, grad, result,
    inn, pool, u_buf, a0, a1, d_buf, ga, hid, dp_buf, x_buf, up_buf, fs, kd, e_buf,
    w, wd0, wu0, wd1, wu1, stage, params, pair, st, sv, cn, ng, ng_in, ar2, ar4, arh, arv,
    v_gain, v_shift, v_short, v_wa0, v_k0, v_ws, v_wd0, v_wu0, v_wc0, v_wa1, v_k1, v_wd1, v_wu1,
    v_wc1, isem, asend, arecv, vsend, vrecv, xsend, xrecv, lsem, gsend, grecv, rsend, rrecv, free,
):
    loads = [
        pltpu.make_async_copy(src, dst, isem.at[at])
        for at, (src, dst) in enumerate(
            (
                (l_wa0, v_wa0), (l_k0, v_k0), (l_ws, v_ws), (l_wd0, v_wd0), (l_wu0, v_wu0),
                (l_wc0, v_wc0), (l_wa1, v_wa1), (l_k1, v_k1), (l_wd1, v_wd1), (l_wu1, v_wu1),
                (l_wc1, v_wc1), (gain_in, v_gain), (shift_in, v_shift), (short_in, v_short),
            )
        )
    ]
    load_map = pltpu.make_async_copy(expand.at[1], e_buf, isem.at[14])
    for copy in loads + [load_map]:
        copy.start()
    section = lax.axis_index("section")
    me = lax.axis_index("dp")
    v = n_dp // MEMBERS
    digit, rest = me // v, lax.rem(me, v)
    other = 1 - section

    def member(hop):
        return lax.rem(digit + hop, MEMBERS) * v + rest

    def near(hop):
        return digit * v + lax.rem(rest + hop, v)

    barrier = pltpu.get_barrier_semaphore()

    def greet(hop):
        pl.semaphore_signal(barrier, inc=1, device_id=(section, member(hop + 1)), device_id_type=MESH)

    def greet_near(hop):
        pl.semaphore_signal(barrier, inc=1, device_id=(section, near(hop + 1)), device_id_type=MESH)

    loop(MEMBERS - 1, greet)
    if v > 1:
        loop(v - 1, greet_near)
    pl.semaphore_signal(barrier, inc=1, device_id=(other, me), device_id_type=MESH)
    def local_copy(src, dst, sem=0):
        return pltpu.make_async_copy(src, dst, lsem.at[sem])

    def to_sibling(src, dst, at):
        return pltpu.make_async_remote_copy(
            src_ref=src, dst_ref=dst, send_sem=xsend.at[at], recv_sem=xrecv.at[at],
            device_id=(other, me), device_id_type=MESH,
        )

    mine = pl.ds(2 * section, 2)
    theirs = pl.ds(2 * other, 2)
    copies = [
        local_copy(features.at[mine], x_buf.at[section], 0),
        local_copy(upstream.at[mine], up_buf.at[section], 1),
    ]
    for copy in copies:
        copy.start()

    def dp_of(c):
        return dp_buf[c, GUARD : GUARD + PX]

    def half_side(c):
        return side_ref[2 * section + c] // 2

    def keep(c, j):
        half = half_side(c)
        bound = jnp.where(j < half, half, 0)
        tile = (lax.broadcasted_iota(jnp.int32, (16, 128), 0) < bound).astype(F32)
        return jnp.concatenate([tile] * (C // 128), 1)

    def crop_count(c):
        half = half_side(c)
        return (half * half).astype(F32)

    def ar_slots(n, c):
        if n >= 6:
            return arh.at[n % 2, c, :, pl.ds(0, 32 if n == 9 else 16)]
        return ar4.at[c] if n == 2 else ar2.at[n % 2, c]

    def ar_start(n, c, rows):
        slots = ar_slots(n, c)
        if n >= 6:
            tiles = [row[:, 128 * k : 128 * k + 128] for row in rows for k in range(8)]
            if n == 9:
                tiles.append(jnp.zeros((8, 128), F32))
            slots[digit] = jnp.concatenate(tiles, 0).astype(BF16)
        else:
            slots[digit] = jnp.concatenate(rows, 0)

        def send(hop):
            pltpu.make_async_remote_copy(
                src_ref=slots.at[digit], dst_ref=slots.at[digit], send_sem=asend.at[n % 2, c],
                recv_sem=arecv.at[n % 2, c], device_id=(section, member(hop + 1)),
                device_id_type=MESH,
            ).start()

        loop(MEMBERS - 1, send)

    def ar_wait(n, c, rows):
        slots = ar_slots(n, c)
        arrived = slots.at[pl.ds(0, MEMBERS - 1)]
        pltpu.make_async_copy(arrived, arrived, asend.at[n % 2, c]).wait()
        pltpu.make_async_copy(arrived, arrived, arecv.at[n % 2, c]).wait()
        total = slots[0].astype(F32)
        for k in range(1, MEMBERS):
            total = total + slots[k].astype(F32)
        if n >= 6:
            total = jnp.concatenate(
                [
                    jnp.concatenate([total[8 * r + k : 8 * r + k + 1] for k in range(8)], 1)
                    for r in range(rows)
                ],
                0,
            )
        if v > 1:
            again = arv.at[n % 2, c]
            spare = [jnp.zeros((4 - rows, C), F32)] if rows < 4 else []
            again[rest] = jnp.concatenate([total] + spare, 0)

            def send(hop):
                pltpu.make_async_remote_copy(
                    src_ref=again.at[rest], dst_ref=again.at[rest], send_sem=vsend.at[n % 2, c],
                    recv_sem=vrecv.at[n % 2, c], device_id=(section, near(hop + 1)),
                    device_id_type=MESH,
                ).start()

            loop(v - 1, send)
            arrived = again.at[pl.ds(0, v - 1)]
            pltpu.make_async_copy(arrived, arrived, vsend.at[n % 2, c]).wait()
            pltpu.make_async_copy(arrived, arrived, vrecv.at[n % 2, c]).wait()
            total = again[0]
            for k in range(1, v):
                total = total + again[k]
        return [total[k : k + 1] for k in range(rows)]

    def down(sums):
        return jnp.sum(sums, axis=0, keepdims=True)

    def fold(value):
        return value[0:8] + value[8:16]

    def zeros(count):
        return tuple(jnp.zeros((8, C), F32) for _ in range(count))

    def each_column(count, body):
        sums = lax.fori_loop(0, 14, body, zeros(count))
        return [down(one) for one in sums]

    def moment_sums(c, value_of):
        def body(j, sums):
            value = value_of(j)
            weighted = value * keep(c, j)
            return (sums[0] + fold(weighted), sums[1] + fold(weighted * value))

        return each_column(2, body)

    def set_stats(c, index, totals, inverse, gain_row):
        center = totals[0] * inverse
        scaling = lax.rsqrt(totals[1] * inverse - center * center + EPSILON)
        gain = params[gain_row : gain_row + 1] * scaling
        shift_row = gain_row + 6 if gain_row < 6 else gain_row + 1
        st[c, index, 0:1] = center
        st[c, index, 1:2] = scaling
        st[c, index, 2:3] = gain
        st[c, index, 3:4] = params[shift_row : shift_row + 1] - center * gain

    def affine(c, index):
        return st[c, index, 2:3], st[c, index, 3:4]

    def hat_of(c, index):
        return st[c, index, 0:1], st[c, index, 1:2]

    def inverse_out(c):
        return cn[c, 1:2]

    def inverse_in(c):
        return cn[c, 2:3]

    def place(shard):
        return shard // 16, lax.rem(shard // 4, 4), lax.rem(shard, 4)

    def cols_of(name, lanes):
        at, count = ROWS[name]
        value = w[:, :, :, at : at + count, lanes]
        return value.reshape(SHARDS * count, value.shape[-1])

    def rows_index(name, n):
        at, count = ROWS[name]
        if count == 16:
            return (n, slice(None), slice(None), slice(at, at + 16))
        return (n // 2, pl.ds(2 * lax.rem(n, 2), 2), slice(None), slice(at, at + 32))

    def rows_of(name, n):
        return w[rows_index(name, n)].reshape(256, C)

    def put_rows(name, n, value):
        shape = (4, 4, 16, C) if ROWS[name][1] == 16 else (2, 4, 32, C)
        w[rows_index(name, n)] = value.astype(BF16).reshape(shape)

    def shard_rows(name, shard):
        at, count = ROWS[name]
        return w[(*place(shard), slice(at, at + count))].astype(F32)

    def put_shard(name, shard, value):
        at, count = ROWS[name]
        w[(*place(shard), slice(at, at + count))] = value.astype(BF16)

    def tile(k):
        return slice(128 * k, 128 * k + 128)

    def build_conv(name):
        def shard(s):
            rows = shard_rows(name, s)
            for a in range(4):
                for k in range(2):
                    fs[pl.ds(2048 * k + 63 * s + a, 16, stride=4)] = rows[:, tile(2 * a + k)]

        loop(SHARDS, shard)
        lane = lax.broadcasted_iota(jnp.int32, (64, 256), 1) // 64

        def block(a):
            for tap in range(9):
                tiles = []
                for k in range(2):
                    at = 2048 * k + 224 * tap
                    tiles.append(
                        jnp.concatenate(
                            [
                                fs[pl.ds(at + a, 28, stride=4)],
                                jnp.zeros((4, 128), F32),
                                fs[pl.ds(at + 112 + a, 28, stride=4)],
                                jnp.zeros((4, 128), F32),
                            ],
                            0,
                        )
                    )
                dense = jnp.concatenate(tiles, 1)
                for g in range(4):
                    kd[a, 256 * tap + 64 * g : 256 * tap + 64 * g + 64] = jnp.where(
                        lane == g, dense, 0.0
                    ).astype(BF16)

        loop(4, block)

    def build_small(b):
        wd, wu = (wd0, wu0) if b == 0 else (wd1, wu1)
        fs[...] = jnp.zeros_like(fs)

        def shard(s):
            rows = shard_rows("misc0" if b == 0 else "misc1", s)
            if b == 0:
                for k in range(8):
                    fs[pl.ds(32 * s + k, 4, stride=8)] = rows[0:4, tile(k)]
                    fs[pl.ds(1024 + 256 * (k % 4) + 7 * s + k // 4, 4, stride=2)] = rows[
                        8:12, tile(k)
                    ]
            else:
                for k in range(8):
                    fs[pl.ds(1024 * (k % 2) + 32 * s + k // 2, 7, stride=4)] = rows[0:7, tile(k)]
                    fs[pl.ds(2048 + 256 * k + 7 * s, 7)] = rows[8:15, tile(k)]

        loop(SHARDS, shard)
        for k in range(1 + b):
            wd[:, tile(k)] = fs[1024 * k : 1024 * k + 1024].astype(BF16)
        gap = jnp.zeros((4, 128), F32)
        for g in range(4 + 4 * b):
            for k in range(8):
                if b == 0:
                    start = 1024 + 256 * (k % 4) + 56 * g + k // 4
                    part = fs[pl.ds(start, 28, stride=2)]
                else:
                    start = 2048 + 256 * k + 28 * g
                    part = fs[start : start + 28]
                wu[32 * g : 32 * g + 32, tile(k)] = jnp.concatenate([part, gap], 0).astype(BF16)

    def taps0():
        for a in range(3):
            for b in range(3):
                yield a * 3 + b, (0 if a == 1 else 1), (0 if b == 1 else 1), a, b

    def both(ref_of):
        return jnp.concatenate([ref_of(0), ref_of(1)], 0)

    def squeeze(c, b, pooled, wd, wu):
        width = wd.shape[1]
        raw = row_dot(pooled, wd[...], nn)
        squeezed = raw * sig(raw)
        gating = sig(row_dot(squeezed, wu[...], nn))
        sv[b, c, 0:1] = pooled
        sv[b, c, 1:2, 0:width] = raw
        sv[b, c, 2:3, 0:width] = squeezed
        sv[b, c, 3:4] = gating
        return gating

    def gate(c, b, index, conv_k, wd, wu, name, proj_k):
        a, shift = affine(c, index)

        def pool_chunk(j, sums):
            z = pool[c, conv_k, chunk(j)] * a + shift
            excited = keep(c, j) * (z * sig(z))
            pool[c, 7, chunk(j)] = excited
            return (sums[0] + fold(excited),)

        pooled = each_column(1, pool_chunk)[0] / crop_count(c)
        gating = squeeze(c, b, pooled, wd, wu)

        def gate_chunk(j):
            ga[b, c, chunk(j)] = (pool[c, 7, chunk(j)] * gating).astype(BF16)

        loop(14, gate_chunk)

        def project(n):
            pool[c, proj_k, :, col(n)] = nn(ga[b, c], cols_of(name, col(n)))

        loop(4, project)
        return moment_sums(c, lambda j: pool[c, proj_k, chunk(j)])

    def ungate(c, b, index, conv_k, wd, wu, name):
        width = wd.shape[1]

        def back(n):
            pool[c, 7, :, col(n)] = nt(dp_of(c), rows_of(name, n))

        loop(4, back)
        a, shift = affine(c, index)

        def gate_chunk(j, sums):
            z = pool[c, conv_k, chunk(j)] * a + shift
            excited = keep(c, j) * (z * sig(z))
            return (sums[0] + fold(pool[c, 7, chunk(j)] * excited),)

        d_gate = each_column(1, gate_chunk)[0]
        poll_crop(c, ("eback" if b == 0 else "bout", "a"))
        gating = sv[b, c, 3:4]
        d_raw = d_gate * gating * (1.0 - gating)
        raw = sv[b, c, 1:2, 0:width]
        d_squeeze = row_dot(d_raw, wu[...], nt) * slope_of(raw, sig(raw))
        d_pool = row_dot(d_squeeze, wd[...], nt) / crop_count(c)
        sv[b, c, 4:5] = d_raw
        sv[b, c, 5:6, 0:width] = d_squeeze
        center, scaling = hat_of(c, index)

        def slope_chunk(j, sums):
            value = pool[c, conv_k, chunk(j)]
            z = value * a + shift
            d = (pool[c, 7, chunk(j)] * gating + d_pool) * (keep(c, j) * slope_of(z, sig(z)))
            pool[c, 7, chunk(j)] = d
            return (sums[0] + fold(d), sums[1] + fold(d * ((value - center) * scaling)))

        return each_column(2, slope_chunk)

    def small_grads(b):
        width = 128 + 128 * b

        def pairs(x_row, x_width, y_row, y_width):
            xs, ys = [], []
            for c in range(2):
                xh, xl = split_rows([sv[b, c, x_row : x_row + 1, 0:x_width]])
                yh, yl = split_rows([sv[b, c, y_row : y_row + 1, 0:y_width]])
                xs += [xh[0], xh[0], xl[0]]
                ys += [yh[0], yl[0], yh[0]]
            return tn(stacked(xs), stacked(ys))

        grad_down = pairs(0, C, 5, width)
        for k in range(1 + b):
            fs[1024 * k : 1024 * k + 1024] = grad_down[:, tile(k)]
        grad_up = pairs(2, width, 4, C)
        for g in range(4 + 4 * b):
            for k in range(8):
                part = grad_up[32 * g : 32 * g + 28, tile(k)]
                if b == 0:
                    fs[pl.ds(1024 + 256 * (k % 4) + 56 * g + k // 4, 28, stride=2)] = part
                else:
                    fs[2048 + 256 * k + 28 * g : 2048 + 256 * k + 28 * g + 28] = part

        def shard(s):
            tiles = []
            for k in range(8):
                if b == 0:
                    count = 4
                    first = fs[pl.ds(32 * s + k, 4, stride=8)]
                    second = fs[pl.ds(1024 + 256 * (k % 4) + 7 * s + k // 4, 4, stride=2)]
                else:
                    count = 7
                    first = fs[pl.ds(1024 * (k % 2) + 32 * s + k // 2, 7, stride=4)]
                    second = fs[pl.ds(2048 + 256 * k + 7 * s, 7)]
                gap = jnp.zeros((8 - count, 128), F32)
                tiles.append(jnp.concatenate([first, gap, second, gap], 0))
            put_shard("misc0" if b == 0 else "misc1", s, jnp.concatenate(tiles, 1))

        loop(SHARDS, shard)

    def norm_coefficients(c, index, totals, inverse, gain_row, kind):
        center, scaling = hat_of(c, index)
        ng[gain_row : gain_row + 1] += totals[1]
        shift_row = gain_row + 6 if gain_row < 6 else gain_row + 1
        ng[shift_row : shift_row + 1] += totals[0]
        a = st[c, index, 2:3]
        slope = -a * scaling * (totals[1] * inverse)
        offset = -a * (totals[0] * inverse) - slope * center
        return a, slope, offset

    def conv_grad(act_of, v_of, name):
        lane = lax.broadcasted_iota(jnp.int32, (64, 256), 1) // 64

        def block(a):
            for tap in range(9):
                dense = tn(
                    both(lambda c: act_of(c, tap, col(a))), both(lambda c: v_of(c, tap, col(a)))
                )
                own = jnp.where(lane == 0, dense[0:64], 0.0)
                for g in range(1, 4):
                    own = own + jnp.where(lane == g, dense[64 * g : 64 * g + 64], 0.0)
                for k in range(2):
                    at = 2048 * k + 224 * tap
                    fs[pl.ds(at + a, 28, stride=4)] = own[0:28, 128 * k : 128 * k + 128]
                    fs[pl.ds(at + 112 + a, 28, stride=4)] = own[32:60, 128 * k : 128 * k + 128]

        loop(4, block)

        def shard(s):
            tiles = [
                fs[pl.ds(2048 * k + 63 * s + a, 16, stride=4)] for a in range(4) for k in range(2)
            ]
            put_shard(name, s, jnp.concatenate(tiles, 1))

        loop(SHARDS, shard)

    def outer(left_of, right_of, name):
        def block(m):
            put_rows(name, m, tn(both(lambda c: left_of(c, col(m))), both(right_of)))

        loop(SHARDS * ROWS[name][1] // 256, block)

    z, yx = digit // 4, lax.rem(digit, 4)
    bits = (1 + section, 2 - section)

    def flip(bit):
        return yx + bit * (1 - 2 * lax.rem(yx // bit, 2))

    def push(src, dst, to, sends, recvs):
        pltpu.make_async_remote_copy(
            src_ref=src, dst_ref=dst, send_sem=sends, recv_sem=recvs,
            device_id=(section, to * v + rest), device_id_type=MESH,
        ).start()

    def push_sibling(src, dst, sends, recvs):
        pltpu.make_async_remote_copy(
            src_ref=src, dst_ref=dst, send_sem=sends, recv_sem=recvs,
            device_id=(other, me), device_id_type=MESH,
        ).start()

    def arrive(ref, sem):
        pltpu.make_async_copy(ref, ref, sem).wait()

    def gather(k, phase):
        start, stop = GATHERS[k]
        rows = pl.ds(start, stop - start)
        sent = w.at[section, :, :, rows]
        if phase > 0:
            sem = grecv.at[k, phase - 1]
            if phase == 1:
                arrive(w.at[section, pl.ds(0, 3), 0, rows], sem)
            elif phase == 2:
                arrive(sent.at[:, 0], sem)
            elif phase == 3:
                arrive(sent.at[:, pl.ds(0, 2)], sem)
            else:
                arrive(sent, sem)
        if phase == 4:
            arrive(w.at[section, pl.ds(0, 3), 0, rows], gsend.at[k, 0])
            arrive(sent.at[:, 0], gsend.at[k, 1])
            arrive(sent.at[:, pl.ds(0, 2)], gsend.at[k, 2])
            arrive(sent, gsend.at[k, 3])
            return
        sems = (gsend.at[k, phase], grecv.at[k, phase])
        if phase == 0:
            own = w.at[section, z, yx, rows]
            for hop in range(1, 4):
                push(own, own, lax.rem(z + hop, 4) * 4 + yx, *sems)
        elif phase == 1:
            push(sent.at[:, yx], sent.at[:, yx], z * 4 + flip(bits[0]), *sems)
        elif phase == 2:
            for at in (yx, flip(bits[0])):
                push(sent.at[:, at], sent.at[:, at], z * 4 + flip(bits[1]), *sems)
        else:
            push_sibling(sent, sent, *sems)

    def poll(point):
        for k, phase in GATHER_PLAN.get(point, ()):
            gather(k, phase)
        for k, phase in SCATTER_PLAN.get(point, ()):
            scatter(k, phase)

    def poll_crop(c, point):
        for one in range(2):
            name = point[0] + str(one) + point[1]
            if name in GATHER_PLAN or name in SCATTER_PLAN:
                pl.when(c == one)(lambda: poll(name))

    def crops(body, point=None):
        def run(c):
            body(c)
            if point is not None:
                poll_crop(c, (point, ""))

        loop(2, run)

    def landing(k, phase, block, count):
        last = k - CHAINED
        if phase == 0:
            if k < 4:
                return e_buf.at[pl.ds(pl.multiple_of(block * count, 16), count)]
            ref = a1 if k == 4 else hid if last == 0 else ga.at[0]
            return ref.at[
                block // 8, pl.ds(pl.multiple_of(lax.rem(block, 8) * count, 16), count)
            ]
        if phase == 1:
            if last < 0:
                return ga.at[1, block // 4, pl.ds(block % 4 * count, count)]
            ref = hid if last == 0 else ga.at[0]
            return ref.at[block // 4, pl.ds(128 + block % 4 * 16, 16)]
        if phase == 2:
            if last < 0:
                return wu1.at[pl.ds(block * count, count)]
            ref = ga.at[0] if last == 0 else hid
            return ref.at[block // 2, pl.ds(192 + block % 2 * 16, 16)]
        if last >= 0:
            return wu0.at[pl.ds(64 * last + 16 * block, 16)]
        if k % 2:
            return wu1.at[pl.ds(160 + block * count, count)]
        return stage.at[block, pl.ds(0, count)]

    def landed(k, phase, count):
        return w.at[section, pl.ds(0, (4, 2, 1, 1)[phase]), pl.ds(0, (4, 4, 4, 3)[phase]), pl.ds(0, count)]

    def add_landed(k, phase, block, place_of, start, count):
        ref = landing(k, phase, block, count)
        index = (section, *place_of(block), pl.ds(start, count))
        w[index] = (w[index].astype(F32) + ref[...].astype(F32)).astype(BF16)

    def credit(at, to):
        pl.semaphore_signal(
            free.at[at], inc=1, device_id=(section, to * v + rest), device_id_type=MESH
        )

    def credit_sibling(at):
        pl.semaphore_signal(free.at[at], inc=1, device_id=(other, me), device_id_type=MESH)

    def credit_z(at):
        for hop in range(1, 4):
            credit(at, lax.rem(z + hop, 4) * 4 + yx)

    def scatter(k, phase):
        start, stop = SCATTERS[k]
        count = stop - start
        rows = pl.ds(start, count)
        first, second = flip(bits[1]), flip(bits[0])
        more = k + 1 < CHAINED
        if phase > 0:
            arrive(landed(k, phase - 1, count), rrecv.at[k, phase - 1])
        if phase == 1:
            loop(16, lambda b: add_landed(k, 0, b, lambda b: (b // 4, lax.rem(b, 4)), start, count))
            if k < 3:
                credit_sibling(0)
        elif phase == 2:
            for b in range(8):
                add_landed(k, 1, b, lambda b: (b // 2, yx if b % 2 == 0 else second), start, count)
            if more:
                credit(1, z * 4 + first)
        elif phase == 3:
            for b in range(4):
                add_landed(k, 2, b, lambda b: (b, yx), start, count)
            if more:
                credit(2, z * 4 + second)
            if k == 0:
                credit_z(5)
        elif phase == 4:
            total = w[section, z, yx, start:stop].astype(F32)
            for b in range(3):
                total = total + landing(k, 3, b, count)[...].astype(F32)
            pool[0, 1, start:stop] = total
            if k + 2 < CHAINED:
                credit_z(5 if k % 2 else 3)
            for sent in range(4):
                arrive(landed(k, sent, count), rsend.at[k, sent])
            return
        sems = (rsend.at[k, phase], rrecv.at[k, phase])
        if phase == 0:
            if k < 4 or k == CHAINED:
                pl.semaphore_wait(free.at[0 if k < 4 else 4], 1)

            def send(b):
                push_sibling(
                    w.at[other, b // 4, lax.rem(b, 4), rows], landing(k, 0, b, count), *sems
                )

            loop(16, send)
        elif phase == 1:
            if k < CHAINED:
                pl.semaphore_wait(free.at[1], 1)
            for b in range(8):
                to = first if b % 2 == 0 else first + second - yx
                push(
                    w.at[section, b // 2, to, rows], landing(k, 1, b, count), z * 4 + first, *sems
                )
        elif phase == 2:
            if k < CHAINED:
                pl.semaphore_wait(free.at[2], 1)
            for b in range(4):
                push(
                    w.at[section, b, second, rows], landing(k, 2, b, count), z * 4 + second, *sems
                )
        else:
            if k < CHAINED:
                pl.semaphore_wait(free.at[5 if k % 2 else 3], 3)
            for hop in range(1, 4):
                to = lax.rem(z + hop, 4)
                push(w.at[section, to, yx, rows], landing(k, 3, hop - 1, count), to * 4 + yx, *sems)

    for copy in loads:
        copy.wait()
    shares = {}
    at = 0
    for name, ref, count in (
        ("wa0", v_wa0, 14), ("k0", v_k0, 16), ("ws", v_ws, 14), ("wd0", v_wd0, 4),
        ("wu0", v_wu0, 4), ("wc0", v_wc0, 28), ("wa1", v_wa1, 28), ("k1", v_k1, 16),
        ("wd1", v_wd1, 7), ("wu1", v_wu1, 7), ("wc1", v_wc1, 28),
    ):
        fs[at : at + ref.shape[0]] = ref[...].astype(F32)
        value = jnp.concatenate([fs[pl.ds(at + k, count, stride=7)] for k in range(7)], 1)
        room = 8 if count < 8 else count + -count % 16
        if room > count:
            value = jnp.concatenate([value, jnp.zeros((room - count, D), F32)], 0)
        shares[name] = value
        at += ref.shape[0] + -ref.shape[0] % 8
    load_map.wait()
    own_rows = jnp.concatenate([shares[name] for name in ORDER], 0).astype(BF16)
    for n in range(4):
        lanes = slice(256 * n, 256 * n + 256)
        w[section, z, yx, :, lanes] = nn(own_rows, e_buf[:, lanes]).astype(BF16)
    pl.semaphore_wait(barrier, MEMBERS + v - 1)
    poll("own")
    exchange = [
        to_sibling(upstream.at[theirs], up_buf.at[section], 1),
        to_sibling(features.at[theirs], x_buf.at[section], 0),
    ]
    for copy in exchange:
        copy.start()
    copies = exchange + copies
    ng[...] = jnp.zeros_like(ng)
    guard = jnp.zeros((GUARD, C), BF16)
    for ref, count in ((a0, 4), (d_buf, 2)):
        for c in range(2):
            for k in range(count):
                ref[c, k, 0:GUARD] = guard
                ref[c, k, GUARD + PX :] = guard
    for c in range(2):
        for ref in (a1, dp_buf):
            ref[c, 0:GUARD] = guard
            ref[c, GUARD + PX :] = guard

    short = v_short[...].astype(F32)
    halves = jnp.concatenate([short[k : k + 1] for k in range(7)], 1)
    pair[section] = jnp.concatenate(
        [v_gain[k] for k in range(3)] + [v_shift[k] for k in range(3)]
        + [halves, jnp.zeros((1, D), F32)],
        0,
    )
    swap = to_sibling(pair.at[section], pair.at[section], 3)
    swap.start()
    swap.wait()
    first, second = pair[0], pair[1]
    short_gain_row = jnp.concatenate([first[6:7, 0:DIN], second[6:7, 0:DIN]], 1)
    short_shift_row = jnp.concatenate([first[6:7, DIN:], second[6:7, DIN:]], 1)
    rows = jnp.concatenate(
        [
            first[0:3], second[0:3], first[3:6], second[3:6], short_gain_row, short_shift_row,
            jnp.zeros((2, D), F32),
        ],
        0,
    )

    wide = nn(thirds(rows), e_buf[...])
    params[...] = wide[0:16] + wide[16:32] + wide[32:48]
    poll("params")

    for copy in copies:
        copy.wait()

    def gather_slices(ref, rows):
        pad = jnp.zeros((16 - rows, D), BF16)
        return jnp.concatenate(
            [jnp.concatenate([ref[:, D * j : D * j + D], pad], 0) for j in range(OUT)], 0
        )

    def cotangent(c):
        for h in range(2):
            x = gather_slices(up_buf.at[h, c], 7)
            for n in range(4):
                y = nn(x, e_buf[:, 256 * n : 256 * n + 256])
                for j in range(OUT):
                    count = 16 if h == 0 else 7
                    pool[c, 3, 16 * j + 7 * h : 16 * j + 7 * h + count, 256 * n : 256 * n + 256] = y[
                        16 * j : 16 * j + count
                    ]

    crops(cotangent, "cot")
    load_map = local_copy(expand.at[0], e_buf, 2)
    load_map.start()
    fs[...] = jnp.zeros_like(fs)
    load_map.wait()

    def phases(c):
        for h in range(2):
            x = gather_slices(x_buf.at[h, c], 14)
            for n in range(4):
                y = nn(x, e_buf[:, 256 * n : 256 * n + 256])
                for j in range(OUT):
                    for k in range(2):
                        fs[pl.ds(512 * (2 * n + k) + 32 * j + 14 * h, 14)] = y[
                            16 * j : 16 * j + 14, 128 * k : 128 * k + 128
                        ]
        for q in range(2):
            def take(j):
                for k in range(8):
                    u_buf[c, q, chunk(j), 128 * k : 128 * k + 128] = fs[
                        pl.ds(512 * k + 32 * j + q, 16, stride=2)
                    ].astype(BF16)

            loop(14, take)

    crops(phases, "ph")
    load_map = local_copy(expand.at[1], e_buf, 2)
    load_map.start()
    poll("need_wa0")

    def entry_inner(c):
        for q in range(2):
            for r in range(2):
                def product(n):
                    inn[c, 2 * q + r, :, col(n)] = nn(
                        u_buf[c, q, :, 512 * r : 512 * r + 512], cols_of("wa0", col(n))
                    )

                loop(4, product)
            poll_crop(c, ("in", "ab"[q]))

        def body(j, sums):
            mask = keep(c, j)
            first, second = sums
            for k in range(4):
                value = inn[c, k, chunk(j)]
                weighted = value * mask
                first = first + fold(weighted)
                second = second + fold(weighted * value)
            return (first, second)

        sums = each_column(2, body)
        spare = lax.broadcasted_iota(jnp.int32, (1, C), 1) == 28
        ar_start(0, c, [jnp.where(spare, crop_count(c), sums[0]), sums[1]])

    crops(entry_inner, "in")
    poll("need_k0")
    build_conv("k0")
    poll("bk0")

    def entry_conv(c):
        totals = ar_wait(0, c, 2)
        count = jnp.zeros((1, C), F32) + totals[0][:, 28:29]
        cn[c, 0:1] = count
        cn[c, 1:2] = 1.0 / count
        cn[c, 2:3] = 0.25 / count
        spare = lax.broadcasted_iota(jnp.int32, (1, C), 1) == 28
        totals[0] = jnp.where(spare, 0.0, totals[0])
        set_stats(c, 0, totals, inverse_in(c), 0)
        a, shift = affine(c, 0)

        def activate(j):
            mask = keep(c, j)
            for q in range(2):
                for r in range(2):
                    z = inn[c, 2 * q + r, chunk(j)] * a + shift
                    act = mask * (z * sig(z))
                    a0[c, 2 * q + r, chunk(j, GUARD)] = act.astype(BF16)
                    if q == 1:
                        d_buf[c, r, chunk(j, GUARD)] = pltpu.roll(act, 1, 0).astype(BF16)

        loop(14, activate)

        poll_crop(c, ("conv", "a"))

        def convolve(n):
            patches = []
            for tap, q, r, ta, tb in taps0():
                at = GUARD - 16 if tb == 0 else GUARD
                src = d_buf.at[c, r] if ta == 0 else a0.at[c, 2 * q + r]
                patches.append(src[at : at + PX, col(n)])
            pool[c, 0, :, col(n)] = nn(jnp.concatenate(patches, 1), kd[n])

        loop(4, convolve)
        ar_start(1, c, moment_sums(c, lambda j: pool[c, 0, chunk(j)]))

    crops(entry_conv, "conv")
    poll("need_ws")

    def strided(c):
        def product(n):
            pool[c, 2, :, col(n)] = nn(u_buf[c, 0, :, 0:512], cols_of("ws", col(n)))

        loop(4, product)

    crops(strided, "str")
    build_small(0)
    poll("need_wc0")

    def entry_gate(c):
        totals = ar_wait(1, c, 2)
        set_stats(c, 1, totals, inverse_out(c), 1)
        sums = gate(c, 0, 1, 0, wd0, wu0, "wc0", 1)
        ar_start(2, c, sums + moment_sums(c, lambda j: pool[c, 2, chunk(j)]))

    crops(entry_gate, "gate")
    poll("need_k1")
    build_conv("k1")
    poll("need_wa1")

    def entry_pre(c, j):
        a, shift = affine(c, 2)
        short_a, short_shift = affine(c, 3)
        return (
            pool[c, 1, chunk(j)] * a + pool[c, 2, chunk(j)] * short_a + (shift + short_shift)
        )

    def entry_out(c):
        totals = ar_wait(2, c, 4)
        set_stats(c, 2, totals[0:2], inverse_out(c), 2)
        set_stats(c, 3, totals[2:4], inverse_out(c), 12)

        def finish(j):
            z = entry_pre(c, j)
            hid[c, chunk(j)] = (keep(c, j) * (z * sig(z))).astype(BF16)

        loop(14, finish)

        def product(n):
            pool[c, 4, :, col(n)] = nn(hid[c], cols_of("wa1", col(n)))

        loop(4, product)
        ar_start(3, c, moment_sums(c, lambda j: pool[c, 4, chunk(j)]))

    crops(entry_out, "out")

    def body_conv(c):
        set_stats(c, 4, ar_wait(3, c, 2), inverse_out(c), 3)
        a, shift = affine(c, 4)

        def activate(j):
            z = pool[c, 4, chunk(j)] * a + shift
            act = keep(c, j) * (z * sig(z))
            a1[c, chunk(j, GUARD)] = act.astype(BF16)
            d_buf[c, 0, chunk(j, GUARD)] = pltpu.roll(act, 1, 0).astype(BF16)
            d_buf[c, 1, chunk(j, GUARD)] = pltpu.roll(act, 15, 0).astype(BF16)

        loop(14, activate)

        def convolve(n):
            rows = (d_buf.at[c, 0], a1.at[c], d_buf.at[c, 1])
            patches = [
                rows[ta][16 * tb : 16 * tb + PX, col(n)] for ta in range(3) for tb in range(3)
            ]
            pool[c, 5, :, col(n)] = nn(jnp.concatenate(patches, 1), kd[n])

        loop(4, convolve)
        ar_start(4, c, moment_sums(c, lambda j: pool[c, 5, chunk(j)]))

    crops(body_conv, "bconv")
    poll("need_wc1")
    build_small(1)

    def body_gate(c):
        set_stats(c, 5, ar_wait(4, c, 2), inverse_out(c), 4)
        ar_start(5, c, gate(c, 1, 5, 5, wd1, wu1, "wc1", 6))

    loop(2, body_gate)

    def body_out(c):
        set_stats(c, 6, ar_wait(5, c, 2), inverse_out(c), 5)
        a, shift = affine(c, 6)
        center, scaling = hat_of(c, 6)

        def finish(j, sums):
            value = pool[c, 6, chunk(j)]
            z = value * a + shift + hid[c, chunk(j)].astype(F32)
            mask = keep(c, j)
            s = sig(z)
            dp_buf[c, chunk(j, GUARD)] = (mask * (z * s)).astype(BF16)
            d_pre = pool[c, 3, chunk(j)] * (mask * slope_of(z, s))
            pool[c, 3, chunk(j)] = d_pre
            return (sums[0] + fold(d_pre), sums[1] + fold(d_pre * ((value - center) * scaling)))

        ar_start(6, c, each_column(2, finish))

    loop(2, body_out)
    load_map.wait()

    def narrow(value, store):
        for start, width in ((0, 256), (256, 256), (512, 256), (768, 128)):
            store(start, width, nt(value, e_buf[start : start + width]))

    def body_emit(c):
        def store(start, width, y):
            for j in range(OUT):
                for h in range(2):
                    up_buf[h, c, :, D * j + start : D * j + start + width] = y[
                        16 * j + 7 * h : 16 * j + 7 * h + 7
                    ].astype(BF16)

        narrow(dp_of(c), store)

    loop(2, body_emit)
    out_copies = [
        to_sibling(up_buf.at[other], out.at[mine], 2),
        local_copy(up_buf.at[section], out.at[mine], 1),
    ]
    for copy in out_copies:
        copy.start()

    credit_sibling(0)

    def body_back_out(c):
        a, slope, offset = norm_coefficients(c, 6, ar_wait(6, c, 2), inverse_out(c), 5, 0)

        def project(j):
            value = pool[c, 6, chunk(j)]
            dp_buf[c, chunk(j, GUARD)] = (
                keep(c, j) * (a * pool[c, 3, chunk(j)] + slope * value + offset)
            ).astype(BF16)

        loop(14, project)
        ar_start(7, c, ungate(c, 1, 5, 5, wd1, wu1, "wc1"))

    crops(body_back_out, "bout")
    credit(2, z * 4 + flip(bits[0]))
    credit_z(3)
    outer(lambda c, l: ga[1, c, :, l], dp_of, "wc1")
    credit(1, z * 4 + flip(bits[1]))
    small_grads(1)
    poll("small1")

    def conv_cotangent(c, index, conv_k, a, slope, offset, versions):
        def body(j):
            d = keep(c, j) * (a * pool[c, 7, chunk(j)] + slope * pool[c, conv_k, chunk(j)] + offset)
            d_buf[c, 0, chunk(j, GUARD)] = d.astype(BF16)
            d_buf[c, 1, chunk(j, GUARD)] = pltpu.roll(d, 15, 0).astype(BF16)
            if versions == 3:
                dp_buf[c, chunk(j, GUARD)] = pltpu.roll(d, 1, 0).astype(BF16)

        loop(14, body)

    def v_body(c, tap, lanes):
        ta, tb = tap // 3, tap % 3
        ref = (d_buf.at[c, 1], d_buf.at[c, 0], dp_buf.at[c])[ta]
        return ref[32 - 16 * tb : 32 - 16 * tb + PX, lanes]

    def v_entry(c, tap, lanes):
        ta, tb = tap // 3, tap % 3
        at = 32 if tb == 0 else 16
        return d_buf[c, 1 if ta == 0 else 0, at : at + PX, lanes]

    def body_back_conv(c):
        a, slope, offset = norm_coefficients(c, 5, ar_wait(7, c, 2), inverse_out(c), 4, 0)
        conv_cotangent(c, 5, 5, a, slope, offset, 3)

        def back(n):
            total = nt(v_body(c, 0, col(n)), kd[n, 0:256])
            for tap in range(1, 9):
                total = total + nt(v_body(c, tap, col(n)), kd[n, 256 * tap : 256 * tap + 256])
            pool[c, 7, :, col(n)] = total

        loop(4, back)
        poll_crop(c, ("bback", "a"))
        a, shift = affine(c, 4)
        center, scaling = hat_of(c, 4)

        def body(j, sums):
            value = pool[c, 4, chunk(j)]
            z = value * a + shift
            d = pool[c, 7, chunk(j)] * (keep(c, j) * slope_of(z, sig(z)))
            pool[c, 7, chunk(j)] = d
            return (sums[0] + fold(d), sums[1] + fold(d * ((value - center) * scaling)))

        ar_start(8, c, each_column(2, body))

    crops(body_back_conv, "bback")
    conv_grad(lambda c, tap, l: a1[c, GUARD : GUARD + PX, l], v_body, "k1")
    poll("k1")

    def body_back_in(c):
        a, slope, offset = norm_coefficients(c, 4, ar_wait(8, c, 2), inverse_out(c), 3, 0)

        def body(j):
            dp_buf[c, chunk(j, GUARD)] = (
                keep(c, j) * (a * pool[c, 7, chunk(j)] + slope * pool[c, 4, chunk(j)] + offset)
            ).astype(BF16)

        loop(14, body)

        def back(n):
            pool[c, 3, :, col(n)] = (
                (nt(dp_of(c), rows_of("wa1", n)) + pool[c, 3, :, col(n)]).astype(BF16).astype(F32)
            )

        loop(4, back)
        poll_crop(c, ("bin", "a"))
        center, scaling = hat_of(c, 2)
        short_center, short_scaling = hat_of(c, 3)

        def pre(j, sums):
            z = entry_pre(c, j)
            d = pool[c, 3, chunk(j)] * (keep(c, j) * slope_of(z, sig(z)))
            pool[c, 3, chunk(j)] = d
            return (
                sums[0] + fold(d),
                sums[1] + fold(d * ((pool[c, 1, chunk(j)] - center) * scaling)),
                sums[2] + fold(d * ((pool[c, 2, chunk(j)] - short_center) * short_scaling)),
            )

        sums = each_column(3, pre)
        ar_start(9, c, sums)

    crops(body_back_in, "bin")
    outer(lambda c, l: hid[c, :, l], dp_of, "wa1")
    poll("wa1")
    build_conv("k0")

    def entry_back_out(c):
        totals = ar_wait(9, c, 3)
        a, slope, offset = norm_coefficients(c, 2, totals[0:2], inverse_out(c), 2, 0)
        short = norm_coefficients(c, 3, [totals[0], totals[2]], inverse_out(c), 12, 0)

        def project(j):
            mask = keep(c, j)
            d = pool[c, 3, chunk(j)]
            dp_buf[c, chunk(j, GUARD)] = (
                mask * (a * d + slope * pool[c, 1, chunk(j)] + offset)
            ).astype(BF16)
            hid[c, chunk(j)] = (
                mask * (short[0] * d + short[1] * pool[c, 2, chunk(j)] + short[2])
            ).astype(BF16)

        loop(14, project)

        def back(n):
            pool[c, 2, :, col(n)] = nt(hid[c], rows_of("ws", n))

        loop(2, back)
        ar_start(10, c, ungate(c, 0, 1, 0, wd0, wu0, "wc0"))

    crops(entry_back_out, "eback")
    outer(lambda c, l: ga[0, c, :, l], dp_of, "wc0")
    poll("wc0")
    outer(lambda c, l: u_buf[c, 0, :, l], lambda c: hid[c], "ws")
    credit_sibling(4)
    small_grads(0)
    poll("small0")

    def entry_back_conv(c):
        a, slope, offset = norm_coefficients(c, 1, ar_wait(10, c, 2), inverse_out(c), 1, 0)
        conv_cotangent(c, 1, 0, a, slope, offset, 2)
        for q in range(2):
            for r in range(2):
                def back(n):
                    total = None
                    for tap, tq, tr, ta, tb in taps0():
                        if (tq, tr) == (q, r):
                            term = nt(v_entry(c, tap, col(n)), kd[n, 256 * tap : 256 * tap + 256])
                            total = term if total is None else total + term
                    pool[c, 4 + 2 * q + r, :, col(n)] = total

                loop(4, back)
            poll_crop(c, ("econv", "ab"[q]))
        a, shift = affine(c, 0)
        center, scaling = hat_of(c, 0)

        def body(j, sums):
            mask = keep(c, j)
            first, second = sums
            for k in range(4):
                value = inn[c, k, chunk(j)]
                z = value * a + shift
                d = pool[c, 4 + k, chunk(j)] * (mask * slope_of(z, sig(z)))
                pool[c, 4 + k, chunk(j)] = d
                first = first + fold(d)
                second = second + fold(d * ((value - center) * scaling))
            return (first, second)

        ar_start(11, c, each_column(2, body))

    crops(entry_back_conv, "econv")

    def act_entry(c, tap, lanes):
        q = 0 if tap // 3 == 1 else 1
        r = 0 if tap % 3 == 1 else 1
        return a0[c, 2 * q + r, GUARD : GUARD + PX, lanes]

    conv_grad(act_entry, v_entry, "k0")
    poll("k0")
    load_map = local_copy(expand.at[0], e_buf, 2)
    load_map.start()
    for copy in out_copies:
        copy.wait()

    def entry_back_in(c):
        a, slope, offset = norm_coefficients(c, 0, ar_wait(11, c, 2), inverse_in(c), 0, 0)

        def body(j):
            mask = keep(c, j)
            for k in range(4):
                a0[c, k, chunk(j, GUARD)] = (
                    mask * (a * pool[c, 4 + k, chunk(j)] + slope * inn[c, k, chunk(j)] + offset)
                ).astype(BF16)

        loop(14, body)

    loop(2, entry_back_in)
    swap = to_sibling(ng, ng_in, 3)
    swap.start()

    def input_grad(m):
        total = None
        for q in range(2):
            for r in range(2):
                at = pl.ds(pl.multiple_of(512 * r + 256 * m, 256), 256)
                term = tn(
                    both(lambda c: u_buf[c, q, :, at]),
                    both(lambda c: a0[c, 2 * q + r, GUARD : GUARD + PX]),
                )
                total = term if total is None else total + term
        return total

    def input_block(m):
        dp_buf[m] = rows_of("wa0", m)
        put_rows("wa0", m, input_grad(m))

    loop(2, input_block)
    poll("wa0")

    def entry_back_input(c):
        for q in range(2):
            for r in range(2):
                def back(n):
                    total = nt(a0[c, 2 * q + r, GUARD : GUARD + PX], dp_buf[n])
                    if q == 0 and r == 0:
                        total = total + pool[c, 2, :, col(n)]
                    at = pl.ds(pl.multiple_of(512 * r + 256 * n, 256), 256)
                    d_buf[c, q, 0:PX, at] = total.astype(BF16)

                loop(2, back)
            if q == 0:
                poll_crop(c, ("input", "a"))

    crops(entry_back_input, "input")

    def entry_emit(c):
        for q in range(2):
            def store(start, width, y):
                for j in range(OUT):
                    for k in range(width // 128):
                        fs[pl.ds(512 * (start // 128 + k) + 32 * j + q, 14, stride=2)] = y[
                            16 * j : 16 * j + 14, 128 * k : 128 * k + 128
                        ]

            narrow(d_buf[c, q, 0:PX], store)
        poll_crop(c, ("emit", "a"))
        for h in range(2):
            for j in range(OUT):
                for k in range(7):
                    x_buf[h, c, :, D * j + 128 * k : D * j + 128 * k + 128] = fs[
                        512 * k + 32 * j + 14 * h : 512 * k + 32 * j + 14 * h + 14
                    ].astype(BF16)

    load_map.wait()
    crops(entry_emit, "emit")
    last = [
        to_sibling(x_buf.at[other], grad.at[mine], 4),
        local_copy(x_buf.at[section], grad.at[mine], 0),
    ]
    for copy in last:
        copy.start()
    swap.wait()
    ng[...] = ng[...] + ng_in[...]
    last.append(local_copy(ng, result.at[pl.ds(192, 16)], 1))
    last[-1].start()
    poll("tail")
    last.append(local_copy(pool.at[0, 1, pl.ds(0, 192)], result.at[pl.ds(0, 192)], 2))
    last[-1].start()
    for copy in last:
        copy.wait()


def thirds(value):
    high = value.astype(BF16)
    left = value - high.astype(F32)
    middle = left.astype(BF16)
    return jnp.concatenate([high, middle, (left - middle.astype(F32)).astype(BF16)], 0)


def final_kernel(result, narrow_map, *refs):
    flat_out, (gain_out, shift_out, short_gain_out, short_shift_out) = refs[:11], refs[11:15]
    flat, (gain, shift, short_gain, short_shift), sems = refs[15:26], refs[26:30], refs[30]
    section = lax.axis_index("section")
    total = nt(thirds(result[192:208]), narrow_map[...])
    total = total[0:16] + total[16:32] + total[32:48]

    def own(top, low):
        return jnp.where(section == 0, top, low)

    for k in range(3):
        gain[k] = own(total[k : k + 1], total[k + 3 : k + 4])
        shift[k] = own(total[k + 6 : k + 7], total[k + 9 : k + 10])
    short_gain[...] = own(total[12:13, 0:DIN], total[12:13, DIN:])
    short_shift[...] = own(total[13:14, 0:DIN], total[13:14, DIN:])
    total = result[0:192]
    high = total.astype(BF16)
    low = (total - high.astype(F32)).astype(BF16)
    final = nt(high, narrow_map[...]) + nt(low, narrow_map[...])
    for (name, count), ref in zip(
        (
            ("wa0", 14), ("k0", 16), ("ws", 14), ("wd0", 4), ("wu0", 4), ("wc0", 28), ("wa1", 28),
            ("k1", 16), ("wd1", 7), ("wu1", 7), ("wc1", 28),
        ),
        flat,
    ):
        if name[1] in "du":
            at = ROWS["misc" + name[2]][0] + (8 if name[1] == "u" else 0)
        else:
            at = ROWS[name][0]
        for k in range(7):
            ref[pl.ds(k, count, stride=7)] = final[at : at + count, 128 * k : 128 * k + 128]
    copies = [
        pltpu.make_async_copy(src, dst, sems.at[at])
        for at, (src, dst) in enumerate(
            zip((*flat, gain, shift, short_gain, short_shift), (*flat_out, gain_out, shift_out, short_gain_out, short_shift_out))
        )
    ]
    for copy in copies:
        copy.start()
    for copy in copies:
        copy.wait()


def final_call(result, narrow_map):
    vmem = pl.BlockSpec(memory_space=pltpu.VMEM)
    shapes = [(count, 128) for count in LINES] + [(3, 1, D), (3, 1, D), (1, DIN), (1, DIN)]
    return pl.pallas_call(
        final_kernel,
        out_shape=[jax.ShapeDtypeStruct(shape, F32) for shape in shapes],
        in_specs=[vmem, vmem],
        out_specs=[pl.BlockSpec(memory_space=pl.ANY)] * 15,
        scratch_shapes=[pltpu.VMEM(shape, F32) for shape in shapes]
        + [pltpu.SemaphoreType.DMA((15,))],
        compiler_params=pltpu.CompilerParams(vmem_limit_bytes=16 << 20),
    )(result, narrow_map)


def lane_maps():
    at = np.arange(D)
    first = np.zeros((D, C), np.float32)
    first[at, at // 14 * 16 + at % 14] = 1
    second = np.zeros((D, C), np.float32)
    second[at, at // 28 * 32 + at % 28] = 1
    return np.stack([first, second])


def main_call(n_dp, *args):
    v = n_dp // MEMBERS
    any_space = pl.BlockSpec(memory_space=pl.ANY)
    smem = pl.BlockSpec(memory_space=pltpu.SMEM)
    shape = lambda *s, dtype=BF16: jax.ShapeDtypeStruct(s, dtype)
    outs = [
        shape(4, 7, 12544), shape(4, 14, 12544), shape(208, C, dtype=F32),
    ]
    dma = pltpu.SemaphoreType.DMA
    scratch = [
        pltpu.VMEM((2, 4, PX, C), F32),
        pltpu.VMEM((2, 8, PX, C), F32),
        pltpu.VMEM((2, 2, PX, C), BF16),
        pltpu.VMEM((2, 4, PX + 2 * GUARD, C), BF16),
        pltpu.VMEM((2, PX + 2 * GUARD, C), BF16),
        pltpu.VMEM((2, 2, PX + 2 * GUARD, C), BF16),
        pltpu.VMEM((2, 2, PX, C), BF16),
        pltpu.VMEM((2, PX, C), BF16),
        pltpu.VMEM((2, PX + 2 * GUARD, C), BF16),
        pltpu.VMEM((2, 2, 14, 12544), BF16),
        pltpu.VMEM((2, 2, 7, 12544), BF16),
        pltpu.VMEM((4096, 128), F32),
        pltpu.VMEM((4, 2304, 256), BF16),
        pltpu.VMEM((D, C), BF16),
        pltpu.VMEM((2, 4, 4, 192, C), BF16),
        pltpu.VMEM((C, 128), BF16),
        pltpu.VMEM((128, C), BF16),
        pltpu.VMEM((C, 256), BF16),
        pltpu.VMEM((256, C), BF16),
        pltpu.VMEM((3, 48, C), BF16),
        pltpu.VMEM((16, C), F32),
        pltpu.VMEM((2, 8, D), F32),
        pltpu.VMEM((2, 7, 8, C), F32),
        pltpu.VMEM((2, 2, 8, C), F32),
        pltpu.VMEM((2, 8, C), F32),
        pltpu.VMEM((16, C), F32),
        pltpu.VMEM((16, C), F32),
        pltpu.VMEM((2, 2, MEMBERS, 2, C), F32),
        pltpu.VMEM((2, MEMBERS, 4, C), F32),
        pltpu.VMEM((2, 2, MEMBERS, 32, 128), BF16),
        pltpu.VMEM((2, 2, v, 4, C), F32),
        pltpu.VMEM((3, 1, D), F32),
        pltpu.VMEM((3, 1, D), F32),
        pltpu.VMEM((7, 128), BF16),
        *[pltpu.VMEM((count, 128), BF16) for count in LINES],
        dma((15,)), dma((2, 2)), dma((2, 2)), dma((2, 2)), dma((2, 2)), dma((5,)), dma((5,)), dma((4,)),
        dma((7, 4)), dma((7, 4)), dma((7, 4)), dma((7, 4)), pltpu.SemaphoreType.REGULAR((6,)),
    ]
    return pl.pallas_call(
        functools.partial(main_kernel, n_dp),
        out_shape=outs,
        in_specs=[any_space, any_space, smem] + [any_space] * 15,
        out_specs=[any_space] * 3,
        scratch_shapes=scratch,
        compiler_params=pltpu.CompilerParams(
            collective_id=1, has_side_effects=True, vmem_limit_bytes=64 << 20
        ),
    )(*args)


def local(
    features, crop_side, upstream,
    entry_in, entry_group, entry_out, entry_down, entry_up, shortcut_weight,
    body_in, body_group, body_out, body_down, body_up,
    norm_gain, norm_shift, shortcut_gain, shortcut_shift,
):
    n_dp = lax.axis_size("dp")
    v = n_dp // MEMBERS
    groups = [[v * member + k for k in range(v)] for member in range(MEMBERS)]
    shards = (
        entry_in, entry_group, shortcut_weight, entry_down, entry_up, entry_out,
        body_in, body_group, body_down, body_up, body_out,
    )

    def lines(shard, count):
        if v > 1:
            shard = lax.all_gather(shard, "dp", axis_index_groups=groups, axis=0, tiled=True)
        return jnp.pad(shard, (0, 128 * count - shard.shape[0])).reshape(count, 128)

    maps = jnp.asarray(lane_maps(), BF16)
    output, d_features, result = main_call(
        n_dp, features, upstream, crop_side, maps,
        norm_gain.transpose(1, 0, 2), norm_shift.transpose(1, 0, 2),
        jnp.concatenate([shortcut_gain, shortcut_shift]).reshape(7, 128),
        *(lines(shard, count) for shard, count in zip(shards, LINES)),
    )
    results = final_call(result, jnp.asarray(lane_maps()[1], BF16))

    def share(values, shard):
        values = values.reshape(-1)[: v * shard.shape[0]]
        if v > 1:
            values = lax.psum_scatter(
                values, "dp", scatter_dimension=0, axis_index_groups=groups, tiled=True
            )
        return values

    wa0, k0, ws, wd0, wu0, wc0, wa1, k1, wd1, wu1, wc1 = (
        share(values, shard) for values, shard in zip(results[:11], shards)
    )
    gains, shifts, short_gain, short_shift = results[11:15]
    return (
        output, d_features, wa0, k0, wc0, wd0, wu0, ws, wa1, k1, wc1, wd1, wu1,
        gains.transpose(1, 0, 2), shifts.transpose(1, 0, 2),
        short_gain[0], short_shift[0],
    )


def solution(mesh):
    rows = P("dp", "section", None)
    flat = P(("section", "dp"))
    params = (P("section", None, None), P("section", None, None), P("section"), P("section"))
    return jax.shard_map(
        local,
        mesh=mesh,
        in_specs=(rows, P("dp"), rows) + (flat,) * 11 + params,
        out_specs=(rows, rows) + (flat,) * 11 + params,
        check_vma=False,
    )
```

```python
import functools

import jax
import jax.numpy as jnp
import numpy as np
from jax import lax
from jax.experimental import pallas as pl
from jax.experimental.pallas import tpu as pltpu
from jax.sharding import PartitionSpec as P

D = 896
DIN = 448
OUT = 14
IN = 28
SE0 = 112
SE1 = 224
EPSILON = 1e-05
F32 = jnp.float32
BF16 = jnp.bfloat16
MESH = pl.DeviceIdType.MESH
C = 1024
PX = 224
GUARD = 16
MEMBERS = 16
SHORT = 12
SHARDS = 32
ROWS = {
    "wa0": (0, 16), "k0": (16, 16), "ws": (32, 16), "misc0": (48, 16), "wc0": (64, 32),
    "k1": (96, 16), "wa1": (112, 32), "misc1": (144, 16), "wc1": (160, 32),
}
ORDER = ("wa0", "k0", "ws", "wd0", "wu0", "wc0", "k1", "wa1", "wd1", "wu1", "wc1")
ORDER_IN = ("wa0", "k0", "ws", "wd0", "wu0", "wc0", "wa1", "k1", "wd1", "wu1", "wc1")
LINES = (98, 112, 98, 28, 28, 196, 196, 112, 49, 49, 196)
GATHERS = ((0, 16), (16, 32), (32, 64), (64, 96), (96, 112), (112, 144), (144, 192))
SCATTERS = (
    (144, 192), (96, 112), (112, 144), (64, 96), (32, 64), (16, 32), (0, 16)
)
CHAINED = 5
GATHER_PLAN = {
    "own": ((0, 0),),
    "params": ((1, 0),),
    "cot0": ((2, 0), (3, 0), (0, 1), (4, 0), (0, 2)),
    "cot1": ((1, 1), (0, 3)),
    "map": ((2, 1), (5, 0)),
    "ph0": ((0, 4), (1, 2)),
    "ph1": ((1, 3),),
    "in0b": ((2, 2), (3, 1)),
    "in0": ((2, 3),),
    "need_wa0": ((0, 5),),
    "in1a": ((1, 4),),
    "in1": ((1, 5), (6, 0), (3, 2), (5, 1), (3, 3)),
    "in1b": ((4, 1),),
    "conv1a": ((2, 4),),
    "bk0": ((4, 2),),
    "conv0a": ((4, 3),),
    "need_ws": ((3, 4), (2, 5)),
    "conv1": ((5, 2),),
    "str0": ((5, 3),),
    "str1": ((6, 1),),
    "need_wc0": ((3, 5), (4, 4)),
    "gate1": ((5, 4),),
    "need_k1": ((6, 2),),
    "out0": ((6, 3),),
    "need_wa1": ((5, 5),),
    "gate1a": ((4, 5),),
    "bconv0a": ((6, 4),),
    "bconv1": ((6, 5),),
}
SCATTER_PLAN = {
    "small1": ((0, 0),),
    "bback0": ((0, 1),),
    "bback1": ((0, 2),),
    "bin0a": ((1, 0),),
    "bin1a": ((0, 3),),
    "wa1": ((1, 1),),
    "bk0b": ((1, 2),),
    "eback0a": ((0, 4), (2, 0)),
    "eback0": ((1, 3),),
    "eback1a": ((2, 1),),
    "eback1": ((2, 2),),
    "wc0": ((1, 4),),
    "small0": ((4, 0), (3, 0)),
    "econv0a": ((2, 3),),
    "econv0": ((0, 5), (1, 5)),
    "econv0b": ((3, 1), (3, 2)),
    "econv1a": ((2, 4),),
    "econv1b": ((3, 3),),
    "econv1": ((4, 1), (4, 2)),
    "d": ((3, 4),),
    "k0": ((5, 0),),
    "wa0": ((4, 3), (5, 1), (6, 0), (5, 2)),
    "input0a": ((2, 5), (6, 1), (6, 2)),
    "input0": ((4, 4), (5, 3), (6, 3), (5, 4)),
    "emit0a": ((4, 5), (3, 5)),
    "input1": ((6, 4),),
    "emit1a": ((5, 5),),
    "tail": ((6, 5),),
}


def dot(a, b, dims):
    return lax.dot_general(a, b, ((dims[:1], dims[1:]), ((), ())), preferred_element_type=F32)


def nn(a, b):
    return dot(a, b, (1, 0))


def nt(a, b):
    return dot(a, b, (1, 1))


def tn(a, b):
    return dot(a, b, (0, 0))


def sig(z):
    return jnp.tanh(z * 0.5) * 0.5 + 0.5


def slope_of(z, s):
    return s * (1.0 + z * (1.0 - s))


def silu_half(h):
    return h * (1.0 + jnp.tanh(h))


def slope_half(h):
    t = jnp.tanh(h)
    return (1.0 + t) * (1.0 + h * (1.0 - t))


def split_rows(rows):
    high = [r.astype(BF16).astype(F32) for r in rows]
    low = [r - h for r, h in zip(rows, high)]
    return high, low


def stacked(rows):
    pad = jnp.zeros((16 - len(rows), rows[0].shape[1]), F32)
    return jnp.concatenate(list(rows) + [pad], 0).astype(BF16)


def row_dot(row, weight, mul):
    high, low = split_rows([row])
    both = mul(stacked(high + low), weight)
    return both[0:1] + both[1:2]


def col(n, width=256):
    return pl.ds(pl.multiple_of(n * width, width), width)


def chunk(j, base=0):
    return pl.ds(pl.multiple_of(j * 16 + base, 16), 16)


def loop(count, body):
    def step(i, carry):
        body(i)
        return carry

    lax.fori_loop(0, count, step, 0)


def main_kernel(
    n_dp, features, upstream, side_ref, expand, gain_in, shift_in, short_gain_in, short_shift_in,
    l_wa0, l_k0, l_ws, l_wd0, l_wu0, l_wc0, l_wa1, l_k1, l_wd1, l_wu1, l_wc1,
    out, grad, result,
    inn, pool, u_buf, a0, a1, d_buf, ga, hid, dp_buf, x_buf, up_buf, fs, kd, e_buf,
    w, wd0, wu0, wd1, wu1, stage, params, pair, st, sv, cn, ng, ng_in, ar2, ars, arh, arv,
    v_gain, v_shift, v_short_gain, v_short_shift, v_wa0, v_k0, v_ws, v_wd0, v_wu0, v_wc0, v_wa1, v_k1, v_wd1, v_wu1,
    v_wc1, isem, asend, arecv, vsend, vrecv, xsend, xrecv, lsem, gsend, grecv, rsend, rrecv, free,
):
    loads = [
        pltpu.make_async_copy(src, dst, isem.at[at])
        for at, (src, dst) in enumerate(
            (
                (l_wa0, v_wa0), (l_k0, v_k0), (l_ws, v_ws), (l_wd0, v_wd0), (l_wu0, v_wu0),
                (l_wc0, v_wc0), (l_wa1, v_wa1), (l_k1, v_k1), (l_wd1, v_wd1), (l_wu1, v_wu1),
                (l_wc1, v_wc1), (gain_in, v_gain), (shift_in, v_shift),
                (short_gain_in, v_short_gain), (short_shift_in, v_short_shift),
            )
        )
    ]
    load_map = pltpu.make_async_copy(expand.at[1], e_buf, isem.at[15])
    for copy in loads + [load_map]:
        copy.start()
    section = lax.axis_index("section")
    me = lax.axis_index("dp")
    v = n_dp // MEMBERS
    digit, rest = me // v, lax.rem(me, v)
    other = 1 - section

    def member(hop):
        return lax.rem(digit + hop, MEMBERS) * v + rest

    def near(hop):
        return digit * v + lax.rem(rest + hop, v)

    barrier = pltpu.get_barrier_semaphore()

    def greet(hop):
        pl.semaphore_signal(barrier, inc=1, device_id=(section, member(hop + 1)), device_id_type=MESH)

    def greet_near(hop):
        pl.semaphore_signal(barrier, inc=1, device_id=(section, near(hop + 1)), device_id_type=MESH)

    loop(MEMBERS - 1, greet)
    if v > 1:
        loop(v - 1, greet_near)
    pl.semaphore_signal(barrier, inc=1, device_id=(other, me), device_id_type=MESH)
    def local_copy(src, dst, sem=0):
        return pltpu.make_async_copy(src, dst, lsem.at[sem])

    def to_sibling(src, dst, at):
        return pltpu.make_async_remote_copy(
            src_ref=src, dst_ref=dst, send_sem=xsend.at[at], recv_sem=xrecv.at[at],
            device_id=(other, me), device_id_type=MESH,
        )

    mine = pl.ds(2 * section, 2)
    theirs = pl.ds(2 * other, 2)
    copies = [
        local_copy(features.at[mine], x_buf.at[section], 0),
        local_copy(upstream.at[mine], up_buf.at[section], 1),
    ]
    for copy in copies:
        copy.start()

    def dp_of(c):
        return dp_buf[c, GUARD : GUARD + PX]

    def half_side(c):
        return side_ref[2 * section + c] // 2

    def keep(c, j, weight=1.0):
        half = half_side(c)
        bound = jnp.where(j < half, half, 0)
        tile = jnp.where(lax.broadcasted_iota(jnp.int32, (16, 128), 0) < bound, weight, 0.0)
        return jnp.concatenate([tile] * (C // 128), 1)

    def crop_count(c):
        half = half_side(c)
        return (half * half).astype(F32)

    def ar_slots(n, c):
        if 6 <= n < SHORT:
            return arh.at[n % 2, c, :, pl.ds(0, 32 if n == 9 else 16)]
        return ars.at[c] if n == SHORT else ar2.at[n % 2, c]

    def ar_lane(n):
        return 2 if n == SHORT else n % 2

    def ar_start(n, c, rows):
        slots = ar_slots(n, c)
        if 6 <= n < SHORT:
            tiles = [row[:, 128 * k : 128 * k + 128] for row in rows for k in range(8)]
            if n == 9:
                tiles.append(jnp.zeros((8, 128), F32))
            slots[digit] = jnp.concatenate(tiles, 0).astype(BF16)
        else:
            slots[digit] = jnp.concatenate(rows, 0)

        def send(hop):
            pltpu.make_async_remote_copy(
                src_ref=slots.at[digit], dst_ref=slots.at[digit], send_sem=asend.at[ar_lane(n), c],
                recv_sem=arecv.at[ar_lane(n), c], device_id=(section, member(hop + 1)),
                device_id_type=MESH,
            ).start()

        loop(MEMBERS - 1, send)

    def ar_wait(n, c, rows):
        slots = ar_slots(n, c)
        arrived = slots.at[pl.ds(0, MEMBERS - 1)]
        pltpu.make_async_copy(arrived, arrived, asend.at[ar_lane(n), c]).wait()
        pltpu.make_async_copy(arrived, arrived, arecv.at[ar_lane(n), c]).wait()
        total = slots[0].astype(F32)
        for k in range(1, MEMBERS):
            total = total + slots[k].astype(F32)
        if 6 <= n < SHORT:
            total = jnp.concatenate(
                [
                    jnp.concatenate([total[8 * r + k : 8 * r + k + 1] for k in range(8)], 1)
                    for r in range(rows)
                ],
                0,
            )
        if v > 1:
            again = arv.at[ar_lane(n), c]
            spare = [jnp.zeros((4 - rows, C), F32)] if rows < 4 else []
            again[rest] = jnp.concatenate([total] + spare, 0)

            def send(hop):
                pltpu.make_async_remote_copy(
                    src_ref=again.at[rest], dst_ref=again.at[rest], send_sem=vsend.at[ar_lane(n), c],
                    recv_sem=vrecv.at[ar_lane(n), c], device_id=(section, near(hop + 1)),
                    device_id_type=MESH,
                ).start()

            loop(v - 1, send)
            arrived = again.at[pl.ds(0, v - 1)]
            pltpu.make_async_copy(arrived, arrived, vsend.at[ar_lane(n), c]).wait()
            pltpu.make_async_copy(arrived, arrived, vrecv.at[ar_lane(n), c]).wait()
            total = again[0]
            for k in range(1, v):
                total = total + again[k]
        return [total[k : k + 1] for k in range(rows)]

    def down(sums):
        return jnp.sum(sums, axis=0, keepdims=True)

    def fold(value):
        return value[0:8] + value[8:16]

    def zeros(count):
        return tuple(jnp.zeros((8, C), F32) for _ in range(count))

    def each_column(count, body):
        sums = lax.fori_loop(0, 14, body, zeros(count))
        return [down(one) for one in sums]

    def scaled(sums, *factors):
        return [sums[0]] + [one * factor for one, factor in zip(sums[1:], factors)]

    def moment_sums(c, value_of):
        def body(j, sums):
            value = value_of(j)
            weighted = value * keep(c, j)
            return (sums[0] + fold(weighted), sums[1] + fold(weighted * value))

        return each_column(2, body)

    def set_stats(c, index, totals, inverse, gain_row):
        center = totals[0] * inverse
        scaling = lax.rsqrt(totals[1] * inverse - center * center + EPSILON)
        gain = params[gain_row : gain_row + 1] * scaling
        shift_row = gain_row + 6 if gain_row < 6 else gain_row + 1
        st[c, index, 0:1] = center
        st[c, index, 1:2] = scaling
        st[c, index, 2:3] = gain
        st[c, index, 3:4] = params[shift_row : shift_row + 1] - center * gain
        st[c, index, 4:6] = st[c, index, 2:4] * 0.5

    def affine(c, index):
        return st[c, index, 4:5], st[c, index, 5:6]

    def hat_of(c, index):
        return st[c, index, 0:1], st[c, index, 1:2]

    def inverse_out(c):
        return cn[c, 1:2]

    def inverse_in(c):
        return cn[c, 2:3]

    def place(shard):
        return shard // 16, lax.rem(shard // 4, 4), lax.rem(shard, 4)

    def cols_of(name, lanes):
        at, count = ROWS[name]
        value = w[:, :, :, at : at + count, lanes]
        return value.reshape(SHARDS * count, value.shape[-1])

    def rows_index(name, n):
        at, count = ROWS[name]
        if count == 16:
            return (n, slice(None), slice(None), slice(at, at + 16))
        return (n // 2, pl.ds(2 * lax.rem(n, 2), 2), slice(None), slice(at, at + 32))

    def rows_of(name, n):
        return w[rows_index(name, n)].reshape(256, C)

    def put_rows(name, n, value):
        shape = (4, 4, 16, C) if ROWS[name][1] == 16 else (2, 4, 32, C)
        w[rows_index(name, n)] = value.astype(BF16).reshape(shape)

    def shard_rows(name, shard):
        at, count = ROWS[name]
        return w[(*place(shard), slice(at, at + count))].astype(F32)

    def put_shard(name, shard, value):
        at, count = ROWS[name]
        w[(*place(shard), slice(at, at + count))] = value.astype(BF16)

    def tile(k):
        return slice(128 * k, 128 * k + 128)

    def build_conv(name):
        def shard(s):
            rows = shard_rows(name, s)
            for a in range(4):
                for k in range(2):
                    fs[pl.ds(2048 * k + 63 * s + a, 16, stride=4)] = rows[:, tile(2 * a + k)]

        loop(SHARDS, shard)
        lane = lax.broadcasted_iota(jnp.int32, (64, 256), 1) // 64

        def block(a):
            for tap in range(9):
                tiles = []
                for k in range(2):
                    at = 2048 * k + 224 * tap
                    tiles.append(
                        jnp.concatenate(
                            [
                                fs[pl.ds(at + a, 28, stride=4)],
                                jnp.zeros((4, 128), F32),
                                fs[pl.ds(at + 112 + a, 28, stride=4)],
                                jnp.zeros((4, 128), F32),
                            ],
                            0,
                        )
                    )
                dense = jnp.concatenate(tiles, 1)
                for g in range(4):
                    kd[a, 256 * tap + 64 * g : 256 * tap + 64 * g + 64] = jnp.where(
                        lane == g, dense, 0.0
                    ).astype(BF16)

        loop(4, block)

    def build_small(b):
        wd, wu = (wd0, wu0) if b == 0 else (wd1, wu1)
        fs[...] = jnp.zeros_like(fs)

        def shard(s):
            rows = shard_rows("misc0" if b == 0 else "misc1", s)
            if b == 0:
                for k in range(8):
                    fs[pl.ds(32 * s + k, 4, stride=8)] = rows[0:4, tile(k)]
                    fs[pl.ds(1024 + 256 * (k % 4) + 7 * s + k // 4, 4, stride=2)] = rows[
                        8:12, tile(k)
                    ]
            else:
                for k in range(8):
                    fs[pl.ds(1024 * (k % 2) + 32 * s + k // 2, 7, stride=4)] = rows[0:7, tile(k)]
                    fs[pl.ds(2048 + 256 * k + 7 * s, 7)] = rows[8:15, tile(k)]

        loop(SHARDS, shard)
        for k in range(1 + b):
            wd[:, tile(k)] = fs[1024 * k : 1024 * k + 1024].astype(BF16)
        gap = jnp.zeros((4, 128), F32)
        for g in range(4 + 4 * b):
            for k in range(8):
                if b == 0:
                    start = 1024 + 256 * (k % 4) + 56 * g + k // 4
                    part = fs[pl.ds(start, 28, stride=2)]
                else:
                    start = 2048 + 256 * k + 28 * g
                    part = fs[start : start + 28]
                wu[32 * g : 32 * g + 32, tile(k)] = jnp.concatenate([part, gap], 0).astype(BF16)

    def taps0():
        for a in range(3):
            for b in range(3):
                yield a * 3 + b, (0 if a == 1 else 1), (0 if b == 1 else 1), a, b

    def both(ref_of):
        return jnp.concatenate([ref_of(0), ref_of(1)], 0)

    def squeeze(c, b, pooled, wd, wu):
        width = wd.shape[1]
        raw = row_dot(pooled, wd[...], nn)
        squeezed = raw * sig(raw)
        gating = sig(row_dot(squeezed, wu[...], nn))
        sv[b, c, 0:1] = pooled
        sv[b, c, 1:2, 0:width] = raw
        sv[b, c, 2:3, 0:width] = squeezed
        sv[b, c, 3:4] = gating
        return gating

    def gate(c, b, index, conv_k, wd, wu, name, proj_k):
        a, shift = affine(c, index)

        def pool_chunk(j, sums):
            z = pool[c, conv_k, chunk(j)] * a + shift
            excited = keep(c, j) * silu_half(z)
            pool[c, 7, chunk(j)] = excited
            return (sums[0] + fold(excited),)

        pooled = each_column(1, pool_chunk)[0] / crop_count(c)
        gating = squeeze(c, b, pooled, wd, wu)
        poll_crop(c, ("gate" if b == 0 else "bgate", "a"))

        def gate_chunk(j):
            ga[b, c, chunk(j)] = (pool[c, 7, chunk(j)] * gating).astype(BF16)

        loop(14, gate_chunk)

        def project(n):
            pool[c, proj_k, :, col(n)] = nn(ga[b, c], cols_of(name, col(n)))

        loop(4, project)
        return moment_sums(c, lambda j: pool[c, proj_k, chunk(j)])

    def ungate(c, b, index, conv_k, wd, wu, name):
        width = wd.shape[1]

        def back(n):
            pool[c, 7, :, col(n)] = nt(dp_of(c), rows_of(name, n))

        loop(4, back)
        a, shift = affine(c, index)

        def gate_chunk(j, sums):
            z = pool[c, conv_k, chunk(j)] * a + shift
            excited = keep(c, j) * silu_half(z)
            return (sums[0] + fold(pool[c, 7, chunk(j)] * excited),)

        d_gate = each_column(1, gate_chunk)[0]
        poll_crop(c, ("eback" if b == 0 else "bout", "a"))
        gating = sv[b, c, 3:4]
        d_raw = d_gate * gating * (1.0 - gating)
        raw = sv[b, c, 1:2, 0:width]
        d_squeeze = row_dot(d_raw, wu[...], nt) * slope_of(raw, sig(raw))
        d_pool = row_dot(d_squeeze, wd[...], nt) / crop_count(c)
        sv[b, c, 4:5] = d_raw
        sv[b, c, 5:6, 0:width] = d_squeeze
        center, scaling = hat_of(c, index)

        def slope_chunk(j, sums):
            value = pool[c, conv_k, chunk(j)]
            z = value * a + shift
            d = (pool[c, 7, chunk(j)] * gating + d_pool) * (keep(c, j, 0.5) * slope_half(z))
            pool[c, 7, chunk(j)] = d
            return (sums[0] + fold(d), sums[1] + fold(d * (value - center)))

        return scaled(each_column(2, slope_chunk), scaling)

    def small_grads(b):
        width = 128 + 128 * b

        def pairs(x_row, x_width, y_row, y_width):
            xs, ys = [], []
            for c in range(2):
                xh, xl = split_rows([sv[b, c, x_row : x_row + 1, 0:x_width]])
                yh, yl = split_rows([sv[b, c, y_row : y_row + 1, 0:y_width]])
                xs += [xh[0], xh[0], xl[0]]
                ys += [yh[0], yl[0], yh[0]]
            return tn(stacked(xs), stacked(ys))

        grad_down = pairs(0, C, 5, width)
        for k in range(1 + b):
            fs[1024 * k : 1024 * k + 1024] = grad_down[:, tile(k)]
        grad_up = pairs(2, width, 4, C)
        for g in range(4 + 4 * b):
            for k in range(8):
                part = grad_up[32 * g : 32 * g + 28, tile(k)]
                if b == 0:
                    fs[pl.ds(1024 + 256 * (k % 4) + 56 * g + k // 4, 28, stride=2)] = part
                else:
                    fs[2048 + 256 * k + 28 * g : 2048 + 256 * k + 28 * g + 28] = part

        def shard(s):
            tiles = []
            for k in range(8):
                if b == 0:
                    count = 4
                    first = fs[pl.ds(32 * s + k, 4, stride=8)]
                    second = fs[pl.ds(1024 + 256 * (k % 4) + 7 * s + k // 4, 4, stride=2)]
                else:
                    count = 7
                    first = fs[pl.ds(1024 * (k % 2) + 32 * s + k // 2, 7, stride=4)]
                    second = fs[pl.ds(2048 + 256 * k + 7 * s, 7)]
                gap = jnp.zeros((8 - count, 128), F32)
                tiles.append(jnp.concatenate([first, gap, second, gap], 0))
            put_shard("misc0" if b == 0 else "misc1", s, jnp.concatenate(tiles, 1))

        loop(SHARDS, shard)

    def norm_coefficients(c, index, totals, inverse, gain_row, kind):
        center, scaling = hat_of(c, index)
        ng[gain_row : gain_row + 1] += totals[1]
        shift_row = gain_row + 6 if gain_row < 6 else gain_row + 1
        ng[shift_row : shift_row + 1] += totals[0]
        a = st[c, index, 2:3]
        slope = -a * scaling * (totals[1] * inverse)
        offset = -a * (totals[0] * inverse) - slope * center
        return a, slope, offset

    def conv_grad(act_of, v_of, name):
        lane = lax.broadcasted_iota(jnp.int32, (64, 256), 1) // 64

        def block(a):
            for tap in range(9):
                dense = tn(
                    both(lambda c: act_of(c, tap, col(a))), both(lambda c: v_of(c, tap, col(a)))
                )
                own = jnp.where(lane == 0, dense[0:64], 0.0)
                for g in range(1, 4):
                    own = own + jnp.where(lane == g, dense[64 * g : 64 * g + 64], 0.0)
                for k in range(2):
                    at = 2048 * k + 224 * tap
                    fs[pl.ds(at + a, 28, stride=4)] = own[0:28, 128 * k : 128 * k + 128]
                    fs[pl.ds(at + 112 + a, 28, stride=4)] = own[32:60, 128 * k : 128 * k + 128]

        loop(4, block)

        def shard(s):
            tiles = [
                fs[pl.ds(2048 * k + 63 * s + a, 16, stride=4)] for a in range(4) for k in range(2)
            ]
            put_shard(name, s, jnp.concatenate(tiles, 1))

        loop(SHARDS, shard)

    def outer(left_of, right_of, name):
        def block(m):
            put_rows(name, m, tn(both(lambda c: left_of(c, col(m))), both(right_of)))

        loop(SHARDS * ROWS[name][1] // 256, block)

    z, yx = digit // 4, lax.rem(digit, 4)
    bits = (1 + section, 2 - section)

    def flip(bit):
        return yx + bit * (1 - 2 * lax.rem(yx // bit, 2))

    def push(src, dst, to, sends, recvs):
        pltpu.make_async_remote_copy(
            src_ref=src, dst_ref=dst, send_sem=sends, recv_sem=recvs,
            device_id=(section, to * v + rest), device_id_type=MESH,
        ).start()

    def push_sibling(src, dst, sends, recvs):
        pltpu.make_async_remote_copy(
            src_ref=src, dst_ref=dst, send_sem=sends, recv_sem=recvs,
            device_id=(other, me), device_id_type=MESH,
        ).start()

    def arrive(ref, sem):
        pltpu.make_async_copy(ref, ref, sem).wait()

    def gather(k, phase):
        start, stop = GATHERS[k]
        rows = pl.ds(start, stop - start)
        sent = w.at[section, :, :, rows]
        amounts = (
            w.at[section, pl.ds(0, 3), 0, rows], sent.at[:, 0], sent.at[:, pl.ds(0, 2)], sent,
        )
        before = (None, 0, 1, None, 2, 3)[phase]
        if before is not None:
            arrive(amounts[before], grecv.at[k, before])
        if phase == 5:
            for at in range(4):
                arrive(amounts[at], gsend.at[k, at])
            return
        sem = (0, 1, 2, 2, 3)[phase]
        sems = (gsend.at[k, sem], grecv.at[k, sem])
        if phase == 0:
            own = w.at[section, z, yx, rows]
            for hop in range(1, 4):
                push(own, own, lax.rem(z + hop, 4) * 4 + yx, *sems)
        elif phase == 1:
            push(sent.at[:, yx], sent.at[:, yx], z * 4 + flip(bits[0]), *sems)
        elif phase in (2, 3):
            at = yx if phase == 2 else flip(bits[0])
            push(sent.at[:, at], sent.at[:, at], z * 4 + flip(bits[1]), *sems)
        else:
            push_sibling(sent, sent, *sems)

    def poll(point):
        for k, phase in GATHER_PLAN.get(point, ()):
            gather(k, phase)
        for k, phase in SCATTER_PLAN.get(point, ()):
            scatter(k, phase)

    def poll_crop(c, point):
        for one in range(2):
            name = point[0] + str(one) + point[1]
            if name in GATHER_PLAN or name in SCATTER_PLAN:
                pl.when(c == one)(lambda: poll(name))

    def crops(body, point=None):
        def run(c):
            body(c)
            if point is not None:
                poll_crop(c, (point, ""))

        loop(2, run)

    def landing(k, phase, block, count):
        last = k - CHAINED
        if phase == 0:
            if k < 4:
                return e_buf.at[pl.ds(pl.multiple_of(block * count, 16), count)]
            ref = a1 if k == 4 else hid if last == 0 else ga.at[0]
            return ref.at[
                block // 8, pl.ds(pl.multiple_of(lax.rem(block, 8) * count, 16), count)
            ]
        if phase == 1:
            if last < 0:
                return ga.at[1, block // 4, pl.ds(block % 4 * count, count)]
            ref = hid if last == 0 else ga.at[0]
            return ref.at[block // 4, pl.ds(128 + block % 4 * 16, 16)]
        if phase == 2:
            if last < 0:
                return wu1.at[pl.ds(block * count, count)]
            ref = ga.at[0] if last == 0 else hid
            return ref.at[block // 2, pl.ds(192 + block % 2 * 16, 16)]
        if last >= 0:
            return wu0.at[pl.ds(64 * last + 16 * block, 16)]
        if k % 2:
            return wu1.at[pl.ds(160 + block * count, count)]
        return stage.at[block, pl.ds(0, count)]

    def landed(k, phase, count):
        return w.at[section, pl.ds(0, (4, 2, 1, 1)[phase]), pl.ds(0, (4, 4, 4, 3)[phase]), pl.ds(0, count)]

    def add_landed(k, phase, block, place_of, start, count):
        ref = landing(k, phase, block, count)
        index = (section, *place_of(block), pl.ds(start, count))
        w[index] = (w[index].astype(F32) + ref[...].astype(F32)).astype(BF16)

    def credit(at, to):
        pl.semaphore_signal(
            free.at[at], inc=1, device_id=(section, to * v + rest), device_id_type=MESH
        )

    def credit_sibling(at):
        pl.semaphore_signal(free.at[at], inc=1, device_id=(other, me), device_id_type=MESH)

    def credit_z(at):
        for hop in range(1, 4):
            credit(at, lax.rem(z + hop, 4) * 4 + yx)

    def scatter(k, phase):
        start, stop = SCATTERS[k]
        count = stop - start
        rows = pl.ds(start, count)
        first, second = flip(bits[1]), flip(bits[0])
        more = k + 1 < CHAINED
        before = (None, 0, None, 1, 2, 3)[phase]
        if before is not None:
            arrive(landed(k, before, count), rrecv.at[k, before])
        if phase == 1:
            loop(16, lambda b: add_landed(k, 0, b, lambda b: (b // 4, lax.rem(b, 4)), start, count))
            if k < 3:
                credit_sibling(0)
        elif phase == 3:
            for b in range(8):
                add_landed(k, 1, b, lambda b: (b // 2, yx if b % 2 == 0 else second), start, count)
            if more:
                credit(1, z * 4 + first)
        elif phase == 4:
            for b in range(4):
                add_landed(k, 2, b, lambda b: (b, yx), start, count)
            if more:
                credit(2, z * 4 + second)
            if k == 0:
                credit_z(5)
        elif phase == 5:
            total = w[section, z, yx, start:stop].astype(F32)
            for b in range(3):
                total = total + landing(k, 3, b, count)[...].astype(F32)
            pool[0, 1, start:stop] = total
            if k + 2 < CHAINED:
                credit_z(5 if k % 2 else 3)
            for sent in range(4):
                arrive(landed(k, sent, count), rsend.at[k, sent])
            return
        sem = (0, 1, 1, 2, 3)[phase]
        sems = (rsend.at[k, sem], rrecv.at[k, sem])
        if phase == 0:
            if k < 4 or k == CHAINED:
                pl.semaphore_wait(free.at[0 if k < 4 else 4], 1)

            def send(b):
                push_sibling(
                    w.at[other, b // 4, lax.rem(b, 4), rows], landing(k, 0, b, count), *sems
                )

            loop(16, send)
        elif phase in (1, 2):
            if k < CHAINED and phase == 1:
                pl.semaphore_wait(free.at[1], 1)
            for b in range(4 * phase - 4, 4 * phase):
                to = first if b % 2 == 0 else first + second - yx
                push(
                    w.at[section, b // 2, to, rows], landing(k, 1, b, count), z * 4 + first, *sems
                )
        elif phase == 3:
            if k < CHAINED:
                pl.semaphore_wait(free.at[2], 1)
            for b in range(4):
                push(
                    w.at[section, b, second, rows], landing(k, 2, b, count), z * 4 + second, *sems
                )
        else:
            if k < CHAINED:
                pl.semaphore_wait(free.at[5 if k % 2 else 3], 3)
            for hop in range(1, 4):
                to = lax.rem(z + hop, 4)
                push(w.at[section, to, yx, rows], landing(k, 3, hop - 1, count), to * 4 + yx, *sems)

    for copy in loads:
        copy.wait()
    shares = {}
    at = 0
    for name, ref, count in (
        ("wa0", v_wa0, 14), ("k0", v_k0, 16), ("ws", v_ws, 14), ("wd0", v_wd0, 4),
        ("wu0", v_wu0, 4), ("wc0", v_wc0, 28), ("wa1", v_wa1, 28), ("k1", v_k1, 16),
        ("wd1", v_wd1, 7), ("wu1", v_wu1, 7), ("wc1", v_wc1, 28),
    ):
        lines = LINES[ORDER_IN.index(name)]
        if len(ref.shape) == 2:
            fs[at : at + lines] = ref[...].astype(F32)
        else:
            whole, left = ref.shape[0] // 128, ref.shape[0] % 128
            fs[at : at + whole] = ref[pl.ds(0, 128 * whole)].astype(F32).reshape(whole, 128)
            rest_row = ref[pl.ds(128 * whole, left)].astype(F32).reshape(1, left)
            rest_row = jnp.concatenate([rest_row, jnp.zeros((1, 128 - left), F32)], 1)
            fs[at + whole : at + lines] = jnp.concatenate(
                [rest_row, jnp.zeros((lines - whole - 1, 128), F32)], 0
            )
        value = jnp.concatenate([fs[pl.ds(at + k, count, stride=7)] for k in range(7)], 1)
        room = 8 if count < 8 else count + -count % 16
        if room > count:
            value = jnp.concatenate([value, jnp.zeros((room - count, D), F32)], 0)
        shares[name] = value
        at += lines + -lines % 8
    load_map.wait()
    own_rows = jnp.concatenate([shares[name] for name in ORDER], 0).astype(BF16)
    for n in range(4):
        lanes = slice(256 * n, 256 * n + 256)
        w[section, z, yx, :, lanes] = nn(own_rows, e_buf[:, lanes]).astype(BF16)
    pl.semaphore_wait(barrier, MEMBERS + v - 1)
    poll("own")
    exchange = [
        to_sibling(upstream.at[theirs], up_buf.at[section], 1),
        to_sibling(features.at[theirs], x_buf.at[section], 0),
    ]
    for copy in exchange:
        copy.start()
    copies = exchange + copies
    ng[...] = jnp.zeros_like(ng)
    guard = jnp.zeros((GUARD, C), BF16)
    for ref, count in ((a0, 4), (d_buf, 2)):
        for c in range(2):
            for k in range(count):
                ref[c, k, 0:GUARD] = guard
                ref[c, k, GUARD + PX :] = guard
    for c in range(2):
        for ref in (a1, dp_buf):
            ref[c, 0:GUARD] = guard
            ref[c, GUARD + PX :] = guard

    halves = jnp.concatenate(
        [ref[...].astype(F32).reshape(1, DIN) for ref in (v_short_gain, v_short_shift)], 1
    )
    pair[section] = jnp.concatenate(
        [v_gain[k] for k in range(3)] + [v_shift[k] for k in range(3)]
        + [halves, jnp.zeros((1, D), F32)],
        0,
    )
    swap = to_sibling(pair.at[section], pair.at[section], 3)
    swap.start()
    swap.wait()
    first, second = pair[0], pair[1]
    short_gain_row = jnp.concatenate([first[6:7, 0:DIN], second[6:7, 0:DIN]], 1)
    short_shift_row = jnp.concatenate([first[6:7, DIN:], second[6:7, DIN:]], 1)
    rows = jnp.concatenate(
        [
            first[0:3], second[0:3], first[3:6], second[3:6], short_gain_row, short_shift_row,
            jnp.zeros((2, D), F32),
        ],
        0,
    )

    wide = nn(thirds(rows), e_buf[...])
    params[...] = wide[0:16] + wide[16:32] + wide[32:48]
    poll("params")

    for copy in copies:
        copy.wait()

    def gather_slices(ref, rows):
        pad = jnp.zeros((16 - rows, D), BF16)
        return jnp.concatenate(
            [jnp.concatenate([ref[:, D * j : D * j + D], pad], 0) for j in range(OUT)], 0
        )

    def cotangent(c):
        for h in range(2):
            x = gather_slices(up_buf.at[h, c], 7)
            for n in range(4):
                y = nn(x, e_buf[:, 256 * n : 256 * n + 256])
                for j in range(OUT):
                    count = 16 if h == 0 else 7
                    pool[c, 3, 16 * j + 7 * h : 16 * j + 7 * h + count, 256 * n : 256 * n + 256] = y[
                        16 * j : 16 * j + count
                    ]

    crops(cotangent, "cot")
    load_map = local_copy(expand.at[0], e_buf, 2)
    load_map.start()
    fs[...] = jnp.zeros_like(fs)
    poll("map")
    load_map.wait()

    def phases(c):
        for h in range(2):
            x = gather_slices(x_buf.at[h, c], 14)
            for n in range(4):
                y = nn(x, e_buf[:, 256 * n : 256 * n + 256])
                for j in range(OUT):
                    for k in range(2):
                        fs[pl.ds(512 * (2 * n + k) + 32 * j + 14 * h, 14)] = y[
                            16 * j : 16 * j + 14, 128 * k : 128 * k + 128
                        ]
        for q in range(2):
            def take(j):
                for k in range(8):
                    u_buf[c, q, chunk(j), 128 * k : 128 * k + 128] = fs[
                        pl.ds(512 * k + 32 * j + q, 16, stride=2)
                    ].astype(BF16)

            loop(14, take)

    crops(phases, "ph")
    load_map = local_copy(expand.at[1], e_buf, 2)
    load_map.start()
    poll("need_wa0")

    def entry_inner(c):
        for q in range(2):
            for r in range(2):
                def product(n):
                    inn[c, 2 * q + r, :, col(n)] = nn(
                        u_buf[c, q, :, 512 * r : 512 * r + 512], cols_of("wa0", col(n))
                    )

                loop(4, product)
            poll_crop(c, ("in", "ab"[q]))

        def body(j, sums):
            mask = keep(c, j)
            first, second = sums
            for k in range(4):
                value = inn[c, k, chunk(j)]
                weighted = value * mask
                first = first + fold(weighted)
                second = second + fold(weighted * value)
            return (first, second)

        sums = each_column(2, body)
        spare = lax.broadcasted_iota(jnp.int32, (1, C), 1) == 28
        ar_start(0, c, [jnp.where(spare, crop_count(c), sums[0]), sums[1]])

    crops(entry_inner, "in")
    poll("need_k0")
    build_conv("k0")
    poll("bk0")

    def entry_conv(c):
        totals = ar_wait(0, c, 2)
        count = jnp.zeros((1, C), F32) + totals[0][:, 28:29]
        cn[c, 0:1] = count
        cn[c, 1:2] = 1.0 / count
        cn[c, 2:3] = 0.25 / count
        spare = lax.broadcasted_iota(jnp.int32, (1, C), 1) == 28
        totals[0] = jnp.where(spare, 0.0, totals[0])
        set_stats(c, 0, totals, inverse_in(c), 0)
        a, shift = affine(c, 0)

        def activate(j):
            mask = keep(c, j)
            for q in range(2):
                for r in range(2):
                    z = inn[c, 2 * q + r, chunk(j)] * a + shift
                    act = mask * silu_half(z)
                    a0[c, 2 * q + r, chunk(j, GUARD)] = act.astype(BF16)
                    if q == 1:
                        d_buf[c, r, chunk(j, GUARD)] = pltpu.roll(act, 1, 0).astype(BF16)

        loop(14, activate)

        poll_crop(c, ("conv", "a"))

        def convolve(n):
            patches = []
            for tap, q, r, ta, tb in taps0():
                at = GUARD - 16 if tb == 0 else GUARD
                src = d_buf.at[c, r] if ta == 0 else a0.at[c, 2 * q + r]
                patches.append(src[at : at + PX, col(n)])
            pool[c, 0, :, col(n)] = nn(jnp.concatenate(patches, 1), kd[n])

        loop(4, convolve)
        ar_start(1, c, moment_sums(c, lambda j: pool[c, 0, chunk(j)]))

    crops(entry_conv, "conv")
    poll("need_ws")

    def strided(c):
        def product(n):
            pool[c, 2, :, col(n)] = nn(u_buf[c, 0, :, 0:512], cols_of("ws", col(n)))

        loop(4, product)
        ar_start(SHORT, c, moment_sums(c, lambda j: pool[c, 2, chunk(j)]))

    crops(strided, "str")
    build_small(0)
    poll("need_wc0")

    def entry_gate(c):
        totals = ar_wait(1, c, 2)
        set_stats(c, 1, totals, inverse_out(c), 1)
        ar_start(2, c, gate(c, 0, 1, 0, wd0, wu0, "wc0", 1))

    crops(entry_gate, "gate")
    poll("need_k1")
    build_conv("k1")
    poll("need_wa1")

    def entry_pre(c, j):
        a, shift = affine(c, 2)
        short_a, short_shift = affine(c, 3)
        return (
            pool[c, 1, chunk(j)] * a + pool[c, 2, chunk(j)] * short_a + (shift + short_shift)
        )

    def entry_out(c):
        set_stats(c, 3, ar_wait(SHORT, c, 2), inverse_out(c), 12)
        set_stats(c, 2, ar_wait(2, c, 2), inverse_out(c), 2)

        def finish(j):
            z = entry_pre(c, j)
            hid[c, chunk(j)] = (keep(c, j) * silu_half(z)).astype(BF16)

        loop(14, finish)
        poll_crop(c, ("out", "a"))

        def product(n):
            pool[c, 4, :, col(n)] = nn(hid[c], cols_of("wa1", col(n)))

        loop(4, product)
        ar_start(3, c, moment_sums(c, lambda j: pool[c, 4, chunk(j)]))

    crops(entry_out, "out")

    def body_conv(c):
        set_stats(c, 4, ar_wait(3, c, 2), inverse_out(c), 3)
        a, shift = affine(c, 4)

        def activate(j):
            z = pool[c, 4, chunk(j)] * a + shift
            act = keep(c, j) * silu_half(z)
            a1[c, chunk(j, GUARD)] = act.astype(BF16)
            d_buf[c, 0, chunk(j, GUARD)] = pltpu.roll(act, 1, 0).astype(BF16)
            d_buf[c, 1, chunk(j, GUARD)] = pltpu.roll(act, 15, 0).astype(BF16)

        loop(14, activate)
        poll_crop(c, ("bconv", "a"))

        def convolve(n):
            rows = (d_buf.at[c, 0], a1.at[c], d_buf.at[c, 1])
            patches = [
                rows[ta][16 * tb : 16 * tb + PX, col(n)] for ta in range(3) for tb in range(3)
            ]
            pool[c, 5, :, col(n)] = nn(jnp.concatenate(patches, 1), kd[n])

        loop(4, convolve)
        ar_start(4, c, moment_sums(c, lambda j: pool[c, 5, chunk(j)]))

    crops(body_conv, "bconv")
    poll("need_wc1")
    build_small(1)
    poll("small1f")

    def body_gate(c):
        set_stats(c, 5, ar_wait(4, c, 2), inverse_out(c), 4)
        ar_start(5, c, gate(c, 1, 5, 5, wd1, wu1, "wc1", 6))

    crops(body_gate, "bgate")

    def body_out(c):
        set_stats(c, 6, ar_wait(5, c, 2), inverse_out(c), 5)
        a, shift = affine(c, 6)
        center, scaling = hat_of(c, 6)

        def finish(j, sums):
            value = pool[c, 6, chunk(j)]
            z = value * a + shift + 0.5 * hid[c, chunk(j)].astype(F32)
            mask = keep(c, j)
            t = jnp.tanh(z)
            dp_buf[c, chunk(j, GUARD)] = (mask * (z * (1.0 + t))).astype(BF16)
            d_pre = pool[c, 3, chunk(j)] * (
                mask * (0.5 * (1.0 + t) * (1.0 + z * (1.0 - t)))
            )
            pool[c, 3, chunk(j)] = d_pre
            return (sums[0] + fold(d_pre), sums[1] + fold(d_pre * (value - center)))

        ar_start(6, c, scaled(each_column(2, finish), scaling))

    crops(body_out, "bo")
    load_map.wait()

    def narrow(value, store):
        for start, width in ((0, 256), (256, 256), (512, 256), (768, 128)):
            store(start, width, nt(value, e_buf[start : start + width]))

    def body_emit(c):
        def store(start, width, y):
            for j in range(OUT):
                for h in range(2):
                    up_buf[h, c, :, D * j + start : D * j + start + width] = y[
                        16 * j + 7 * h : 16 * j + 7 * h + 7
                    ].astype(BF16)

        narrow(dp_of(c), store)

    loop(2, body_emit)
    poll("bemit")
    out_copies = [
        to_sibling(up_buf.at[other], out.at[mine], 2),
        local_copy(up_buf.at[section], out.at[mine], 1),
    ]
    for copy in out_copies:
        copy.start()

    credit_sibling(0)

    def body_back_out(c):
        a, slope, offset = norm_coefficients(c, 6, ar_wait(6, c, 2), inverse_out(c), 5, 0)

        def project(j):
            value = pool[c, 6, chunk(j)]
            dp_buf[c, chunk(j, GUARD)] = (
                keep(c, j) * (a * pool[c, 3, chunk(j)] + slope * value + offset)
            ).astype(BF16)

        loop(14, project)
        ar_start(7, c, ungate(c, 1, 5, 5, wd1, wu1, "wc1"))

    crops(body_back_out, "bout")
    credit(2, z * 4 + flip(bits[0]))
    credit_z(3)
    outer(lambda c, l: ga[1, c, :, l], dp_of, "wc1")
    credit(1, z * 4 + flip(bits[1]))
    small_grads(1)
    poll("small1")

    def conv_cotangent(c, index, conv_k, a, slope, offset, versions):
        def body(j):
            d = keep(c, j) * (a * pool[c, 7, chunk(j)] + slope * pool[c, conv_k, chunk(j)] + offset)
            d_buf[c, 0, chunk(j, GUARD)] = d.astype(BF16)
            d_buf[c, 1, chunk(j, GUARD)] = pltpu.roll(d, 15, 0).astype(BF16)
            if versions == 3:
                dp_buf[c, chunk(j, GUARD)] = pltpu.roll(d, 1, 0).astype(BF16)

        loop(14, body)

    def v_body(c, tap, lanes):
        ta, tb = tap // 3, tap % 3
        ref = (d_buf.at[c, 1], d_buf.at[c, 0], dp_buf.at[c])[ta]
        return ref[32 - 16 * tb : 32 - 16 * tb + PX, lanes]

    def v_entry(c, tap, lanes):
        ta, tb = tap // 3, tap % 3
        at = 32 if tb == 0 else 16
        return d_buf[c, 1 if ta == 0 else 0, at : at + PX, lanes]

    def body_back_conv(c):
        a, slope, offset = norm_coefficients(c, 5, ar_wait(7, c, 2), inverse_out(c), 4, 0)
        conv_cotangent(c, 5, 5, a, slope, offset, 3)

        def back(n):
            total = nt(v_body(c, 0, col(n)), kd[n, 0:256])
            for tap in range(1, 9):
                total = total + nt(v_body(c, tap, col(n)), kd[n, 256 * tap : 256 * tap + 256])
            pool[c, 7, :, col(n)] = total

        loop(4, back)
        poll_crop(c, ("bback", "a"))
        a, shift = affine(c, 4)
        center, scaling = hat_of(c, 4)

        def body(j, sums):
            value = pool[c, 4, chunk(j)]
            z = value * a + shift
            d = pool[c, 7, chunk(j)] * (keep(c, j, 0.5) * slope_half(z))
            pool[c, 7, chunk(j)] = d
            return (sums[0] + fold(d), sums[1] + fold(d * (value - center)))

        ar_start(8, c, scaled(each_column(2, body), scaling))

    crops(body_back_conv, "bback")
    conv_grad(lambda c, tap, l: a1[c, GUARD : GUARD + PX, l], v_body, "k1")
    poll("k1")

    def body_back_in(c):
        a, slope, offset = norm_coefficients(c, 4, ar_wait(8, c, 2), inverse_out(c), 3, 0)

        def body(j):
            dp_buf[c, chunk(j, GUARD)] = (
                keep(c, j) * (a * pool[c, 7, chunk(j)] + slope * pool[c, 4, chunk(j)] + offset)
            ).astype(BF16)

        loop(14, body)

        def back(n):
            pool[c, 3, :, col(n)] = (
                (nt(dp_of(c), rows_of("wa1", n)) + pool[c, 3, :, col(n)]).astype(BF16).astype(F32)
            )

        loop(4, back)
        poll_crop(c, ("bin", "a"))
        center, scaling = hat_of(c, 2)
        short_center, short_scaling = hat_of(c, 3)

        def pre(j, sums):
            z = entry_pre(c, j)
            d = pool[c, 3, chunk(j)] * (keep(c, j, 0.5) * slope_half(z))
            pool[c, 3, chunk(j)] = d
            return (
                sums[0] + fold(d),
                sums[1] + fold(d * (pool[c, 1, chunk(j)] - center)),
                sums[2] + fold(d * (pool[c, 2, chunk(j)] - short_center)),
            )

        sums = each_column(3, pre)
        ar_start(9, c, scaled(sums, scaling, short_scaling))

    crops(body_back_in, "bin")
    outer(lambda c, l: hid[c, :, l], dp_of, "wa1")
    poll("wa1")
    build_conv("k0")
    poll("bk0b")

    def entry_back_out(c):
        totals = ar_wait(9, c, 3)
        a, slope, offset = norm_coefficients(c, 2, totals[0:2], inverse_out(c), 2, 0)
        short = norm_coefficients(c, 3, [totals[0], totals[2]], inverse_out(c), 12, 0)

        def project(j):
            mask = keep(c, j)
            d = pool[c, 3, chunk(j)]
            dp_buf[c, chunk(j, GUARD)] = (
                mask * (a * d + slope * pool[c, 1, chunk(j)] + offset)
            ).astype(BF16)
            hid[c, chunk(j)] = (
                mask * (short[0] * d + short[1] * pool[c, 2, chunk(j)] + short[2])
            ).astype(BF16)

        loop(14, project)

        def back(n):
            pool[c, 2, :, col(n)] = nt(hid[c], rows_of("ws", n))

        loop(2, back)
        ar_start(10, c, ungate(c, 0, 1, 0, wd0, wu0, "wc0"))

    crops(entry_back_out, "eback")
    outer(lambda c, l: ga[0, c, :, l], dp_of, "wc0")
    poll("wc0")
    outer(lambda c, l: u_buf[c, 0, :, l], lambda c: hid[c], "ws")
    credit_sibling(4)
    small_grads(0)
    poll("small0")

    def entry_back_conv(c):
        a, slope, offset = norm_coefficients(c, 1, ar_wait(10, c, 2), inverse_out(c), 1, 0)
        conv_cotangent(c, 1, 0, a, slope, offset, 2)
        for q in range(2):
            for r in range(2):
                def back(n):
                    total = None
                    for tap, tq, tr, ta, tb in taps0():
                        if (tq, tr) == (q, r):
                            term = nt(v_entry(c, tap, col(n)), kd[n, 256 * tap : 256 * tap + 256])
                            total = term if total is None else total + term
                    pool[c, 4 + 2 * q + r, :, col(n)] = total

                loop(4, back)
            poll_crop(c, ("econv", "ab"[q]))
        a, shift = affine(c, 0)
        center, scaling = hat_of(c, 0)

        def body(j, sums):
            mask = keep(c, j, 0.5)
            first, second = sums
            for k in range(4):
                value = inn[c, k, chunk(j)]
                z = value * a + shift
                d = pool[c, 4 + k, chunk(j)] * (mask * slope_half(z))
                pool[c, 4 + k, chunk(j)] = d
                first = first + fold(d)
                second = second + fold(d * (value - center))
            return (first, second)

        ar_start(11, c, scaled(each_column(2, body), scaling))

    crops(entry_back_conv, "econv")

    def act_entry(c, tap, lanes):
        q = 0 if tap // 3 == 1 else 1
        r = 0 if tap % 3 == 1 else 1
        return a0[c, 2 * q + r, GUARD : GUARD + PX, lanes]

    conv_grad(act_entry, v_entry, "k0")
    poll("k0")
    load_map = local_copy(expand.at[0], e_buf, 2)
    load_map.start()
    for copy in out_copies:
        copy.wait()

    def entry_back_in(c):
        a, slope, offset = norm_coefficients(c, 0, ar_wait(11, c, 2), inverse_in(c), 0, 0)

        def body(j):
            mask = keep(c, j)
            for k in range(4):
                a0[c, k, chunk(j, GUARD)] = (
                    mask * (a * pool[c, 4 + k, chunk(j)] + slope * inn[c, k, chunk(j)] + offset)
                ).astype(BF16)

        loop(14, body)

    loop(2, entry_back_in)
    poll("d")
    swap = to_sibling(ng, ng_in, 3)
    swap.start()

    def input_grad(m):
        total = None
        for q in range(2):
            for r in range(2):
                at = pl.ds(pl.multiple_of(512 * r + 256 * m, 256), 256)
                term = tn(
                    both(lambda c: u_buf[c, q, :, at]),
                    both(lambda c: a0[c, 2 * q + r, GUARD : GUARD + PX]),
                )
                total = term if total is None else total + term
        return total

    def input_block(m):
        dp_buf[m] = rows_of("wa0", m)
        put_rows("wa0", m, input_grad(m))

    loop(2, input_block)
    poll("wa0")

    def entry_back_input(c):
        for q in range(2):
            for r in range(2):
                def back(n):
                    total = nt(a0[c, 2 * q + r, GUARD : GUARD + PX], dp_buf[n])
                    if q == 0 and r == 0:
                        total = total + pool[c, 2, :, col(n)]
                    at = pl.ds(pl.multiple_of(512 * r + 256 * n, 256), 256)
                    d_buf[c, q, 0:PX, at] = total.astype(BF16)

                loop(2, back)
            if q == 0:
                poll_crop(c, ("input", "a"))

    crops(entry_back_input, "input")

    def entry_emit(c):
        for q in range(2):
            def store(start, width, y):
                for j in range(OUT):
                    for k in range(width // 128):
                        fs[pl.ds(512 * (start // 128 + k) + 32 * j + q, 14, stride=2)] = y[
                            16 * j : 16 * j + 14, 128 * k : 128 * k + 128
                        ]

            narrow(d_buf[c, q, 0:PX], store)
        poll_crop(c, ("emit", "a"))
        for h in range(2):
            for j in range(OUT):
                for k in range(7):
                    x_buf[h, c, :, D * j + 128 * k : D * j + 128 * k + 128] = fs[
                        512 * k + 32 * j + 14 * h : 512 * k + 32 * j + 14 * h + 14
                    ].astype(BF16)

    load_map.wait()
    crops(entry_emit, "emit")
    last = [
        to_sibling(x_buf.at[other], grad.at[mine], 4),
        local_copy(x_buf.at[section], grad.at[mine], 0),
    ]
    for copy in last:
        copy.start()
    swap.wait()
    ng[...] = ng[...] + ng_in[...]
    last.append(local_copy(ng, result.at[pl.ds(192, 16)], 1))
    last[-1].start()
    poll("tail")
    last.append(local_copy(pool.at[0, 1, pl.ds(0, 192)], result.at[pl.ds(0, 192)], 2))
    last[-1].start()
    for copy in last:
        copy.wait()


def thirds(value):
    high = value.astype(BF16)
    left = value - high.astype(F32)
    middle = left.astype(BF16)
    return jnp.concatenate([high, middle, (left - middle.astype(F32)).astype(BF16)], 0)


def final_kernel(result, narrow_map, *refs):
    flat_out, (gain_out, shift_out, short_gain_out, short_shift_out) = refs[:11], refs[11:15]
    flat, (gain, shift, short_gain, short_shift), sems = refs[15:26], refs[26:30], refs[30]
    section = lax.axis_index("section")
    total = nt(thirds(result[192:208]), narrow_map[...])
    total = total[0:16] + total[16:32] + total[32:48]

    def own(top, low):
        return jnp.where(section == 0, top, low)

    for k in range(3):
        gain[k] = own(total[k : k + 1], total[k + 3 : k + 4])
        shift[k] = own(total[k + 6 : k + 7], total[k + 9 : k + 10])
    short_gain[...] = own(total[12:13, 0:DIN], total[12:13, DIN:])
    short_shift[...] = own(total[13:14, 0:DIN], total[13:14, DIN:])
    total = result[0:192]
    high = total.astype(BF16)
    low = (total - high.astype(F32)).astype(BF16)
    final = nt(high, narrow_map[...]) + nt(low, narrow_map[...])
    for (name, count), ref in zip(
        (
            ("wa0", 14), ("k0", 16), ("ws", 14), ("wd0", 4), ("wu0", 4), ("wc0", 28), ("wa1", 28),
            ("k1", 16), ("wd1", 7), ("wu1", 7), ("wc1", 28),
        ),
        flat,
    ):
        if name[1] in "du":
            at = ROWS["misc" + name[2]][0] + (8 if name[1] == "u" else 0)
        else:
            at = ROWS[name][0]
        for k in range(7):
            ref[pl.ds(k, count, stride=7)] = final[at : at + count, 128 * k : 128 * k + 128]
    copies = [
        pltpu.make_async_copy(src, dst, sems.at[at])
        for at, (src, dst) in enumerate(
            zip((*flat, gain, shift, short_gain, short_shift), (*flat_out, gain_out, shift_out, short_gain_out, short_shift_out))
        )
    ]
    for copy in copies:
        copy.start()
    for copy in copies:
        copy.wait()


def final_call(result, narrow_map):
    vmem = pl.BlockSpec(memory_space=pltpu.VMEM)
    shapes = [(count, 128) for count in LINES] + [(3, 1, D), (3, 1, D), (1, DIN), (1, DIN)]
    return pl.pallas_call(
        final_kernel,
        out_shape=[jax.ShapeDtypeStruct(shape, F32) for shape in shapes],
        in_specs=[vmem, vmem],
        out_specs=[pl.BlockSpec(memory_space=pl.ANY)] * 15,
        scratch_shapes=[pltpu.VMEM(shape, F32) for shape in shapes]
        + [pltpu.SemaphoreType.DMA((15,))],
        compiler_params=pltpu.CompilerParams(vmem_limit_bytes=16 << 20),
    )(result, narrow_map)


def lane_maps():
    at = np.arange(D)
    first = np.zeros((D, C), np.float32)
    first[at, at // 14 * 16 + at % 14] = 1
    second = np.zeros((D, C), np.float32)
    second[at, at // 28 * 32 + at % 28] = 1
    return np.stack([first, second])


def main_call(n_dp, *args):
    v = n_dp // MEMBERS
    any_space = pl.BlockSpec(memory_space=pl.ANY)
    smem = pl.BlockSpec(memory_space=pltpu.SMEM)
    shape = lambda *s, dtype=BF16: jax.ShapeDtypeStruct(s, dtype)
    outs = [
        shape(4, 7, 12544), shape(4, 14, 12544), shape(208, C, dtype=F32),
    ]
    dma = pltpu.SemaphoreType.DMA
    scratch = [
        pltpu.VMEM((2, 4, PX, C), F32),
        pltpu.VMEM((2, 8, PX, C), F32),
        pltpu.VMEM((2, 2, PX, C), BF16),
        pltpu.VMEM((2, 4, PX + 2 * GUARD, C), BF16),
        pltpu.VMEM((2, PX + 2 * GUARD, C), BF16),
        pltpu.VMEM((2, 2, PX + 2 * GUARD, C), BF16),
        pltpu.VMEM((2, 2, PX, C), BF16),
        pltpu.VMEM((2, PX, C), BF16),
        pltpu.VMEM((2, PX + 2 * GUARD, C), BF16),
        pltpu.VMEM((2, 2, 14, 12544), BF16),
        pltpu.VMEM((2, 2, 7, 12544), BF16),
        pltpu.VMEM((4096, 128), F32),
        pltpu.VMEM((4, 2304, 256), BF16),
        pltpu.VMEM((D, C), BF16),
        pltpu.VMEM((2, 4, 4, 192, C), BF16),
        pltpu.VMEM((C, 128), BF16),
        pltpu.VMEM((128, C), BF16),
        pltpu.VMEM((C, 256), BF16),
        pltpu.VMEM((256, C), BF16),
        pltpu.VMEM((3, 48, C), BF16),
        pltpu.VMEM((16, C), F32),
        pltpu.VMEM((2, 8, D), F32),
        pltpu.VMEM((2, 7, 8, C), F32),
        pltpu.VMEM((2, 2, 8, C), F32),
        pltpu.VMEM((2, 8, C), F32),
        pltpu.VMEM((16, C), F32),
        pltpu.VMEM((16, C), F32),
        pltpu.VMEM((2, 2, MEMBERS, 2, C), F32),
        pltpu.VMEM((2, MEMBERS, 2, C), F32),
        pltpu.VMEM((2, 2, MEMBERS, 32, 128), BF16),
        pltpu.VMEM((3, 2, v, 4, C), F32),
        pltpu.VMEM((3, 1, D), F32),
        pltpu.VMEM((3, 1, D), F32),
        pltpu.VMEM((DIN,), BF16),
        pltpu.VMEM((DIN,), BF16),
        *[pltpu.VMEM(shard.shape, BF16) for shard in args[8:]],
        dma((16,)), dma((3, 2)), dma((3, 2)), dma((3, 2)), dma((3, 2)), dma((5,)), dma((5,)), dma((4,)),
        dma((7, 4)), dma((7, 4)), dma((7, 4)), dma((7, 4)), pltpu.SemaphoreType.REGULAR((6,)),
    ]
    return pl.pallas_call(
        functools.partial(main_kernel, n_dp),
        out_shape=outs,
        in_specs=[any_space, any_space, smem] + [any_space] * 16,
        out_specs=[any_space] * 3,
        scratch_shapes=scratch,
        compiler_params=pltpu.CompilerParams(
            collective_id=1, has_side_effects=True, vmem_limit_bytes=64 << 20
        ),
    )(*args)


def local(
    features, crop_side, upstream,
    entry_in, entry_group, entry_out, entry_down, entry_up, shortcut_weight,
    body_in, body_group, body_out, body_down, body_up,
    norm_gain, norm_shift, shortcut_gain, shortcut_shift,
):
    n_dp = lax.axis_size("dp")
    v = n_dp // MEMBERS
    groups = [[v * member + k for k in range(v)] for member in range(MEMBERS)]
    shards = (
        entry_in, entry_group, shortcut_weight, entry_down, entry_up, entry_out,
        body_in, body_group, body_down, body_up, body_out,
    )

    def lines(shard, count):
        if v > 1:
            shard = lax.all_gather(shard, "dp", axis_index_groups=groups, axis=0, tiled=True)
        return shard.reshape(count, 128) if shard.shape[0] == 128 * count else shard

    maps = jnp.asarray(lane_maps(), BF16)
    output, d_features, result = main_call(
        n_dp, features, upstream, crop_side, maps,
        norm_gain.transpose(1, 0, 2), norm_shift.transpose(1, 0, 2),
        shortcut_gain, shortcut_shift,
        *(lines(shard, count) for shard, count in zip(shards, LINES)),
    )
    results = final_call(result, jnp.asarray(lane_maps()[1], BF16))

    def share(values, shard):
        values = values.reshape(-1)[: v * shard.shape[0]]
        if v > 1:
            values = lax.psum_scatter(
                values, "dp", scatter_dimension=0, axis_index_groups=groups, tiled=True
            )
        return values

    wa0, k0, ws, wd0, wu0, wc0, wa1, k1, wd1, wu1, wc1 = (
        share(values, shard) for values, shard in zip(results[:11], shards)
    )
    gains, shifts, short_gain, short_shift = results[11:15]
    return (
        output, d_features, wa0, k0, wc0, wd0, wu0, ws, wa1, k1, wc1, wd1, wu1,
        gains.transpose(1, 0, 2), shifts.transpose(1, 0, 2),
        short_gain[0], short_shift[0],
    )


def solution(mesh):
    rows = P("dp", "section", None)
    flat = P(("section", "dp"))
    params = (P("section", None, None), P("section", None, None), P("section"), P("section"))
    return jax.shard_map(
        local,
        mesh=mesh,
        in_specs=(rows, P("dp"), rows) + (flat,) * 11 + params,
        out_specs=(rows, rows) + (flat,) * 11 + params,
        check_vma=False,
    )
```

```python
import functools

import jax
import jax.numpy as jnp
import numpy as np
from jax import lax
from jax.experimental import pallas as pl
from jax.experimental.pallas import tpu as pltpu
from jax.sharding import PartitionSpec as P

D = 896
DIN = 448
OUT = 14
IN = 28
SE0 = 112
SE1 = 224
EPSILON = 1e-05
F32 = jnp.float32
BF16 = jnp.bfloat16
MESH = pl.DeviceIdType.MESH
C = 1024
PX = 224
GUARD = 16
MEMBERS = 16
SHORT = 12
SHARDS = 32
ROWS = {
    "wa0": (0, 16), "k0": (16, 16), "ws": (32, 16), "misc0": (48, 16), "wc0": (64, 32),
    "k1": (96, 16), "wa1": (112, 32), "misc1": (144, 16), "wc1": (160, 32),
}
ORDER = ("wa0", "k0", "ws", "wd0", "wu0", "wc0", "k1", "wa1", "wd1", "wu1", "wc1")
ORDER_IN = ("wa0", "k0", "ws", "wd0", "wu0", "wc0", "wa1", "k1", "wd1", "wu1", "wc1")
LINES = (98, 112, 98, 28, 28, 196, 196, 112, 49, 49, 196)
GATHERS = ((0, 16), (16, 32), (32, 64), (64, 96), (96, 112), (112, 144), (144, 192))
SCATTERS = (
    (144, 192), (96, 112), (112, 144), (64, 96), (32, 64), (16, 32), (0, 16)
)
CHAINED = 5
GATHER_PLAN = {
    "own": ((0, 0),),
    "params": ((1, 0),),
    "cot0": ((2, 0), (3, 0), (0, 1), (4, 0), (0, 2)),
    "cot1": ((1, 1), (0, 3)),
    "map": ((2, 1), (5, 0)),
    "ph0": ((0, 4), (1, 2)),
    "ph1": ((1, 3),),
    "in0b": ((2, 2), (3, 1)),
    "in0": ((2, 3),),
    "need_wa0": ((0, 5),),
    "in1a": ((1, 4),),
    "in1": ((1, 5), (6, 0), (3, 2), (5, 1), (3, 3)),
    "in1b": ((4, 1),),
    "conv1a": ((2, 4),),
    "bk0": ((4, 2),),
    "conv0a": ((4, 3),),
    "need_ws": ((3, 4), (2, 5)),
    "conv1": ((5, 2),),
    "str0": ((5, 3),),
    "str1": ((6, 1),),
    "need_wc0": ((3, 5), (4, 4)),
    "gate1": ((5, 4),),
    "need_k1": ((6, 2),),
    "out0": ((6, 3),),
    "need_wa1": ((5, 5),),
    "gate1a": ((4, 5),),
    "bconv0a": ((6, 4),),
    "bconv1": ((6, 5),),
}
SCATTER_PLAN = {
    "small1": ((0, 0),),
    "bback0": ((0, 1),),
    "bback1": ((0, 2),),
    "bin0a": ((1, 0),),
    "bin1a": ((0, 3),),
    "wa1": ((1, 1),),
    "bk0b": ((1, 2),),
    "eback0a": ((0, 4), (2, 0)),
    "eback0": ((1, 3),),
    "eback1a": ((2, 1),),
    "eback1": ((2, 2),),
    "wc0": ((1, 4),),
    "small0": ((4, 0), (3, 0)),
    "econv0a": ((2, 3),),
    "econv0": ((0, 5), (1, 5)),
    "econv0b": ((3, 1), (3, 2)),
    "econv1a": ((2, 4),),
    "econv1b": ((3, 3),),
    "econv1": ((4, 1), (4, 2)),
    "d": ((3, 4),),
    "k0": ((5, 0),),
    "wa0": ((4, 3), (5, 1), (6, 0), (5, 2)),
    "input0a": ((2, 5), (6, 1), (6, 2)),
    "input0": ((4, 4), (5, 3), (6, 3), (5, 4)),
    "emit0a": ((4, 5), (3, 5)),
    "input1": ((6, 4),),
    "emit1a": ((5, 5),),
    "tail": ((6, 5),),
}


def dot(a, b, dims):
    return lax.dot_general(a, b, ((dims[:1], dims[1:]), ((), ())), preferred_element_type=F32)


def nn(a, b):
    return dot(a, b, (1, 0))


def nt(a, b):
    return dot(a, b, (1, 1))


def tn(a, b):
    return dot(a, b, (0, 0))


def sig(z):
    return jnp.tanh(z * 0.5) * 0.5 + 0.5


def slope_of(z, s):
    return s * (1.0 + z * (1.0 - s))


def silu_half(h):
    return h * (1.0 + jnp.tanh(h))


def slope_half(h):
    t = jnp.tanh(h)
    return (1.0 + t) * (1.0 + h * (1.0 - t))


def split_rows(rows):
    high = [r.astype(BF16).astype(F32) for r in rows]
    low = [r - h for r, h in zip(rows, high)]
    return high, low


def stacked(rows):
    pad = jnp.zeros((16 - len(rows), rows[0].shape[1]), F32)
    return jnp.concatenate(list(rows) + [pad], 0).astype(BF16)


def row_dot(row, weight, mul):
    high, low = split_rows([row])
    both = mul(stacked(high + low), weight)
    return both[0:1] + both[1:2]


def col(n, width=256):
    return pl.ds(pl.multiple_of(n * width, width), width)


def chunk(j, base=0):
    return pl.ds(pl.multiple_of(j * 16 + base, 16), 16)


def loop(count, body):
    def step(i, carry):
        body(i)
        return carry

    lax.fori_loop(0, count, step, 0)


def main_kernel(
    n_dp, features, upstream, side_ref, expand, gain_in, shift_in, short_gain_in, short_shift_in,
    l_wa0, l_k0, l_ws, l_wd0, l_wu0, l_wc0, l_wa1, l_k1, l_wd1, l_wu1, l_wc1,
    out, grad, result,
    inn, pool, u_buf, a0, a1, d_buf, ga, hid, dp_buf, x_buf, up_buf, fs, kd, e_buf,
    w, wd0, wu0, wd1, wu1, stage, params, pair, st, sv, cn, ng, ng_in, ar2, ars, arh, arv,
    v_gain, v_shift, v_short_gain, v_short_shift, v_wa0, v_k0, v_ws, v_wd0, v_wu0, v_wc0, v_wa1, v_k1, v_wd1, v_wu1,
    v_wc1, isem, asend, arecv, vsend, vrecv, xsend, xrecv, lsem, gsend, grecv, rsend, rrecv, free,
):
    loads = [
        pltpu.make_async_copy(src, dst, isem.at[at])
        for at, (src, dst) in enumerate(
            (
                (l_wa0, v_wa0), (l_k0, v_k0), (l_ws, v_ws), (l_wd0, v_wd0), (l_wu0, v_wu0),
                (l_wc0, v_wc0), (l_wa1, v_wa1), (l_k1, v_k1), (l_wd1, v_wd1), (l_wu1, v_wu1),
                (l_wc1, v_wc1), (gain_in, v_gain), (shift_in, v_shift),
                (short_gain_in, v_short_gain), (short_shift_in, v_short_shift),
            )
        )
    ]
    load_map = pltpu.make_async_copy(expand.at[1], e_buf, isem.at[15])
    for copy in loads + [load_map]:
        copy.start()
    section = lax.axis_index("section")
    me = lax.axis_index("dp")
    v = n_dp // MEMBERS
    digit, rest = me // v, lax.rem(me, v)
    other = 1 - section

    def member(hop):
        return lax.rem(digit + hop, MEMBERS) * v + rest

    def near(hop):
        return digit * v + lax.rem(rest + hop, v)

    barrier = pltpu.get_barrier_semaphore()

    def greet(hop):
        pl.semaphore_signal(barrier, inc=1, device_id=(section, member(hop + 1)), device_id_type=MESH)

    def greet_near(hop):
        pl.semaphore_signal(barrier, inc=1, device_id=(section, near(hop + 1)), device_id_type=MESH)

    loop(MEMBERS - 1, greet)
    if v > 1:
        loop(v - 1, greet_near)
    pl.semaphore_signal(barrier, inc=1, device_id=(other, me), device_id_type=MESH)
    def local_copy(src, dst, sem=0):
        return pltpu.make_async_copy(src, dst, lsem.at[sem])

    def to_sibling(src, dst, at):
        return pltpu.make_async_remote_copy(
            src_ref=src, dst_ref=dst, send_sem=xsend.at[at], recv_sem=xrecv.at[at],
            device_id=(other, me), device_id_type=MESH,
        )

    mine = pl.ds(2 * section, 2)
    theirs = pl.ds(2 * other, 2)
    copies = [
        local_copy(features.at[mine], x_buf.at[section], 0),
        local_copy(upstream.at[mine], up_buf.at[section], 1),
    ]
    for copy in copies:
        copy.start()

    def dp_of(c):
        return dp_buf[c, GUARD : GUARD + PX]

    def half_side(c):
        return side_ref[2 * section + c] // 2

    def keep(c, j, weight=1.0):
        half = half_side(c)
        bound = jnp.where(j < half, half, 0)
        tile = jnp.where(lax.broadcasted_iota(jnp.int32, (16, 128), 0) < bound, weight, 0.0)
        return jnp.concatenate([tile] * (C // 128), 1)

    def crop_count(c):
        half = half_side(c)
        return (half * half).astype(F32)

    def ar_slots(n, c):
        if 6 <= n < SHORT:
            return arh.at[n % 2, c, :, pl.ds(0, 32 if n == 9 else 16)]
        return ars.at[c] if n == SHORT else ar2.at[n % 2, c]

    def ar_lane(n):
        return 2 if n == SHORT else n % 2

    def ar_start(n, c, rows):
        slots = ar_slots(n, c)
        if 6 <= n < SHORT:
            tiles = [row[:, 128 * k : 128 * k + 128] for row in rows for k in range(8)]
            if n == 9:
                tiles.append(jnp.zeros((8, 128), F32))
            slots[digit] = jnp.concatenate(tiles, 0).astype(BF16)
        else:
            slots[digit] = jnp.concatenate(rows, 0)

        def send(hop):
            pltpu.make_async_remote_copy(
                src_ref=slots.at[digit], dst_ref=slots.at[digit], send_sem=asend.at[ar_lane(n), c],
                recv_sem=arecv.at[ar_lane(n), c], device_id=(section, member(hop + 1)),
                device_id_type=MESH,
            ).start()

        loop(MEMBERS - 1, send)

    def ar_wait(n, c, rows):
        slots = ar_slots(n, c)
        arrived = slots.at[pl.ds(0, MEMBERS - 1)]
        pltpu.make_async_copy(arrived, arrived, asend.at[ar_lane(n), c]).wait()
        pltpu.make_async_copy(arrived, arrived, arecv.at[ar_lane(n), c]).wait()
        total = slots[0].astype(F32)
        for k in range(1, MEMBERS):
            total = total + slots[k].astype(F32)
        if 6 <= n < SHORT:
            total = jnp.concatenate(
                [
                    jnp.concatenate([total[8 * r + k : 8 * r + k + 1] for k in range(8)], 1)
                    for r in range(rows)
                ],
                0,
            )
        if v > 1:
            again = arv.at[ar_lane(n), c]
            spare = [jnp.zeros((4 - rows, C), F32)] if rows < 4 else []
            again[rest] = jnp.concatenate([total] + spare, 0)

            def send(hop):
                pltpu.make_async_remote_copy(
                    src_ref=again.at[rest], dst_ref=again.at[rest], send_sem=vsend.at[ar_lane(n), c],
                    recv_sem=vrecv.at[ar_lane(n), c], device_id=(section, near(hop + 1)),
                    device_id_type=MESH,
                ).start()

            loop(v - 1, send)
            arrived = again.at[pl.ds(0, v - 1)]
            pltpu.make_async_copy(arrived, arrived, vsend.at[ar_lane(n), c]).wait()
            pltpu.make_async_copy(arrived, arrived, vrecv.at[ar_lane(n), c]).wait()
            total = again[0]
            for k in range(1, v):
                total = total + again[k]
        return [total[k : k + 1] for k in range(rows)]

    def down(sums):
        return jnp.sum(sums, axis=0, keepdims=True)

    def fold(value):
        return value[0:8] + value[8:16]

    def zeros(count):
        return tuple(jnp.zeros((8, C), F32) for _ in range(count))

    def each_column(count, body):
        sums = lax.fori_loop(0, 14, body, zeros(count))
        return [down(one) for one in sums]

    def scaled(sums, *factors):
        return [sums[0]] + [one * factor for one, factor in zip(sums[1:], factors)]

    def moment_sums(c, value_of):
        def body(j, sums):
            value = value_of(j)
            weighted = value * keep(c, j)
            return (sums[0] + fold(weighted), sums[1] + fold(weighted * value))

        return each_column(2, body)

    def set_stats(c, index, totals, inverse, gain_row):
        center = totals[0] * inverse
        scaling = lax.rsqrt(totals[1] * inverse - center * center + EPSILON)
        gain = params[gain_row : gain_row + 1] * scaling
        shift_row = gain_row + 6 if gain_row < 6 else gain_row + 1
        st[c, index, 0:1] = center
        st[c, index, 1:2] = scaling
        st[c, index, 2:3] = gain
        st[c, index, 3:4] = params[shift_row : shift_row + 1] - center * gain
        st[c, index, 4:6] = st[c, index, 2:4] * 0.5

    def affine(c, index):
        return st[c, index, 4:5], st[c, index, 5:6]

    def hat_of(c, index):
        return st[c, index, 0:1], st[c, index, 1:2]

    def inverse_out(c):
        return cn[c, 1:2]

    def inverse_in(c):
        return cn[c, 2:3]

    def place(shard):
        return shard // 16, lax.rem(shard // 4, 4), lax.rem(shard, 4)

    def cols_of(name, lanes):
        at, count = ROWS[name]
        value = w[:, :, :, at : at + count, lanes]
        return value.reshape(SHARDS * count, value.shape[-1])

    def rows_index(name, n):
        at, count = ROWS[name]
        if count == 16:
            return (n, slice(None), slice(None), slice(at, at + 16))
        return (n // 2, pl.ds(2 * lax.rem(n, 2), 2), slice(None), slice(at, at + 32))

    def rows_of(name, n):
        return w[rows_index(name, n)].reshape(256, C)

    def put_rows(name, n, value):
        shape = (4, 4, 16, C) if ROWS[name][1] == 16 else (2, 4, 32, C)
        w[rows_index(name, n)] = value.astype(BF16).reshape(shape)

    def shard_rows(name, shard):
        at, count = ROWS[name]
        return w[(*place(shard), slice(at, at + count))].astype(F32)

    def put_shard(name, shard, value):
        at, count = ROWS[name]
        w[(*place(shard), slice(at, at + count))] = value.astype(BF16)

    def tile(k):
        return slice(128 * k, 128 * k + 128)

    def build_conv(name):
        def shard(s):
            rows = shard_rows(name, s)
            for a in range(4):
                for k in range(2):
                    fs[pl.ds(2048 * k + 63 * s + a, 16, stride=4)] = rows[:, tile(2 * a + k)]

        loop(SHARDS, shard)
        lane = lax.broadcasted_iota(jnp.int32, (64, 256), 1) // 64

        def block(a):
            for tap in range(9):
                tiles = []
                for k in range(2):
                    at = 2048 * k + 224 * tap
                    tiles.append(
                        jnp.concatenate(
                            [
                                fs[pl.ds(at + a, 28, stride=4)],
                                jnp.zeros((4, 128), F32),
                                fs[pl.ds(at + 112 + a, 28, stride=4)],
                                jnp.zeros((4, 128), F32),
                            ],
                            0,
                        )
                    )
                dense = jnp.concatenate(tiles, 1)
                for g in range(4):
                    kd[a, 256 * tap + 64 * g : 256 * tap + 64 * g + 64] = jnp.where(
                        lane == g, dense, 0.0
                    ).astype(BF16)

        loop(4, block)

    def build_small(b):
        wd, wu = (wd0, wu0) if b == 0 else (wd1, wu1)
        fs[...] = jnp.zeros_like(fs)

        def shard(s):
            rows = shard_rows("misc0" if b == 0 else "misc1", s)
            if b == 0:
                for k in range(8):
                    fs[pl.ds(32 * s + k, 4, stride=8)] = rows[0:4, tile(k)]
                    fs[pl.ds(1024 + 256 * (k % 4) + 7 * s + k // 4, 4, stride=2)] = rows[
                        8:12, tile(k)
                    ]
            else:
                for k in range(8):
                    fs[pl.ds(1024 * (k % 2) + 32 * s + k // 2, 7, stride=4)] = rows[0:7, tile(k)]
                    fs[pl.ds(2048 + 256 * k + 7 * s, 7)] = rows[8:15, tile(k)]

        loop(SHARDS, shard)
        for k in range(1 + b):
            wd[:, tile(k)] = fs[1024 * k : 1024 * k + 1024].astype(BF16)
        gap = jnp.zeros((4, 128), F32)
        for g in range(4 + 4 * b):
            for k in range(8):
                if b == 0:
                    start = 1024 + 256 * (k % 4) + 56 * g + k // 4
                    part = fs[pl.ds(start, 28, stride=2)]
                else:
                    start = 2048 + 256 * k + 28 * g
                    part = fs[start : start + 28]
                wu[32 * g : 32 * g + 32, tile(k)] = jnp.concatenate([part, gap], 0).astype(BF16)

    def taps0():
        for a in range(3):
            for b in range(3):
                yield a * 3 + b, (0 if a == 1 else 1), (0 if b == 1 else 1), a, b

    def both(ref_of):
        return jnp.concatenate([ref_of(0), ref_of(1)], 0)

    def squeeze(c, b, pooled, wd, wu):
        width = wd.shape[1]
        raw = row_dot(pooled, wd[...], nn)
        squeezed = raw * sig(raw)
        gating = sig(row_dot(squeezed, wu[...], nn))
        sv[b, c, 0:1] = pooled
        sv[b, c, 1:2, 0:width] = raw
        sv[b, c, 2:3, 0:width] = squeezed
        sv[b, c, 3:4] = gating
        return gating

    def gate(c, b, index, conv_k, wd, wu, name, proj_k):
        a, shift = affine(c, index)

        def pool_chunk(j, sums):
            z = pool[c, conv_k, chunk(j)] * a + shift
            excited = keep(c, j) * silu_half(z)
            pool[c, 7, chunk(j)] = excited
            return (sums[0] + fold(excited),)

        pooled = each_column(1, pool_chunk)[0] / crop_count(c)
        gating = squeeze(c, b, pooled, wd, wu)
        poll_crop(c, ("gate" if b == 0 else "bgate", "a"))

        def gate_chunk(j):
            ga[b, c, chunk(j)] = (pool[c, 7, chunk(j)] * gating).astype(BF16)

        loop(14, gate_chunk)

        def project(n):
            pool[c, proj_k, :, col(n)] = nn(ga[b, c], cols_of(name, col(n)))

        loop(4, project)
        return moment_sums(c, lambda j: pool[c, proj_k, chunk(j)])

    def ungate(c, b, index, conv_k, wd, wu, name):
        width = wd.shape[1]

        def back(n):
            pool[c, 7, :, col(n)] = nt(dp_of(c), rows_of(name, n))

        loop(4, back)
        a, shift = affine(c, index)

        def gate_chunk(j, sums):
            z = pool[c, conv_k, chunk(j)] * a + shift
            excited = keep(c, j) * silu_half(z)
            return (sums[0] + fold(pool[c, 7, chunk(j)] * excited),)

        d_gate = each_column(1, gate_chunk)[0]
        poll_crop(c, ("eback" if b == 0 else "bout", "a"))
        gating = sv[b, c, 3:4]
        d_raw = d_gate * gating * (1.0 - gating)
        raw = sv[b, c, 1:2, 0:width]
        d_squeeze = row_dot(d_raw, wu[...], nt) * slope_of(raw, sig(raw))
        d_pool = row_dot(d_squeeze, wd[...], nt) / crop_count(c)
        sv[b, c, 4:5] = d_raw
        sv[b, c, 5:6, 0:width] = d_squeeze
        center, scaling = hat_of(c, index)

        def slope_chunk(j, sums):
            value = pool[c, conv_k, chunk(j)]
            z = value * a + shift
            d = (pool[c, 7, chunk(j)] * gating + d_pool) * (keep(c, j, 0.5) * slope_half(z))
            pool[c, 7, chunk(j)] = d
            return (sums[0] + fold(d), sums[1] + fold(d * (value - center)))

        return scaled(each_column(2, slope_chunk), scaling)

    def small_grads(b):
        width = 128 + 128 * b

        def pairs(x_row, x_width, y_row, y_width):
            xs, ys = [], []
            for c in range(2):
                xh, xl = split_rows([sv[b, c, x_row : x_row + 1, 0:x_width]])
                yh, yl = split_rows([sv[b, c, y_row : y_row + 1, 0:y_width]])
                xs += [xh[0], xh[0], xl[0]]
                ys += [yh[0], yl[0], yh[0]]
            return tn(stacked(xs), stacked(ys))

        grad_down = pairs(0, C, 5, width)
        for k in range(1 + b):
            fs[1024 * k : 1024 * k + 1024] = grad_down[:, tile(k)]
        grad_up = pairs(2, width, 4, C)
        for g in range(4 + 4 * b):
            for k in range(8):
                part = grad_up[32 * g : 32 * g + 28, tile(k)]
                if b == 0:
                    fs[pl.ds(1024 + 256 * (k % 4) + 56 * g + k // 4, 28, stride=2)] = part
                else:
                    fs[2048 + 256 * k + 28 * g : 2048 + 256 * k + 28 * g + 28] = part

        def shard(s):
            tiles = []
            for k in range(8):
                if b == 0:
                    count = 4
                    first = fs[pl.ds(32 * s + k, 4, stride=8)]
                    second = fs[pl.ds(1024 + 256 * (k % 4) + 7 * s + k // 4, 4, stride=2)]
                else:
                    count = 7
                    first = fs[pl.ds(1024 * (k % 2) + 32 * s + k // 2, 7, stride=4)]
                    second = fs[pl.ds(2048 + 256 * k + 7 * s, 7)]
                gap = jnp.zeros((8 - count, 128), F32)
                tiles.append(jnp.concatenate([first, gap, second, gap], 0))
            put_shard("misc0" if b == 0 else "misc1", s, jnp.concatenate(tiles, 1))

        loop(SHARDS, shard)

    def norm_coefficients(c, index, totals, inverse, gain_row, kind):
        center, scaling = hat_of(c, index)
        ng[gain_row : gain_row + 1] += totals[1]
        shift_row = gain_row + 6 if gain_row < 6 else gain_row + 1
        ng[shift_row : shift_row + 1] += totals[0]
        a = st[c, index, 2:3]
        slope = -a * scaling * (totals[1] * inverse)
        offset = -a * (totals[0] * inverse) - slope * center
        return a, slope, offset

    def conv_grad(act_of, v_of, name):
        lane = lax.broadcasted_iota(jnp.int32, (64, 256), 1) // 64

        def block(a):
            for tap in range(9):
                dense = tn(
                    both(lambda c: act_of(c, tap, col(a))), both(lambda c: v_of(c, tap, col(a)))
                )
                own = jnp.where(lane == 0, dense[0:64], 0.0)
                for g in range(1, 4):
                    own = own + jnp.where(lane == g, dense[64 * g : 64 * g + 64], 0.0)
                for k in range(2):
                    at = 2048 * k + 224 * tap
                    fs[pl.ds(at + a, 28, stride=4)] = own[0:28, 128 * k : 128 * k + 128]
                    fs[pl.ds(at + 112 + a, 28, stride=4)] = own[32:60, 128 * k : 128 * k + 128]

        loop(4, block)

        def shard(s):
            tiles = [
                fs[pl.ds(2048 * k + 63 * s + a, 16, stride=4)] for a in range(4) for k in range(2)
            ]
            put_shard(name, s, jnp.concatenate(tiles, 1))

        loop(SHARDS, shard)

    def outer(left_of, right_of, name):
        def block(m):
            put_rows(name, m, tn(both(lambda c: left_of(c, col(m))), both(right_of)))

        loop(SHARDS * ROWS[name][1] // 256, block)

    z, yx = digit // 4, lax.rem(digit, 4)
    bits = (1 + section, 2 - section)

    def flip(bit):
        return yx + bit * (1 - 2 * lax.rem(yx // bit, 2))

    def push(src, dst, to, sends, recvs):
        pltpu.make_async_remote_copy(
            src_ref=src, dst_ref=dst, send_sem=sends, recv_sem=recvs,
            device_id=(section, to * v + rest), device_id_type=MESH,
        ).start()

    def push_sibling(src, dst, sends, recvs):
        pltpu.make_async_remote_copy(
            src_ref=src, dst_ref=dst, send_sem=sends, recv_sem=recvs,
            device_id=(other, me), device_id_type=MESH,
        ).start()

    def arrive(ref, sem):
        pltpu.make_async_copy(ref, ref, sem).wait()

    def gather(k, phase):
        start, stop = GATHERS[k]
        rows = pl.ds(start, stop - start)
        sent = w.at[section, :, :, rows]
        amounts = (
            w.at[section, pl.ds(0, 3), 0, rows], sent.at[:, 0], sent.at[:, pl.ds(0, 2)], sent,
        )
        before = (None, 0, 1, None, 2, 3)[phase]
        if before is not None:
            arrive(amounts[before], grecv.at[k, before])
        if phase == 5:
            for at in range(4):
                arrive(amounts[at], gsend.at[k, at])
            return
        sem = (0, 1, 2, 2, 3)[phase]
        sems = (gsend.at[k, sem], grecv.at[k, sem])
        if phase == 0:
            own = w.at[section, z, yx, rows]
            for hop in range(1, 4):
                push(own, own, lax.rem(z + hop, 4) * 4 + yx, *sems)
        elif phase == 1:
            push(sent.at[:, yx], sent.at[:, yx], z * 4 + flip(bits[0]), *sems)
        elif phase in (2, 3):
            at = yx if phase == 2 else flip(bits[0])
            push(sent.at[:, at], sent.at[:, at], z * 4 + flip(bits[1]), *sems)
        else:
            push_sibling(sent, sent, *sems)

    def poll(point):
        for k, phase in GATHER_PLAN.get(point, ()):
            gather(k, phase)
        for k, phase in SCATTER_PLAN.get(point, ()):
            scatter(k, phase)

    def poll_crop(c, point):
        for one in range(2):
            name = point[0] + str(one) + point[1]
            if name in GATHER_PLAN or name in SCATTER_PLAN:
                pl.when(c == one)(lambda: poll(name))

    def crops(body, point=None):
        def run(c):
            body(c)
            if point is not None:
                poll_crop(c, (point, ""))

        loop(2, run)

    def landing(k, phase, block, count):
        last = k - CHAINED
        if phase == 0:
            if k < 4:
                return e_buf.at[pl.ds(pl.multiple_of(block * count, 16), count)]
            ref = a1 if k == 4 else hid if last == 0 else ga.at[0]
            return ref.at[
                block // 8, pl.ds(pl.multiple_of(lax.rem(block, 8) * count, 16), count)
            ]
        if phase == 1:
            if last < 0:
                return ga.at[1, block // 4, pl.ds(block % 4 * count, count)]
            ref = hid if last == 0 else ga.at[0]
            return ref.at[block // 4, pl.ds(128 + block % 4 * 16, 16)]
        if phase == 2:
            if last < 0:
                return wu1.at[pl.ds(block * count, count)]
            ref = ga.at[0] if last == 0 else hid
            return ref.at[block // 2, pl.ds(192 + block % 2 * 16, 16)]
        if last >= 0:
            return wu0.at[pl.ds(64 * last + 16 * block, 16)]
        if k % 2:
            return wu1.at[pl.ds(160 + block * count, count)]
        return stage.at[block, pl.ds(0, count)]

    def landed(k, phase, count):
        return w.at[section, pl.ds(0, (4, 2, 1, 1)[phase]), pl.ds(0, (4, 4, 4, 3)[phase]), pl.ds(0, count)]

    def add_landed(k, phase, block, place_of, start, count):
        ref = landing(k, phase, block, count)
        index = (section, *place_of(block), pl.ds(start, count))
        w[index] = (w[index].astype(F32) + ref[...].astype(F32)).astype(BF16)

    def credit(at, to):
        pl.semaphore_signal(
            free.at[at], inc=1, device_id=(section, to * v + rest), device_id_type=MESH
        )

    def credit_sibling(at):
        pl.semaphore_signal(free.at[at], inc=1, device_id=(other, me), device_id_type=MESH)

    def credit_z(at):
        for hop in range(1, 4):
            credit(at, lax.rem(z + hop, 4) * 4 + yx)

    def scatter(k, phase):
        start, stop = SCATTERS[k]
        count = stop - start
        rows = pl.ds(start, count)
        first, second = flip(bits[1]), flip(bits[0])
        more = k + 1 < CHAINED
        before = (None, 0, None, 1, 2, 3)[phase]
        if before is not None:
            arrive(landed(k, before, count), rrecv.at[k, before])
        if phase == 1:
            loop(16, lambda b: add_landed(k, 0, b, lambda b: (b // 4, lax.rem(b, 4)), start, count))
            if k < 3:
                credit_sibling(0)
        elif phase == 3:
            for b in range(8):
                add_landed(k, 1, b, lambda b: (b // 2, yx if b % 2 == 0 else second), start, count)
            if more:
                credit(1, z * 4 + first)
        elif phase == 4:
            for b in range(4):
                add_landed(k, 2, b, lambda b: (b, yx), start, count)
            if more:
                credit(2, z * 4 + second)
            if k == 0:
                credit_z(5)
        elif phase == 5:
            total = w[section, z, yx, start:stop].astype(F32)
            for b in range(3):
                total = total + landing(k, 3, b, count)[...].astype(F32)
            pool[0, 1, start:stop] = total
            if k + 2 < CHAINED:
                credit_z(5 if k % 2 else 3)
            for sent in range(4):
                arrive(landed(k, sent, count), rsend.at[k, sent])
            return
        sem = (0, 1, 1, 2, 3)[phase]
        sems = (rsend.at[k, sem], rrecv.at[k, sem])
        if phase == 0:
            if k < 4 or k == CHAINED:
                pl.semaphore_wait(free.at[0 if k < 4 else 4], 1)

            def send(b):
                push_sibling(
                    w.at[other, b // 4, lax.rem(b, 4), rows], landing(k, 0, b, count), *sems
                )

            loop(16, send)
        elif phase in (1, 2):
            if k < CHAINED and phase == 1:
                pl.semaphore_wait(free.at[1], 1)
            for b in range(4 * phase - 4, 4 * phase):
                to = first if b % 2 == 0 else first + second - yx
                push(
                    w.at[section, b // 2, to, rows], landing(k, 1, b, count), z * 4 + first, *sems
                )
        elif phase == 3:
            if k < CHAINED:
                pl.semaphore_wait(free.at[2], 1)
            for b in range(4):
                push(
                    w.at[section, b, second, rows], landing(k, 2, b, count), z * 4 + second, *sems
                )
        else:
            if k < CHAINED:
                pl.semaphore_wait(free.at[5 if k % 2 else 3], 3)
            for hop in range(1, 4):
                to = lax.rem(z + hop, 4)
                push(w.at[section, to, yx, rows], landing(k, 3, hop - 1, count), to * 4 + yx, *sems)

    for copy in loads:
        copy.wait()
    shares = {}
    at = 0
    for name, ref, count in (
        ("wa0", v_wa0, 14), ("k0", v_k0, 16), ("ws", v_ws, 14), ("wd0", v_wd0, 4),
        ("wu0", v_wu0, 4), ("wc0", v_wc0, 28), ("wa1", v_wa1, 28), ("k1", v_k1, 16),
        ("wd1", v_wd1, 7), ("wu1", v_wu1, 7), ("wc1", v_wc1, 28),
    ):
        lines = LINES[ORDER_IN.index(name)]
        if len(ref.shape) == 2:
            fs[at : at + lines] = ref[...].astype(F32)
        else:
            whole, left = ref.shape[0] // 128, ref.shape[0] % 128
            fs[at : at + whole] = ref[pl.ds(0, 128 * whole)].astype(F32).reshape(whole, 128)
            rest_row = ref[pl.ds(128 * whole, left)].astype(F32).reshape(1, left)
            rest_row = jnp.concatenate([rest_row, jnp.zeros((1, 128 - left), F32)], 1)
            fs[at + whole : at + lines] = jnp.concatenate(
                [rest_row, jnp.zeros((lines - whole - 1, 128), F32)], 0
            )
        value = jnp.concatenate([fs[pl.ds(at + k, count, stride=7)] for k in range(7)], 1)
        room = 8 if count < 8 else count + -count % 16
        if room > count:
            value = jnp.concatenate([value, jnp.zeros((room - count, D), F32)], 0)
        shares[name] = value
        at += lines + -lines % 8
    load_map.wait()
    own_rows = jnp.concatenate([shares[name] for name in ORDER], 0).astype(BF16)
    for n in range(4):
        lanes = slice(256 * n, 256 * n + 256)
        w[section, z, yx, :, lanes] = nn(own_rows, e_buf[:, lanes]).astype(BF16)
    pl.semaphore_wait(barrier, MEMBERS + v - 1)
    poll("own")
    exchange = [
        to_sibling(upstream.at[theirs], up_buf.at[section], 1),
        to_sibling(features.at[theirs], x_buf.at[section], 0),
    ]
    for copy in exchange:
        copy.start()
    copies = exchange + copies
    ng[...] = jnp.zeros_like(ng)
    guard = jnp.zeros((GUARD, C), BF16)
    for ref, count in ((a0, 4), (d_buf, 2)):
        for c in range(2):
            for k in range(count):
                ref[c, k, 0:GUARD] = guard
                ref[c, k, GUARD + PX :] = guard
    for c in range(2):
        for ref in (a1, dp_buf):
            ref[c, 0:GUARD] = guard
            ref[c, GUARD + PX :] = guard

    halves = jnp.concatenate(
        [ref[...].astype(F32).reshape(1, DIN) for ref in (v_short_gain, v_short_shift)], 1
    )
    pair[section] = jnp.concatenate(
        [v_gain[k] for k in range(3)] + [v_shift[k] for k in range(3)]
        + [halves, jnp.zeros((1, D), F32)],
        0,
    )
    swap = to_sibling(pair.at[section], pair.at[section], 3)
    swap.start()
    swap.wait()
    first, second = pair[0], pair[1]
    short_gain_row = jnp.concatenate([first[6:7, 0:DIN], second[6:7, 0:DIN]], 1)
    short_shift_row = jnp.concatenate([first[6:7, DIN:], second[6:7, DIN:]], 1)
    rows = jnp.concatenate(
        [
            first[0:3], second[0:3], first[3:6], second[3:6], short_gain_row, short_shift_row,
            jnp.zeros((2, D), F32),
        ],
        0,
    )

    wide = nn(thirds(rows), e_buf[...])
    params[...] = wide[0:16] + wide[16:32] + wide[32:48]
    poll("params")

    for copy in copies:
        copy.wait()

    def gather_slices(ref, rows):
        pad = jnp.zeros((16 - rows, D), BF16)
        return jnp.concatenate(
            [jnp.concatenate([ref[:, D * j : D * j + D], pad], 0) for j in range(OUT)], 0
        )

    def cotangent(c):
        for h in range(2):
            x = gather_slices(up_buf.at[h, c], 7)
            for n in range(4):
                y = nn(x, e_buf[:, 256 * n : 256 * n + 256])
                for j in range(OUT):
                    count = 16 if h == 0 else 7
                    pool[c, 3, 16 * j + 7 * h : 16 * j + 7 * h + count, 256 * n : 256 * n + 256] = y[
                        16 * j : 16 * j + count
                    ]

    crops(cotangent, "cot")
    load_map = local_copy(expand.at[0], e_buf, 2)
    load_map.start()
    fs[...] = jnp.zeros_like(fs)
    poll("map")
    load_map.wait()

    def phases(c):
        for h in range(2):
            x = gather_slices(x_buf.at[h, c], 14)
            for n in range(4):
                y = nn(x, e_buf[:, 256 * n : 256 * n + 256])
                for j in range(OUT):
                    for k in range(2):
                        fs[pl.ds(512 * (2 * n + k) + 32 * j + 14 * h, 14)] = y[
                            16 * j : 16 * j + 14, 128 * k : 128 * k + 128
                        ]
        for q in range(2):
            def take(j):
                for k in range(8):
                    u_buf[c, q, chunk(j), 128 * k : 128 * k + 128] = fs[
                        pl.ds(512 * k + 32 * j + q, 16, stride=2)
                    ].astype(BF16)

            loop(14, take)

    crops(phases, "ph")
    load_map = local_copy(expand.at[1], e_buf, 2)
    load_map.start()
    poll("need_wa0")

    def entry_inner(c):
        for q in range(2):
            for r in range(2):
                def product(n):
                    inn[c, 2 * q + r, :, col(n)] = nn(
                        u_buf[c, q, :, 512 * r : 512 * r + 512], cols_of("wa0", col(n))
                    )

                loop(4, product)
            poll_crop(c, ("in", "ab"[q]))

        def body(j, sums):
            mask = keep(c, j)
            first, second = sums
            for k in range(4):
                value = inn[c, k, chunk(j)]
                weighted = value * mask
                first = first + fold(weighted)
                second = second + fold(weighted * value)
            return (first, second)

        sums = each_column(2, body)
        spare = lax.broadcasted_iota(jnp.int32, (1, C), 1) == 28
        ar_start(0, c, [jnp.where(spare, crop_count(c), sums[0]), sums[1]])

    crops(entry_inner, "in")
    poll("need_k0")
    build_conv("k0")
    poll("bk0")

    def entry_conv(c):
        totals = ar_wait(0, c, 2)
        count = jnp.zeros((1, C), F32) + totals[0][:, 28:29]
        cn[c, 0:1] = count
        cn[c, 1:2] = 1.0 / count
        cn[c, 2:3] = 0.25 / count
        spare = lax.broadcasted_iota(jnp.int32, (1, C), 1) == 28
        totals[0] = jnp.where(spare, 0.0, totals[0])
        set_stats(c, 0, totals, inverse_in(c), 0)
        a, shift = affine(c, 0)

        def activate(j):
            mask = keep(c, j)
            for q in range(2):
                for r in range(2):
                    z = inn[c, 2 * q + r, chunk(j)] * a + shift
                    act = mask * silu_half(z)
                    a0[c, 2 * q + r, chunk(j, GUARD)] = act.astype(BF16)
                    if q == 1:
                        d_buf[c, r, chunk(j, GUARD)] = pltpu.roll(act, 1, 0).astype(BF16)

        loop(14, activate)

        poll_crop(c, ("conv", "a"))

        def convolve(n):
            patches = []
            for tap, q, r, ta, tb in taps0():
                at = GUARD - 16 if tb == 0 else GUARD
                src = d_buf.at[c, r] if ta == 0 else a0.at[c, 2 * q + r]
                patches.append(src[at : at + PX, col(n)])
            pool[c, 0, :, col(n)] = nn(jnp.concatenate(patches, 1), kd[n])

        loop(4, convolve)
        ar_start(1, c, moment_sums(c, lambda j: pool[c, 0, chunk(j)]))

    crops(entry_conv, "conv")
    poll("need_ws")

    def strided(c):
        def product(n):
            pool[c, 2, :, col(n)] = nn(u_buf[c, 0, :, 0:512], cols_of("ws", col(n)))

        loop(4, product)
        ar_start(SHORT, c, moment_sums(c, lambda j: pool[c, 2, chunk(j)]))

    crops(strided, "str")
    build_small(0)
    poll("need_wc0")

    def entry_gate(c):
        totals = ar_wait(1, c, 2)
        set_stats(c, 1, totals, inverse_out(c), 1)
        ar_start(2, c, gate(c, 0, 1, 0, wd0, wu0, "wc0", 1))

    crops(entry_gate, "gate")
    poll("need_k1")
    build_conv("k1")
    poll("need_wa1")

    def entry_pre(c, j):
        a, shift = affine(c, 2)
        short_a, short_shift = affine(c, 3)
        return (
            pool[c, 1, chunk(j)] * a + pool[c, 2, chunk(j)] * short_a + (shift + short_shift)
        )

    def entry_out(c):
        set_stats(c, 3, ar_wait(SHORT, c, 2), inverse_out(c), 12)
        set_stats(c, 2, ar_wait(2, c, 2), inverse_out(c), 2)

        def finish(j):
            z = entry_pre(c, j)
            hid[c, chunk(j)] = (keep(c, j) * silu_half(z)).astype(BF16)

        loop(14, finish)
        poll_crop(c, ("out", "a"))

        def product(n):
            pool[c, 4, :, col(n)] = nn(hid[c], cols_of("wa1", col(n)))

        loop(4, product)
        ar_start(3, c, moment_sums(c, lambda j: pool[c, 4, chunk(j)]))

    crops(entry_out, "out")

    def body_conv(c):
        set_stats(c, 4, ar_wait(3, c, 2), inverse_out(c), 3)
        a, shift = affine(c, 4)

        def activate(j):
            z = pool[c, 4, chunk(j)] * a + shift
            act = keep(c, j) * silu_half(z)
            a1[c, chunk(j, GUARD)] = act.astype(BF16)
            d_buf[c, 0, chunk(j, GUARD)] = pltpu.roll(act, 1, 0).astype(BF16)
            d_buf[c, 1, chunk(j, GUARD)] = pltpu.roll(act, 15, 0).astype(BF16)

        loop(14, activate)
        poll_crop(c, ("bconv", "a"))

        def convolve(n):
            rows = (d_buf.at[c, 0], a1.at[c], d_buf.at[c, 1])
            patches = [
                rows[ta][16 * tb : 16 * tb + PX, col(n)] for ta in range(3) for tb in range(3)
            ]
            pool[c, 5, :, col(n)] = nn(jnp.concatenate(patches, 1), kd[n])

        loop(4, convolve)
        ar_start(4, c, moment_sums(c, lambda j: pool[c, 5, chunk(j)]))

    crops(body_conv, "bconv")
    poll("need_wc1")
    build_small(1)
    poll("small1f")

    def body_gate(c):
        set_stats(c, 5, ar_wait(4, c, 2), inverse_out(c), 4)
        ar_start(5, c, gate(c, 1, 5, 5, wd1, wu1, "wc1", 6))

    crops(body_gate, "bgate")

    def body_out(c):
        set_stats(c, 6, ar_wait(5, c, 2), inverse_out(c), 5)
        a, shift = affine(c, 6)
        center, scaling = hat_of(c, 6)

        def finish(j, sums):
            value = pool[c, 6, chunk(j)]
            z = value * a + shift + 0.5 * hid[c, chunk(j)].astype(F32)
            mask = keep(c, j)
            t = jnp.tanh(z)
            dp_buf[c, chunk(j, GUARD)] = (mask * (z * (1.0 + t))).astype(BF16)
            d_pre = pool[c, 3, chunk(j)] * (
                mask * (0.5 * (1.0 + t) * (1.0 + z * (1.0 - t)))
            )
            pool[c, 3, chunk(j)] = d_pre
            return (sums[0] + fold(d_pre), sums[1] + fold(d_pre * (value - center)))

        ar_start(6, c, scaled(each_column(2, finish), scaling))

    crops(body_out, "bo")
    load_map.wait()

    def narrow(value, store):
        for start, width in ((0, 256), (256, 256), (512, 256), (768, 128)):
            store(start, width, nt(value, e_buf[start : start + width]))

    def body_emit(c):
        def store(start, width, y):
            for j in range(OUT):
                for h in range(2):
                    up_buf[h, c, :, D * j + start : D * j + start + width] = y[
                        16 * j + 7 * h : 16 * j + 7 * h + 7
                    ].astype(BF16)

        narrow(dp_of(c), store)

    loop(2, body_emit)
    poll("bemit")
    out_copies = [
        to_sibling(up_buf.at[other], out.at[mine], 2),
        local_copy(up_buf.at[section], out.at[mine], 1),
    ]
    for copy in out_copies:
        copy.start()

    credit_sibling(0)

    def body_back_out(c):
        a, slope, offset = norm_coefficients(c, 6, ar_wait(6, c, 2), inverse_out(c), 5, 0)

        def project(j):
            value = pool[c, 6, chunk(j)]
            dp_buf[c, chunk(j, GUARD)] = (
                keep(c, j) * (a * pool[c, 3, chunk(j)] + slope * value + offset)
            ).astype(BF16)

        loop(14, project)
        ar_start(7, c, ungate(c, 1, 5, 5, wd1, wu1, "wc1"))

    crops(body_back_out, "bout")
    credit(2, z * 4 + flip(bits[0]))
    credit_z(3)
    outer(lambda c, l: ga[1, c, :, l], dp_of, "wc1")
    credit(1, z * 4 + flip(bits[1]))
    small_grads(1)
    poll("small1")

    def conv_cotangent(c, index, conv_k, a, slope, offset, versions):
        def body(j):
            d = keep(c, j) * (a * pool[c, 7, chunk(j)] + slope * pool[c, conv_k, chunk(j)] + offset)
            d_buf[c, 0, chunk(j, GUARD)] = d.astype(BF16)
            d_buf[c, 1, chunk(j, GUARD)] = pltpu.roll(d, 15, 0).astype(BF16)
            if versions == 3:
                dp_buf[c, chunk(j, GUARD)] = pltpu.roll(d, 1, 0).astype(BF16)

        loop(14, body)

    def v_body(c, tap, lanes):
        ta, tb = tap // 3, tap % 3
        ref = (d_buf.at[c, 1], d_buf.at[c, 0], dp_buf.at[c])[ta]
        return ref[32 - 16 * tb : 32 - 16 * tb + PX, lanes]

    def v_entry(c, tap, lanes):
        ta, tb = tap // 3, tap % 3
        at = 32 if tb == 0 else 16
        return d_buf[c, 1 if ta == 0 else 0, at : at + PX, lanes]

    def body_back_conv(c):
        a, slope, offset = norm_coefficients(c, 5, ar_wait(7, c, 2), inverse_out(c), 4, 0)
        conv_cotangent(c, 5, 5, a, slope, offset, 3)

        def back(n):
            total = nt(v_body(c, 0, col(n)), kd[n, 0:256])
            for tap in range(1, 9):
                total = total + nt(v_body(c, tap, col(n)), kd[n, 256 * tap : 256 * tap + 256])
            pool[c, 7, :, col(n)] = total

        loop(4, back)
        poll_crop(c, ("bback", "a"))
        a, shift = affine(c, 4)
        center, scaling = hat_of(c, 4)

        def body(j, sums):
            value = pool[c, 4, chunk(j)]
            z = value * a + shift
            d = pool[c, 7, chunk(j)] * (keep(c, j, 0.5) * slope_half(z))
            pool[c, 7, chunk(j)] = d
            return (sums[0] + fold(d), sums[1] + fold(d * (value - center)))

        ar_start(8, c, scaled(each_column(2, body), scaling))

    crops(body_back_conv, "bback")
    conv_grad(lambda c, tap, l: a1[c, GUARD : GUARD + PX, l], v_body, "k1")
    poll("k1")

    def body_back_in(c):
        a, slope, offset = norm_coefficients(c, 4, ar_wait(8, c, 2), inverse_out(c), 3, 0)

        def body(j):
            dp_buf[c, chunk(j, GUARD)] = (
                keep(c, j) * (a * pool[c, 7, chunk(j)] + slope * pool[c, 4, chunk(j)] + offset)
            ).astype(BF16)

        loop(14, body)

        def back(n):
            pool[c, 3, :, col(n)] = (
                (nt(dp_of(c), rows_of("wa1", n)) + pool[c, 3, :, col(n)]).astype(BF16).astype(F32)
            )

        loop(4, back)
        poll_crop(c, ("bin", "a"))
        center, scaling = hat_of(c, 2)
        short_center, short_scaling = hat_of(c, 3)

        def pre(j, sums):
            z = entry_pre(c, j)
            d = pool[c, 3, chunk(j)] * (keep(c, j, 0.5) * slope_half(z))
            pool[c, 3, chunk(j)] = d
            return (
                sums[0] + fold(d),
                sums[1] + fold(d * (pool[c, 1, chunk(j)] - center)),
                sums[2] + fold(d * (pool[c, 2, chunk(j)] - short_center)),
            )

        sums = each_column(3, pre)
        ar_start(9, c, scaled(sums, scaling, short_scaling))

    crops(body_back_in, "bin")
    outer(lambda c, l: hid[c, :, l], dp_of, "wa1")
    poll("wa1")
    build_conv("k0")
    poll("bk0b")

    def entry_back_out(c):
        totals = ar_wait(9, c, 3)
        a, slope, offset = norm_coefficients(c, 2, totals[0:2], inverse_out(c), 2, 0)
        short = norm_coefficients(c, 3, [totals[0], totals[2]], inverse_out(c), 12, 0)

        def project(j):
            mask = keep(c, j)
            d = pool[c, 3, chunk(j)]
            dp_buf[c, chunk(j, GUARD)] = (
                mask * (a * d + slope * pool[c, 1, chunk(j)] + offset)
            ).astype(BF16)
            hid[c, chunk(j)] = (
                mask * (short[0] * d + short[1] * pool[c, 2, chunk(j)] + short[2])
            ).astype(BF16)

        loop(14, project)

        def back(n):
            pool[c, 2, :, col(n)] = nt(hid[c], rows_of("ws", n))

        loop(2, back)
        ar_start(10, c, ungate(c, 0, 1, 0, wd0, wu0, "wc0"))

    crops(entry_back_out, "eback")
    outer(lambda c, l: ga[0, c, :, l], dp_of, "wc0")
    poll("wc0")
    outer(lambda c, l: u_buf[c, 0, :, l], lambda c: hid[c], "ws")
    credit_sibling(4)
    small_grads(0)
    poll("small0")

    def entry_back_conv(c):
        a, slope, offset = norm_coefficients(c, 1, ar_wait(10, c, 2), inverse_out(c), 1, 0)
        conv_cotangent(c, 1, 0, a, slope, offset, 2)
        for q in range(2):
            for r in range(2):
                def back(n):
                    total = None
                    for tap, tq, tr, ta, tb in taps0():
                        if (tq, tr) == (q, r):
                            term = nt(v_entry(c, tap, col(n)), kd[n, 256 * tap : 256 * tap + 256])
                            total = term if total is None else total + term
                    pool[c, 4 + 2 * q + r, :, col(n)] = total

                loop(4, back)
            poll_crop(c, ("econv", "ab"[q]))
        a, shift = affine(c, 0)
        center, scaling = hat_of(c, 0)

        def body(j, sums):
            mask = keep(c, j, 0.5)
            first, second = sums
            for k in range(4):
                value = inn[c, k, chunk(j)]
                z = value * a + shift
                d = pool[c, 4 + k, chunk(j)] * (mask * slope_half(z))
                pool[c, 4 + k, chunk(j)] = d
                first = first + fold(d)
                second = second + fold(d * (value - center))
            return (first, second)

        ar_start(11, c, scaled(each_column(2, body), scaling))

    crops(entry_back_conv, "econv")

    def act_entry(c, tap, lanes):
        q = 0 if tap // 3 == 1 else 1
        r = 0 if tap % 3 == 1 else 1
        return a0[c, 2 * q + r, GUARD : GUARD + PX, lanes]

    conv_grad(act_entry, v_entry, "k0")
    poll("k0")
    load_map = local_copy(expand.at[0], e_buf, 2)
    load_map.start()
    for copy in out_copies:
        copy.wait()

    def entry_back_in(c):
        a, slope, offset = norm_coefficients(c, 0, ar_wait(11, c, 2), inverse_in(c), 0, 0)

        def body(j):
            mask = keep(c, j)
            for k in range(4):
                a0[c, k, chunk(j, GUARD)] = (
                    mask * (a * pool[c, 4 + k, chunk(j)] + slope * inn[c, k, chunk(j)] + offset)
                ).astype(BF16)

        loop(14, body)

    loop(2, entry_back_in)
    poll("d")
    swap = to_sibling(ng, ng_in, 3)
    swap.start()

    def input_grad(m):
        total = None
        for q in range(2):
            for r in range(2):
                at = pl.ds(pl.multiple_of(512 * r + 256 * m, 256), 256)
                term = tn(
                    both(lambda c: u_buf[c, q, :, at]),
                    both(lambda c: a0[c, 2 * q + r, GUARD : GUARD + PX]),
                )
                total = term if total is None else total + term
        return total

    def input_block(m):
        dp_buf[m] = rows_of("wa0", m)
        put_rows("wa0", m, input_grad(m))

    loop(2, input_block)
    poll("wa0")

    def entry_back_input(c):
        for q in range(2):
            for r in range(2):
                def back(n):
                    total = nt(a0[c, 2 * q + r, GUARD : GUARD + PX], dp_buf[n])
                    if q == 0 and r == 0:
                        total = total + pool[c, 2, :, col(n)]
                    at = pl.ds(pl.multiple_of(512 * r + 256 * n, 256), 256)
                    d_buf[c, q, 0:PX, at] = total.astype(BF16)

                loop(2, back)
            if q == 0:
                poll_crop(c, ("input", "a"))

    crops(entry_back_input, "input")

    def entry_emit(c):
        for q in range(2):
            def store(start, width, y):
                for j in range(OUT):
                    for k in range(width // 128):
                        fs[pl.ds(512 * (start // 128 + k) + 32 * j + q, 14, stride=2)] = y[
                            16 * j : 16 * j + 14, 128 * k : 128 * k + 128
                        ]

            narrow(d_buf[c, q, 0:PX], store)
        poll_crop(c, ("emit", "a"))
        for h in range(2):
            for j in range(OUT):
                for k in range(7):
                    x_buf[h, c, :, D * j + 128 * k : D * j + 128 * k + 128] = fs[
                        512 * k + 32 * j + 14 * h : 512 * k + 32 * j + 14 * h + 14
                    ].astype(BF16)

    load_map.wait()
    crops(entry_emit, "emit")
    last = [
        to_sibling(x_buf.at[other], grad.at[mine], 4),
        local_copy(x_buf.at[section], grad.at[mine], 0),
    ]
    for copy in last:
        copy.start()
    swap.wait()
    ng[...] = ng[...] + ng_in[...]
    last.append(local_copy(ng, result.at[pl.ds(192, 16)], 1))
    last[-1].start()
    poll("tail")
    last.append(local_copy(pool.at[0, 1, pl.ds(0, 192)], result.at[pl.ds(0, 192)], 2))
    last[-1].start()
    for copy in last:
        copy.wait()


def thirds(value):
    high = value.astype(BF16)
    left = value - high.astype(F32)
    middle = left.astype(BF16)
    return jnp.concatenate([high, middle, (left - middle.astype(F32)).astype(BF16)], 0)


def final_kernel(result_in, map_in, *refs):
    flat_out, (gain_out, shift_out, short_gain_out, short_shift_out) = refs[:11], refs[11:15]
    flat, (gain, shift, short_gain, short_shift), sems = refs[15:26], refs[26:30], refs[30]
    result, narrow_map = refs[31:33]
    loads = [
        pltpu.make_async_copy(result_in, result, sems.at[15]),
        pltpu.make_async_copy(map_in, narrow_map, sems.at[16]),
    ]
    for copy in loads:
        copy.start()
    for copy in loads:
        copy.wait()
    section = lax.axis_index("section")
    total = nt(thirds(result[192:208]), narrow_map[...])
    total = total[0:16] + total[16:32] + total[32:48]

    def own(top, low):
        return jnp.where(section == 0, top, low)

    for k in range(3):
        gain[k] = own(total[k : k + 1], total[k + 3 : k + 4])
        shift[k] = own(total[k + 6 : k + 7], total[k + 9 : k + 10])
    short_gain[...] = own(total[12:13, 0:DIN], total[12:13, DIN:])
    short_shift[...] = own(total[13:14, 0:DIN], total[13:14, DIN:])
    total = result[0:192]
    high = total.astype(BF16)
    low = (total - high.astype(F32)).astype(BF16)
    final = nt(high, narrow_map[...]) + nt(low, narrow_map[...])
    for (name, count), ref in zip(
        (
            ("wa0", 14), ("k0", 16), ("ws", 14), ("wd0", 4), ("wu0", 4), ("wc0", 28), ("wa1", 28),
            ("k1", 16), ("wd1", 7), ("wu1", 7), ("wc1", 28),
        ),
        flat,
    ):
        if name[1] in "du":
            at = ROWS["misc" + name[2]][0] + (8 if name[1] == "u" else 0)
        else:
            at = ROWS[name][0]
        for k in range(7):
            ref[pl.ds(k, count, stride=7)] = final[at : at + count, 128 * k : 128 * k + 128]
    copies = [
        pltpu.make_async_copy(src, dst, sems.at[at])
        for at, (src, dst) in enumerate(
            zip((*flat, gain, shift, short_gain, short_shift), (*flat_out, gain_out, shift_out, short_gain_out, short_shift_out))
        )
    ]
    for copy in copies:
        copy.start()
    for copy in copies:
        copy.wait()


def final_call(result, narrow_map):
    shapes = [(count, 128) for count in LINES] + [(3, 1, D), (3, 1, D), (1, DIN), (1, DIN)]
    return pl.pallas_call(
        final_kernel,
        out_shape=[jax.ShapeDtypeStruct(shape, F32) for shape in shapes],
        in_specs=[pl.BlockSpec(memory_space=pl.ANY)] * 2,
        out_specs=[pl.BlockSpec(memory_space=pl.ANY)] * 15,
        scratch_shapes=[pltpu.VMEM(shape, F32) for shape in shapes]
        + [pltpu.SemaphoreType.DMA((17,)), pltpu.VMEM((208, C), F32), pltpu.VMEM((D, C), BF16)],
        compiler_params=pltpu.CompilerParams(vmem_limit_bytes=60 << 20),
    )(result, narrow_map)


def lane_maps():
    at = np.arange(D)
    first = np.zeros((D, C), np.float32)
    first[at, at // 14 * 16 + at % 14] = 1
    second = np.zeros((D, C), np.float32)
    second[at, at // 28 * 32 + at % 28] = 1
    return np.stack([first, second])


def main_call(n_dp, *args):
    v = n_dp // MEMBERS
    any_space = pl.BlockSpec(memory_space=pl.ANY)
    smem = pl.BlockSpec(memory_space=pltpu.SMEM)
    shape = lambda *s, dtype=BF16: jax.ShapeDtypeStruct(s, dtype)
    outs = [
        shape(4, 7, 12544), shape(4, 14, 12544), shape(208, C, dtype=F32),
    ]
    dma = pltpu.SemaphoreType.DMA
    scratch = [
        pltpu.VMEM((2, 4, PX, C), F32),
        pltpu.VMEM((2, 8, PX, C), F32),
        pltpu.VMEM((2, 2, PX, C), BF16),
        pltpu.VMEM((2, 4, PX + 2 * GUARD, C), BF16),
        pltpu.VMEM((2, PX + 2 * GUARD, C), BF16),
        pltpu.VMEM((2, 2, PX + 2 * GUARD, C), BF16),
        pltpu.VMEM((2, 2, PX, C), BF16),
        pltpu.VMEM((2, PX, C), BF16),
        pltpu.VMEM((2, PX + 2 * GUARD, C), BF16),
        pltpu.VMEM((2, 2, 14, 12544), BF16),
        pltpu.VMEM((2, 2, 7, 12544), BF16),
        pltpu.VMEM((4096, 128), F32),
        pltpu.VMEM((4, 2304, 256), BF16),
        pltpu.VMEM((D, C), BF16),
        pltpu.VMEM((2, 4, 4, 192, C), BF16),
        pltpu.VMEM((C, 128), BF16),
        pltpu.VMEM((128, C), BF16),
        pltpu.VMEM((C, 256), BF16),
        pltpu.VMEM((256, C), BF16),
        pltpu.VMEM((3, 48, C), BF16),
        pltpu.VMEM((16, C), F32),
        pltpu.VMEM((2, 8, D), F32),
        pltpu.VMEM((2, 7, 8, C), F32),
        pltpu.VMEM((2, 2, 8, C), F32),
        pltpu.VMEM((2, 8, C), F32),
        pltpu.VMEM((16, C), F32),
        pltpu.VMEM((16, C), F32),
        pltpu.VMEM((2, 2, MEMBERS, 2, C), F32),
        pltpu.VMEM((2, MEMBERS, 2, C), F32),
        pltpu.VMEM((2, 2, MEMBERS, 32, 128), BF16),
        pltpu.VMEM((3, 2, v, 4, C), F32),
        pltpu.VMEM((3, 1, D), F32),
        pltpu.VMEM((3, 1, D), F32),
        pltpu.VMEM((DIN,), BF16),
        pltpu.VMEM((DIN,), BF16),
        *[pltpu.VMEM(shard.shape, BF16) for shard in args[8:]],
        dma((16,)), dma((3, 2)), dma((3, 2)), dma((3, 2)), dma((3, 2)), dma((5,)), dma((5,)), dma((4,)),
        dma((7, 4)), dma((7, 4)), dma((7, 4)), dma((7, 4)), pltpu.SemaphoreType.REGULAR((6,)),
    ]
    return pl.pallas_call(
        functools.partial(main_kernel, n_dp),
        out_shape=outs,
        in_specs=[any_space, any_space, smem] + [any_space] * 16,
        out_specs=[any_space] * 3,
        scratch_shapes=scratch,
        compiler_params=pltpu.CompilerParams(
            collective_id=1, has_side_effects=True, vmem_limit_bytes=64 << 20
        ),
    )(*args)


def local(
    features, crop_side, upstream,
    entry_in, entry_group, entry_out, entry_down, entry_up, shortcut_weight,
    body_in, body_group, body_out, body_down, body_up,
    norm_gain, norm_shift, shortcut_gain, shortcut_shift,
):
    n_dp = lax.axis_size("dp")
    v = n_dp // MEMBERS
    groups = [[v * member + k for k in range(v)] for member in range(MEMBERS)]
    shards = (
        entry_in, entry_group, shortcut_weight, entry_down, entry_up, entry_out,
        body_in, body_group, body_down, body_up, body_out,
    )

    def lines(shard, count):
        if v > 1:
            shard = lax.all_gather(shard, "dp", axis_index_groups=groups, axis=0, tiled=True)
        return shard.reshape(count, 128) if shard.shape[0] == 128 * count else shard

    maps = jnp.asarray(lane_maps(), BF16)
    output, d_features, result = main_call(
        n_dp, features, upstream, crop_side, maps,
        norm_gain.transpose(1, 0, 2), norm_shift.transpose(1, 0, 2),
        shortcut_gain, shortcut_shift,
        *(lines(shard, count) for shard, count in zip(shards, LINES)),
    )
    results = final_call(result, jnp.asarray(lane_maps()[1], BF16))

    def share(values, shard):
        values = values.reshape(-1)[: v * shard.shape[0]]
        if v > 1:
            values = lax.psum_scatter(
                values, "dp", scatter_dimension=0, axis_index_groups=groups, tiled=True
            )
        return values

    wa0, k0, ws, wd0, wu0, wc0, wa1, k1, wd1, wu1, wc1 = (
        share(values, shard) for values, shard in zip(results[:11], shards)
    )
    gains, shifts, short_gain, short_shift = results[11:15]
    return (
        output, d_features, wa0, k0, wc0, wd0, wu0, ws, wa1, k1, wc1, wd1, wu1,
        gains.transpose(1, 0, 2), shifts.transpose(1, 0, 2),
        short_gain[0], short_shift[0],
    )


def solution(mesh):
    rows = P("dp", "section", None)
    flat = P(("section", "dp"))
    params = (P("section", None, None), P("section", None, None), P("section"), P("section"))
    return jax.shard_map(
        local,
        mesh=mesh,
        in_specs=(rows, P("dp"), rows) + (flat,) * 11 + params,
        out_specs=(rows, rows) + (flat,) * 11 + params,
        check_vma=False,
    )
```
